256 devices in a mesh: dp: 4 (over x), space: 64 (over y, z, core).
Axes of the slice: x: 4, y: 4, z: 8, core: 2. Of those that a mesh axis runs over, the one named last changes fastest.
Arguments:
- video_latent: bfloat16 [4, 8, 128, 16, 256], P('dp', None, 'space'), may hold values from -18 to 18
- frame_counts: int32 [4], P('dp'), may hold values from 1 to 8, as said below
- conv_kernel: bfloat16 [27, 256, 256], replicated, may hold values from -0.078125 to 0.078125
- norm_gain: float32 [256], replicated, may hold values from 0.5 to 1.5
- output_grad: bfloat16 [4, 8, 128, 16, 256], P('dp', None, 'space'), may hold values from -6 to 6
Outputs:
- block_output: bfloat16 [4, 8, 128, 16, 256], P('dp', None, 'space')
- input_grad: bfloat16 [4, 8, 128, 16, 256], P('dp', None, 'space')
- kernel_grad: float32 [256, 27, 256], P('space')
- gain_grad: float32 [256], replicated
The draws below stay inside these ranges and needn't reach their ends.
Inputs may be any that keep to these rules, and one draw needn't show every extreme that they name: `frame_counts`: frames from this count on are padding.
All inputs are finite; a program needn't handle non-finite values.
Results may differ from the reference program's by a relative error of at most 0.0028.
Values may be sent and summed in bfloat16 or wider, within the bound.
No kernel may reach another device: no remote copies, remote signals or barrier semaphores. Data moves between devices by JAX's collectives and lax.ppermute only.
A program may use at most 128 MiB of HBM per device.

```python
import math
import jax
import jax.numpy as jnp
from jax import lax

CHANNELS = 256
GROUPS = 32
FRAMES = 8
COLS = 16
CLIPS = 4
HEIGHT = 128


def draw_video_latent(key, part):
    key = jax.random.fold_in(key, 11)
    key_noise, key_chan = jax.random.split(key, 2)
    row_scale = 0.5 * 3.0 ** (jnp.arange(HEIGHT, dtype=jnp.float32) / (HEIGHT - 1))
    channel_scale = jnp.exp(jax.random.uniform(key_chan, (CHANNELS,), jnp.float32, math.log(0.3), math.log(3.0)))
    scale_full = row_scale[None, None, :, None, None] * channel_scale[None, None, None, None, :]
    shape_full = (CLIPS, FRAMES, HEIGHT, COLS, CHANNELS)
    base_values = jnp.clip(jax.random.normal(key_noise, shape_full, jnp.float32), -4.0, 4.0)
    return (base_values * scale_full).astype(jnp.bfloat16)


def draw_frame_counts(key, part):
    key = jax.random.fold_in(key, 23)
    key_base, key_long, key_short = jax.random.split(key, 3)
    base_counts = jax.random.randint(key_base, (CLIPS,), 1, FRAMES + 1)
    long_clip = jax.random.randint(key_long, (), 0, CLIPS)
    short_clip = (long_clip + jax.random.randint(key_short, (), 1, CLIPS)) % CLIPS
    positions = jnp.arange(CLIPS, dtype=jnp.int32)
    return jnp.where(positions == long_clip, FRAMES, jnp.where(positions == short_clip, 1, base_counts)).astype(jnp.int32)


def block_scale(own_key, shape, cuts, least, largest):
    level, own = 1.0, jax.random.fold_in(own_key, 6)
    for axis_at, blocks in cuts:
        steps = jnp.exp(jax.random.uniform(jax.random.fold_in(own, axis_at), (blocks,), jnp.float32, least / len(cuts), largest / len(cuts)))
        level = level * jnp.repeat(steps, shape[axis_at] // blocks).reshape([-1 if axis == axis_at else 1 for axis in range(len(shape))])
    return level


def scatter_about(rng, dims, width, most, cuts=(), kind=jnp.bfloat16):
    result = jax.random.normal(rng, dims, jnp.float32) * width
    if len(cuts) > 0:
        result = block_scale(rng, dims, cuts, -0.22, 0.18) * result
    return jnp.clip(result, min=-most, max=most).astype(kind)


def setup_inputs(seed: int = 0) -> dict:
    key_of = jax.random.split(jax.random.key(seed), 6)
    video_latent = draw_video_latent(jax.random.fold_in(key_of[5], 71), 0)
    frame_counts = draw_frame_counts(jax.random.fold_in(key_of[5], 71), 0)
    conv_kernel = scatter_about(key_of[2], (27, CHANNELS, CHANNELS), (27 * CHANNELS) ** -0.5, 0.078125)
    norm_gain = jnp.clip(1.0 + 0.1 * jax.random.normal(key_of[3], (CHANNELS,), jnp.float32), 0.5, 1.5)
    output_grad = scatter_about(key_of[4], (CLIPS, FRAMES, HEIGHT, COLS, CHANNELS), 1.0, 6.0, ((0, 4), (2, 64)))
    return dict(video_latent=video_latent, frame_counts=frame_counts, conv_kernel=conv_kernel, norm_gain=norm_gain, output_grad=output_grad)


EPSILON = 1e-05

def tap_products(padded, kernel, frame_slots):
    clip_count = padded.shape[0]
    local_rows = padded.shape[2] - 2
    width_cols = padded.shape[3] - 2
    channels = padded.shape[4]
    running_sum = jnp.zeros((clip_count * frame_slots * local_rows * width_cols, kernel.shape[2]), jnp.float32)
    for tap_time in range(3):
        for tap_row in range(3):
            for tap_col in range(3):
                window = padded[:, tap_time:tap_time + frame_slots, tap_row:tap_row + local_rows, tap_col:tap_col + width_cols, :]
                running_sum = running_sum + jnp.dot(window.reshape(-1, channels), kernel[(tap_time * 3 + tap_row) * 3 + tap_col], preferred_element_type=jnp.float32)
    return running_sum.reshape(clip_count, frame_slots, local_rows, width_cols, kernel.shape[2])

def kernel_terms(padded, grad_slab):
    frame_slots = grad_slab.shape[1]
    local_rows = grad_slab.shape[2]
    width_cols = grad_slab.shape[3]
    grad_rows = grad_slab.reshape(-1, grad_slab.shape[4])
    tap_terms = []
    for tap_time in range(3):
        for tap_row in range(3):
            for tap_col in range(3):
                window = padded[:, tap_time:tap_time + frame_slots, tap_row:tap_row + local_rows, tap_col:tap_col + width_cols, :]
                tap_terms.append(lax.dot_general(window.reshape(-1, padded.shape[4]), grad_rows, (((0,), (0,)), ((), ())), preferred_element_type=jnp.float32))
    return jnp.stack(tap_terms, axis=1)

def flip_kernel(kernel):
    channels = kernel.shape[1]
    reversed_taps = kernel.reshape(3, 3, 3, channels, channels)[::-1, ::-1, ::-1]
    return jnp.swapaxes(reversed_taps, 3, 4).reshape(27, channels, channels)

def group_view(values):
    shape_now = values.shape
    return values.reshape(shape_now[0], shape_now[1], shape_now[2], shape_now[3], GROUPS, shape_now[4] // GROUPS)

def reference(video_latent, frame_counts, conv_kernel, norm_gain, output_grad):
    frame_slots = video_latent.shape[1]
    live_mask = (jnp.arange(frame_slots, dtype=jnp.int32)[None, :] < frame_counts[:, None]).astype(jnp.float32)
    mask_full = live_mask[:, :, None, None, None]
    latent_float = video_latent.astype(jnp.float32)
    grouped = group_view(latent_float)
    group_mean = lax.optimization_barrier(jnp.mean(grouped, axis=(2, 3, 5), keepdims=True))
    centered = grouped - group_mean
    variance = lax.optimization_barrier(jnp.mean(centered * centered, axis=(2, 3, 5), keepdims=True))
    inverse_std = lax.rsqrt(variance + EPSILON)
    normalized = (centered * inverse_std).reshape(video_latent.shape)
    gated_input = normalized * norm_gain
    activated = jax.nn.silu(gated_input).astype(jnp.bfloat16)
    padded = jnp.pad(activated, ((0, 0), (2, 0), (1, 1), (1, 1), (0, 0)))
    conv_out = tap_products(padded, conv_kernel, frame_slots)
    block_output = ((latent_float + conv_out) * mask_full).astype(jnp.bfloat16)
    masked_grad = (output_grad.astype(jnp.float32) * mask_full).astype(jnp.bfloat16)
    grad_padded = jnp.pad(masked_grad, ((0, 0), (0, 2), (1, 1), (1, 1), (0, 0)))
    act_grad = tap_products(grad_padded, flip_kernel(conv_kernel), frame_slots)
    sigmoid_value = jax.nn.sigmoid(gated_input)
    pre_grad = act_grad * sigmoid_value * (1.0 + gated_input * (1.0 - sigmoid_value))
    gain_grad = lax.optimization_barrier(jnp.sum(pre_grad * normalized, axis=(0, 1, 2, 3)))
    scaled_grad = pre_grad * norm_gain
    scaled_groups = group_view(scaled_grad)
    normal_groups = group_view(normalized)
    first_mean = lax.optimization_barrier(jnp.mean(scaled_groups, axis=(2, 3, 5), keepdims=True))
    second_mean = lax.optimization_barrier(jnp.mean(scaled_groups * normal_groups, axis=(2, 3, 5), keepdims=True))
    norm_grad = (inverse_std * (scaled_groups - first_mean - normal_groups * second_mean)).reshape(video_latent.shape)
    input_grad = (masked_grad.astype(jnp.float32) + norm_grad).astype(jnp.bfloat16)
    kernel_grad = kernel_terms(padded, masked_grad)
    return (block_output, input_grad, kernel_grad, gain_grad)
```

```python
import jax
import jax.numpy as jnp
from jax import lax
from jax.experimental import pallas as pl
from jax.experimental.pallas import tpu as pltpu
from jax.sharding import Mesh
from jax.sharding import PartitionSpec as P

F32 = jnp.float32
BF16 = jnp.bfloat16
NX, NY, NZ, NC = 4, 4, 8, 2
SPACE = NY * NZ * NC
FR, ROWS, COLS, CH = 8, 2, 16, 256
CELLS = ROWS * COLS
GROUPS = 32
GC = CH // GROUPS
ASL = CH // NY
BSL = CH // NC
EPSILON = 1e-05
COUNT = CELLS * SPACE * GC
AROWS = FR // 2 * 3 * COLS
GROWS = FR * ROWS * COLS
HI = lax.Precision.HIGHEST


def hdot(a, b):
    return jnp.dot(a, b, preferred_element_type=F32, precision=HI)


def gather_matrix():
    lane = lax.broadcasted_iota(jnp.int32, (CH, GROUPS), 0)
    group = lax.broadcasted_iota(jnp.int32, (CH, GROUPS), 1)
    return (lane // GC == group).astype(F32)


def spread_matrix():
    group = lax.broadcasted_iota(jnp.int32, (GROUPS, CH), 0)
    lane = lax.broadcasted_iota(jnp.int32, (GROUPS, CH), 1)
    return (lane // GC == group).astype(F32)


def frame_mask(shape, count):
    return lax.broadcasted_iota(jnp.int32, shape, 0) < count


def shifted(cells, k):
    if k == 1:
        return cells
    zero = jnp.zeros(cells.shape[:-2] + (1, cells.shape[-1]), cells.dtype)
    if k == 0:
        return jnp.concatenate([zero, cells[..., :-1, :]], axis=-2)
    return jnp.concatenate([cells[..., 1:, :], zero], axis=-2)


def edges_and_sums(x_ref, g_ref, up_ref, dn_ref, st_ref):
    up_ref[0] = x_ref[:, 0]
    up_ref[1] = g_ref[:, 0]
    dn_ref[0] = x_ref[:, 1]
    dn_ref[1] = g_ref[:, 1]
    xf = x_ref[...].astype(F32).reshape(FR, CELLS, CH)
    gather = gather_matrix()
    mean = hdot(jnp.sum(xf, axis=1), gather) / (CELLS * GC)
    centered = xf - hdot(mean, spread_matrix())[:, None, :]
    squares = hdot(jnp.sum(centered * centered, axis=1), gather)
    both = jnp.concatenate([mean, squares], axis=1)
    st_ref[...] = jnp.broadcast_to(both[None], (SPACE, FR, 2 * GROUPS))


def pack_slices(x_ref, g_ref, hp_ref, hn_ref, c_ref, out_ref):
    upper = c_ref[0] == 0
    own = [x_ref[:, 0], x_ref[:, 1]]
    before, after = hp_ref[0], hn_ref[0]
    rows = [
        jnp.where(upper, before, own[0]),
        jnp.where(upper, own[0], own[1]),
        jnp.where(upper, own[1], after),
    ]
    three = jnp.stack(rows, axis=1).reshape(FR // 2, 2, 3, COLS, CH)
    for y in range(NY):
        part = three[..., y * ASL : (y + 1) * ASL]
        pair = jnp.concatenate([part[:, 0], part[:, 1]], axis=-1).reshape(AROWS, 2 * ASL)
        for c in range(NC):
            out_ref[y * NC + c, :AROWS] = pair
            out_ref[y * NC + c, AROWS:] = g_ref[..., c * BSL : (c + 1) * BSL].reshape(GROWS, BSL)


def backward_conv(g_ref, hp_ref, hn_ref, k_ref, n_ref, out_ref, pad_ref):
    count = n_ref[0]
    rows = [hp_ref[1], g_ref[:, 0], g_ref[:, 1], hn_ref[1]]
    for r in range(4):
        cells = rows[r].astype(F32)
        cells = jnp.where(frame_mask(cells.shape, count), cells, 0.0)
        for k in range(3):
            pad_ref[k, :FR, r] = shifted(cells, k).astype(BF16)
    pad_ref[:, FR:] = jnp.zeros((3, 2, 4, COLS, CH), BF16)
    total = jnp.zeros((FR * CELLS, CH), F32)
    for i in range(3):
        for j in range(3):
            for k in range(3):
                window = pad_ref[2 - k, 2 - i : 2 - i + FR, 2 - j : 4 - j]
                total = total + lax.dot_general(
                    window.reshape(FR * CELLS, CH),
                    k_ref[(i * 3 + j) * 3 + k],
                    (((1,), (1,)), ((), ())),
                    preferred_element_type=F32,
                )
    out_ref[...] = total


def group_terms(st_ref, x_ref, ag_ref, gain_ref, out_ref, sc_ref, mean_ref, inv_ref):
    means = st_ref[:, :, :GROUPS]
    squares = st_ref[:, :, GROUPS:]
    mean = jnp.sum(means, axis=0) / SPACE
    apart = means - mean[None]
    whole = jnp.sum(squares + (CELLS * GC) * (apart * apart), axis=0)
    spread = spread_matrix()
    mean_all = hdot(mean, spread)
    inv_all = hdot(lax.rsqrt(whole / COUNT + EPSILON), spread)
    mean_ref[...] = mean_all
    inv_ref[...] = inv_all
    gain = gain_ref[...][None]
    xf = x_ref[...].astype(F32).reshape(FR, CELLS, CH)
    normalized = (xf - mean_all[:, None, :]) * inv_all[:, None, :]
    gated = normalized * gain
    sig = jax.nn.sigmoid(gated)
    pre = ag_ref[...].reshape(FR, CELLS, CH) * sig * (1.0 + gated * (1.0 - sig))
    scaled = pre * gain
    sc_ref[...] = scaled
    gather = gather_matrix()
    first = hdot(jnp.sum(scaled, axis=1), gather)
    by_channel = jnp.sum(pre * normalized, axis=1)
    second = hdot(by_channel * gain_ref[...], gather)
    gain_part = jnp.sum(by_channel, axis=0, keepdims=True)
    row = lax.broadcasted_iota(jnp.int32, (FR, CH), 0)
    lane = lax.broadcasted_iota(jnp.int32, (FR, CH), 1)
    folded = jnp.where(lane // GROUPS == row, jnp.broadcast_to(gain_part, (FR, CH)), 0.0)
    fold_lane = lax.broadcasted_iota(jnp.int32, (CH, GROUPS), 0)
    fold_at = lax.broadcasted_iota(jnp.int32, (CH, GROUPS), 1)
    folded = hdot(folded, (fold_lane % GROUPS == fold_at).astype(F32))
    everything = jnp.concatenate([first, second, folded], axis=1)
    out_ref[...] = jnp.broadcast_to(everything[None], (SPACE, FR, 3 * GROUPS))


def kernel_part(in_ref, mean_ref, inv_ref, gain_ref, at_ref, out_ref, pad_ref, grad_ref, sum_ref):
    count, y_at, z_at = at_ref[0], at_ref[1], at_ref[2]
    lane = lax.broadcasted_iota(jnp.int32, (CH, 2 * ASL), 0)
    slot = lax.broadcasted_iota(jnp.int32, (CH, 2 * ASL), 1)
    pick = (lane == y_at * ASL + slot % ASL).astype(F32)
    mean2 = hdot(mean_ref[...], pick)
    inv2 = hdot(inv_ref[...], pick)
    gain2 = hdot(gain_ref[...], pick)
    low = lax.broadcasted_iota(jnp.int32, (1, 2 * ASL), 1) < ASL
    lowest = lax.broadcasted_iota(jnp.int32, (3, COLS, 2 * ASL), 2) < ASL
    top = (lax.broadcasted_iota(jnp.int32, (3, COLS, 2 * ASL), 0) == 0) & (z_at == 0)
    bottom = (lax.broadcasted_iota(jnp.int32, (3, COLS, 2 * ASL), 0) == 2) & (z_at == NZ - 1)
    for y in range(NY):
        for c in range(NC):
            before = jnp.zeros((3, COLS, 2 * ASL), F32)
            block = 3 * COLS
            for m in range(FR // 2 + 1):
                if m < FR // 2:
                    raw = in_ref[y * NC + c, m * block : (m + 1) * block].astype(F32)
                    center = jnp.where(low, mean2[2 * m : 2 * m + 1], mean2[2 * m + 1 : 2 * m + 2])
                    scale = jnp.where(low, inv2[2 * m : 2 * m + 1], inv2[2 * m + 1 : 2 * m + 2])
                    gated = (raw - center) * scale * gain2
                    act = (gated * jax.nn.sigmoid(gated)).reshape(3, COLS, 2 * ASL)
                    if y == 0 and c == 0:
                        act = jnp.where(top, 0.0, act)
                    if y == NY - 1 and c == NC - 1:
                        act = jnp.where(bottom, 0.0, act)
                else:
                    act = jnp.zeros((3, COLS, 2 * ASL), F32)
                turned = pltpu.roll(act, ASL, 2)
                odd = jnp.where(lowest, before, turned)
                before = turned
                for k in range(3):
                    if m < FR // 2:
                        pad_ref[k, 2 * m + 2, y, 3 * c : 3 * c + 3] = shifted(act, k).astype(BF16)
                    pad_ref[k, 2 * m + 1, y, 3 * c : 3 * c + 3] = shifted(odd, k).astype(BF16)
            cells = in_ref[y * NC + c, AROWS:].reshape(FR, ROWS, COLS, BSL)
            live = frame_mask(cells.shape, count)
            cells = jnp.where(live, cells.astype(F32), 0.0)
            grad_ref[:, y, 2 * c : 2 * c + 2] = cells
    pad_ref[:, 0] = jnp.zeros((3, NY, 6, COLS, 2 * ASL), BF16)
    turned_grad = grad_ref[...].reshape(FR * NY * 4 * COLS, BSL).T.astype(BF16)
    for j in range(3):
        for k in range(3):
            early = pad_ref[k, 0:FR, :, j : j + 4].reshape(FR * NY * 4 * COLS, 2 * ASL)
            late = pad_ref[k, 2 : 2 + FR, :, j : j + 4].reshape(FR * NY * 4 * COLS, 2 * ASL)
            product = jnp.dot(
                turned_grad,
                jnp.concatenate([early, late], axis=1),
                preferred_element_type=F32,
            ).T
            for i in range(3):
                tap = (i * 3 + j) * 3 + k
                piece = product[i * ASL : (i + 1) * ASL].reshape(NZ, ASL // NZ, BSL)
                sum_ref[:, tap * 8 : tap * 8 + 8] = piece
    out_ref[...] = sum_ref[...].astype(BF16)


def forward_conv(x_ref, hp_ref, hn_ref, mean_ref, inv_ref, gain_ref, k_ref, at_ref, out_ref, pad_ref):
    count, s_at = at_ref[0], at_ref[3]
    rows = [hp_ref[0], x_ref[:, 0], x_ref[:, 1], hn_ref[0]]
    mean = mean_ref[...][:, None, :]
    inv = inv_ref[...][:, None, :]
    gain = gain_ref[...][None]
    for r in range(4):
        gated = (rows[r].astype(F32) - mean) * inv * gain
        act = gated * jax.nn.sigmoid(gated)
        if r == 0:
            act = jnp.where(s_at == 0, 0.0, act)
        if r == 3:
            act = jnp.where(s_at == SPACE - 1, 0.0, act)
        for k in range(3):
            pad_ref[k, 2:, r] = shifted(act, k).astype(BF16)
    pad_ref[:, :2] = jnp.zeros((3, 2, 4, COLS, CH), BF16)
    total = jnp.zeros((FR * CELLS, CH), F32)
    for i in range(3):
        for j in range(3):
            for k in range(3):
                window = pad_ref[k, i : i + FR, j : j + 2]
                total = total + jnp.dot(
                    window.reshape(FR * CELLS, CH),
                    k_ref[(i * 3 + j) * 3 + k],
                    preferred_element_type=F32,
                )
    cells = total.reshape(FR, ROWS, COLS, CH) + x_ref[...].astype(F32)
    out_ref[...] = jnp.where(frame_mask(cells.shape, count), cells, 0.0).astype(BF16)


def finish_input(b_ref, sc_ref, x_ref, g_ref, mean_ref, inv_ref, at_ref, out_ref, gain_ref):
    count = at_ref[0]
    sums = jnp.sum(b_ref[...], axis=0)
    spread = spread_matrix()
    first = hdot(sums[:, :GROUPS] / COUNT, spread)[:, None, :]
    second = hdot(sums[:, GROUPS : 2 * GROUPS] / COUNT, spread)[:, None, :]
    inv = inv_ref[...][:, None, :]
    xf = x_ref[...].astype(F32).reshape(FR, CELLS, CH)
    normalized = (xf - mean_ref[...][:, None, :]) * inv
    norm_grad = inv * (sc_ref[...] - first - normalized * second)
    grad = g_ref[...].astype(F32).reshape(FR, CELLS, CH)
    grad = jnp.where(frame_mask(grad.shape, count), grad, 0.0)
    out_ref[...] = (grad + norm_grad).astype(BF16).reshape(FR, ROWS, COLS, CH)
    fold_at = lax.broadcasted_iota(jnp.int32, (GROUPS, CH), 0)
    fold_lane = lax.broadcasted_iota(jnp.int32, (GROUPS, CH), 1)
    wide = hdot(sums[:, 2 * GROUPS :], (fold_lane % GROUPS == fold_at).astype(F32))
    row = lax.broadcasted_iota(jnp.int32, (FR, CH), 0)
    lane = lax.broadcasted_iota(jnp.int32, (FR, CH), 1)
    gain = jnp.sum(jnp.where(lane // GROUPS == row, wide, 0.0), axis=0, keepdims=True)
    gain_ref[0:1] = gain[:, :BSL]
    gain_ref[1:2] = gain[:, BSL:]


def sum_rows(in_ref, gain_ref, out_ref):
    total = jnp.sum(in_ref[...].astype(F32), axis=0).reshape(27, 8, BSL)
    gain = jnp.concatenate([gain_ref[...], jnp.zeros((2, BSL), F32)], axis=0)
    for x in range(NX):
        for c in range(NC):
            out_ref[x * NC + c, :27] = total[:, 4 * c : 4 * c + 4]
            out_ref[x * NC + c, 27] = gain


def sum_clips(in_ref, kg_ref, gain_ref):
    for c in range(NC):
        total = in_ref[c]
        for x in range(1, NX):
            total = total + in_ref[x * NC + c]
        kg_ref[:, :, c * BSL : (c + 1) * BSL] = total[:27]
        if c == 0:
            gain_ref[:, :BSL] = total[27, 0:1]
            gain_ref[:, BSL:] = total[27, 1:2]


def run(body, outs, args, scratch=(), smem=(), flops=0, out_tuple=True):
    specs = [
        pl.BlockSpec(memory_space=pltpu.SMEM if at in smem else pltpu.VMEM) for at in range(len(args))
    ]
    size = sum(a.size * a.dtype.itemsize for a in args)
    return pl.pallas_call(
        body,
        out_shape=tuple(jax.ShapeDtypeStruct(s, d) for s, d in outs),
        in_specs=specs,
        out_specs=tuple(pl.BlockSpec(memory_space=pltpu.VMEM) for _ in outs),
        scratch_shapes=list(scratch),
        compiler_params=pltpu.CompilerParams(vmem_limit_bytes=44 * 2**20),
        cost_estimate=pl.CostEstimate(flops=flops, bytes_accessed=size, transcendentals=0),
        name=body.__name__,
    )(*args)


def local(video_latent, frame_counts, conv_kernel, norm_gain, output_grad):
    x = video_latent.reshape(FR, ROWS, COLS, CH)
    g = output_grad.reshape(FR, ROWS, COLS, CH)
    gain = norm_gain.reshape(1, CH)
    y_at, z_at, c_at = lax.axis_index("y"), lax.axis_index("z"), lax.axis_index("c")
    s_at = (y_at * NZ + z_at) * NC + c_at
    at = jnp.stack([frame_counts[0], y_at, z_at, s_at]).astype(jnp.int32)
    space = ("y", "z", "c")
    cells = (FR, ROWS, COLS, CH)
    wide = (FR, CH)

    up, dn, stats = run(
        edges_and_sums,
        [((2, FR, COLS, CH), BF16), ((2, FR, COLS, CH), BF16), ((SPACE, FR, 2 * GROUPS), F32)],
        (x, g),
    )
    hp = lax.ppermute(dn, space, [(i, i + 1) for i in range(SPACE - 1)])
    hn = lax.ppermute(up, space, [(i + 1, i) for i in range(SPACE - 1)])
    stats = lax.all_to_all(stats, space, 0, 0)
    (packed,) = run(
        pack_slices,
        [((NY * NC, AROWS + GROWS, BSL), BF16)],
        (x, g, hp, hn, c_at.reshape(1).astype(jnp.int32)),
        smem=(4,),
    )
    packed = lax.all_to_all(packed, ("y", "c"), 0, 0)
    conv_flops = 2 * 27 * FR * CELLS * CH * CH
    padded = pltpu.VMEM((3, FR + 2, 4, COLS, CH), BF16)
    (act_grad,) = run(
        backward_conv,
        [((FR * CELLS, CH), F32)],
        (g, hp, hn, conv_kernel, at),
        scratch=[padded],
        smem=(4,),
        flops=conv_flops,
    )
    terms, scaled, mean, inv = run(
        group_terms,
        [((SPACE, FR, 3 * GROUPS), F32), ((FR, CELLS, CH), F32), (wide, F32), (wide, F32)],
        (stats, x, act_grad, gain),
    )
    terms = lax.all_to_all(terms, space, 0, 0)
    (partial,) = run(
        kernel_part,
        [((NZ, 27 * 8, BSL), BF16)],
        (packed, mean, inv, gain, at),
        scratch=[
            pltpu.VMEM((3, FR + 2, NY, 6, COLS, 2 * ASL), BF16),
            pltpu.VMEM((FR, NY, 4, COLS, BSL), F32),
            pltpu.VMEM((NZ, 27 * 8, BSL), F32),
        ],
        smem=(4,),
        flops=conv_flops,
    )
    partial = lax.all_to_all(partial, "z", 0, 0)
    (block_output,) = run(
        forward_conv,
        [(cells, BF16)],
        (x, hp, hn, mean, inv, gain, conv_kernel, at),
        scratch=[padded],
        smem=(7,),
        flops=conv_flops,
    )
    input_grad, gain_sum = run(
        finish_input,
        [(cells, BF16), ((2, BSL), F32)],
        (terms, scaled, x, g, mean, inv, at),
        smem=(6,),
    )
    (sums,) = run(sum_rows, [((NX * NC, 28, 4, BSL), F32)], (partial, gain_sum))
    sums = lax.all_to_all(sums, ("x", "c"), 0, 0)
    kernel_grad, gain_grad = run(sum_clips, [((27, 4, CH), F32), ((1, CH), F32)], (sums,))
    whole = (1,) + cells
    return (
        block_output.reshape(whole),
        input_grad.reshape(whole),
        jnp.swapaxes(kernel_grad, 0, 1),
        gain_grad.reshape(CH),
    )


def solution(mesh):
    fine = Mesh(mesh.devices.reshape(NX, NY, NZ, NC), ("x", "y", "z", "c"))
    space = ("y", "z", "c")
    cells = P("x", None, space, None, None)
    return jax.shard_map(
        local,
        mesh=fine,
        in_specs=(cells, P("x"), P(), P(), cells),
        out_specs=(cells, cells, P(space, None, None), P()),
        check_vma=False,
    )
```

```python
import jax
import jax.numpy as jnp
from jax import lax
from jax.experimental import pallas as pl
from jax.experimental.pallas import tpu as pltpu
from jax.sharding import Mesh
from jax.sharding import PartitionSpec as P

F32 = jnp.float32
BF16 = jnp.bfloat16
NX, NY, NZ, NC = 4, 4, 8, 2
SPACE = NY * NZ * NC
FR, ROWS, COLS, CH = 8, 2, 16, 256
CELLS = ROWS * COLS
GROUPS = 32
GC = CH // GROUPS
ASL = CH // NY
BSL = CH // NC
EPSILON = 1e-05
COUNT = CELLS * SPACE * GC
AROWS = FR // 2 * 3 * COLS
GROWS = FR * ROWS * COLS
TAPS = 27
PROWS = 112
HI = lax.Precision.HIGHEST


def hdot(a, b):
    return jnp.dot(a, b, preferred_element_type=F32, precision=HI)


def gather_matrix():
    lane = lax.broadcasted_iota(jnp.int32, (CH, GROUPS), 0)
    group = lax.broadcasted_iota(jnp.int32, (CH, GROUPS), 1)
    return (lane // GC == group).astype(F32)


def spread_matrix():
    group = lax.broadcasted_iota(jnp.int32, (GROUPS, CH), 0)
    lane = lax.broadcasted_iota(jnp.int32, (GROUPS, CH), 1)
    return (lane // GC == group).astype(F32)


def shifted(cells, k):
    if k == 1:
        return cells
    zero = jnp.zeros(cells.shape[:-2] + (1, cells.shape[-1]), cells.dtype)
    if k == 0:
        return jnp.concatenate([zero, cells[..., :-1, :]], axis=-2)
    return jnp.concatenate([cells[..., 1:, :], zero], axis=-2)


def edges_and_sums(x_ref, g_ref, n_ref, up_ref, dn_ref, st_ref, live_ref):
    up_ref[0] = x_ref[:, 0]
    up_ref[1] = g_ref[:, 0]
    dn_ref[0] = x_ref[:, 1]
    dn_ref[1] = g_ref[:, 1]
    live_ref[...] = (lax.broadcasted_iota(jnp.int32, (FR, CH), 0) < n_ref[0]).astype(F32)
    xf = x_ref[...].astype(F32).reshape(FR, CELLS, CH)
    gather = gather_matrix()
    mean = hdot(jnp.sum(xf, axis=1), gather) / (CELLS * GC)
    centered = xf - hdot(mean, spread_matrix())[:, None, :]
    squares = hdot(jnp.sum(centered * centered, axis=1), gather)
    st_ref[...] = jnp.concatenate([mean, squares, jnp.zeros((FR, 2 * GROUPS), F32)], axis=1)


def combined(parts, squares, each):
    count = parts.shape[0]
    mean = jnp.sum(parts, axis=0) / count
    apart = parts - mean[None]
    return mean, jnp.sum(squares + each * (apart * apart), axis=0)


def pair_sums(own_ref, other_ref, out_ref):
    both = jnp.stack([own_ref[...], other_ref[...]])
    mean, squares = combined(both[:, :, :GROUPS], both[:, :, GROUPS : 2 * GROUPS], CELLS * GC)
    row = jnp.concatenate([mean, squares, jnp.zeros((FR, 2 * GROUPS), F32)], axis=1)
    out_ref[...] = jnp.broadcast_to(row[None], (NY * NZ, FR, 128))


def pack_slices(x_ref, g_ref, hp_ref, hn_ref, out_ref):
    upper = lax.axis_index("c") == 0
    own = [x_ref[:, 0], x_ref[:, 1]]
    before, after = hp_ref[0], hn_ref[0]
    rows = [
        jnp.where(upper, before, own[0]),
        jnp.where(upper, own[0], own[1]),
        jnp.where(upper, own[1], after),
    ]
    three = jnp.stack(rows, axis=1).reshape(FR // 2, 2, 3, COLS, CH)
    for y in range(NY):
        part = three[..., y * ASL : (y + 1) * ASL]
        pair = jnp.concatenate([part[:, 0], part[:, 1]], axis=-1)
        out_ref[y, :AROWS] = pair.reshape(AROWS, 2 * ASL)
        for c in range(NC):
            at = AROWS + c * GROWS
            out_ref[y, at : at + GROWS] = g_ref[..., c * BSL : (c + 1) * BSL].reshape(GROWS, BSL)


def backward_conv(g_ref, hp_ref, hn_ref, k_ref, live_ref, out_ref, pad_ref):
    live = live_ref[...][:, None, :]
    rows = [hp_ref[1], g_ref[:, 0], g_ref[:, 1], hn_ref[1]]
    for r in range(4):
        cells = rows[r].astype(F32) * live
        for k in range(3):
            pad_ref[k, :FR, r] = shifted(cells, k).astype(BF16)
    pad_ref[:, FR:] = jnp.zeros((3, 2, 4, COLS, CH), BF16)
    total = jnp.zeros((FR * CELLS, CH), F32)
    for i in range(3):
        for j in range(3):
            for k in range(3):
                window = pad_ref[2 - k, 2 - i : 2 - i + FR, 2 - j : 4 - j]
                total = total + lax.dot_general(
                    window.reshape(FR * CELLS, CH),
                    k_ref[(i * 3 + j) * 3 + k],
                    (((1,), (1,)), ((), ())),
                    preferred_element_type=F32,
                )
    out_ref[...] = total


def group_terms(st_ref, x_ref, ag_ref, gain_ref, out_ref, sc_ref, mean_ref, inv_ref):
    mean, whole = combined(
        st_ref[:, :, :GROUPS], st_ref[:, :, GROUPS : 2 * GROUPS], NC * CELLS * GC
    )
    spread = spread_matrix()
    mean_all = hdot(mean, spread)
    inv_all = hdot(lax.rsqrt(whole / COUNT + EPSILON), spread)
    mean_ref[...] = mean_all
    inv_ref[...] = inv_all
    gain = gain_ref[...][None]
    xf = x_ref[...].astype(F32).reshape(FR, CELLS, CH)
    normalized = (xf - mean_all[:, None, :]) * inv_all[:, None, :]
    gated = normalized * gain
    sig = jax.nn.sigmoid(gated)
    pre = ag_ref[...].reshape(FR, CELLS, CH) * sig * (1.0 + gated * (1.0 - sig))
    scaled = pre * gain
    sc_ref[...] = scaled
    gather = gather_matrix()
    first = hdot(jnp.sum(scaled, axis=1), gather)
    by_channel = jnp.sum(pre * normalized, axis=1)
    second = hdot(by_channel * gain_ref[...], gather)
    gain_part = jnp.sum(by_channel, axis=0, keepdims=True)
    row = lax.broadcasted_iota(jnp.int32, (FR, CH), 0)
    lane = lax.broadcasted_iota(jnp.int32, (FR, CH), 1)
    folded = jnp.where(lane // GROUPS == row, jnp.broadcast_to(gain_part, (FR, CH)), 0.0)
    fold_lane = lax.broadcasted_iota(jnp.int32, (CH, GROUPS), 0)
    fold_at = lax.broadcasted_iota(jnp.int32, (CH, GROUPS), 1)
    folded = hdot(folded, (fold_lane % GROUPS == fold_at).astype(F32))
    everything = jnp.concatenate([first, second, folded, jnp.zeros((FR, GROUPS), F32)], axis=1)
    out_ref[...] = jnp.broadcast_to(everything[None], (NY * NC, FR, 128))


def kernel_part(*refs):
    blocks, (mean_h, inv_h, gain_h, live_h, keep_h, give_h) = refs[:8], refs[8:14]
    in_ref, mean_ref, inv_ref, gain_ref, live_ref, out_ref, pad_ref, grad_ref, sum_ref, sem = refs[14:]
    y_at, z_at, c_at = lax.axis_index("y"), lax.axis_index("z"), lax.axis_index("c")
    grads_at = pl.multiple_of(AROWS + c_at * GROWS, 64)
    copies = []
    for n in range(8):
        copies.append(
            pltpu.make_async_copy(blocks[n].at[:AROWS], in_ref.at[n, :AROWS], sem.at[2 * n])
        )
        copies.append(
            pltpu.make_async_copy(
                blocks[n].at[pl.ds(grads_at, GROWS)], in_ref.at[n, AROWS:], sem.at[2 * n + 1]
            )
        )
    for n, (src, dst) in enumerate(
        ((mean_h, mean_ref), (inv_h, inv_ref), (gain_h, gain_ref), (live_h, live_ref))
    ):
        copies.append(pltpu.make_async_copy(src, dst, sem.at[16 + n]))
    for copy in copies:
        copy.start()
    pad_ref[:, 0] = jnp.zeros((3, NY, 6, COLS, 2 * ASL), BF16)
    for copy in copies[16:]:
        copy.wait()
    lane = lax.broadcasted_iota(jnp.int32, (CH, 2 * ASL), 0)
    slot = lax.broadcasted_iota(jnp.int32, (CH, 2 * ASL), 1)
    pick = (lane == y_at * ASL + slot % ASL).astype(F32)
    mean2 = hdot(mean_ref[...], pick)
    inv2 = hdot(inv_ref[...], pick)
    gain2 = hdot(gain_ref[...], pick)
    live = live_ref[:, :BSL][:, None, None, :]
    shape = (3, COLS, 2 * ASL)
    low = lax.broadcasted_iota(jnp.int32, (1, 2 * ASL), 1) < ASL
    lowest = lax.broadcasted_iota(jnp.int32, shape, 2) < ASL
    row = lax.broadcasted_iota(jnp.int32, shape, 0)
    block = 3 * COLS
    for n in range(8):
        copies[2 * n].wait()
        copies[2 * n + 1].wait()
        d = n % 4
        y = lax.rem(y_at + NY - d, NY)
        c = c_at if n < 4 else 1 - c_at
        top = (y == 0) & (z_at == 0) & (c == 0)
        bottom = (y == NY - 1) & (z_at == NZ - 1) & (c == NC - 1)
        edge = jnp.where(top, 0, jnp.where(bottom, 2, 3))
        inside = (row != edge).astype(F32)
        before = jnp.zeros(shape, F32)
        for m in range(FR // 2 + 1):
            if m < FR // 2:
                raw = in_ref[n, m * block : (m + 1) * block].astype(F32)
                center = jnp.where(low, mean2[2 * m : 2 * m + 1], mean2[2 * m + 1 : 2 * m + 2])
                scale = jnp.where(low, inv2[2 * m : 2 * m + 1], inv2[2 * m + 1 : 2 * m + 2])
                gated = (raw - center) * scale * gain2
                act = (gated * jax.nn.sigmoid(gated)).reshape(shape) * inside
            else:
                act = jnp.zeros(shape, F32)
            turned = pltpu.roll(act, ASL, 2)
            odd = jnp.where(lowest, before, turned)
            before = turned
            for k in range(3):
                if m < FR // 2:
                    pad_ref[k, 2 * m + 2, d, pl.ds(3 * c, 3)] = shifted(act, k).astype(BF16)
                pad_ref[k, 2 * m + 1, d, pl.ds(3 * c, 3)] = shifted(odd, k).astype(BF16)
        cells = in_ref[n, AROWS:].astype(F32).reshape(FR, ROWS, COLS, BSL) * live
        grad_ref[:, d, pl.ds(2 * c, 2)] = cells
    turned_grad = grad_ref[...].reshape(FR * NY * 4 * COLS, BSL).T.astype(BF16)
    sum_ref[:, :, 4 * TAPS :] = jnp.zeros((NC, NZ, PROWS - 4 * TAPS, BSL), F32)
    for j in range(3):
        for k in range(3):
            early = pad_ref[k, 0:FR, :, j : j + 4].reshape(FR * NY * 4 * COLS, 2 * ASL)
            late = pad_ref[k, 2 : 2 + FR, :, j : j + 4].reshape(FR * NY * 4 * COLS, 2 * ASL)
            product = jnp.dot(
                turned_grad,
                jnp.concatenate([early, late], axis=1),
                preferred_element_type=F32,
            ).T
            for i in range(3):
                tap = (i * 3 + j) * 3 + k
                piece = product[i * ASL : (i + 1) * ASL].reshape(NZ, ASL // NZ, BSL)
                sum_ref[0, :, tap * 4 : tap * 4 + 4] = piece[:, :4]
                sum_ref[1, :, tap * 4 : tap * 4 + 4] = piece[:, 4:]
    out_ref[...] = sum_ref[...].astype(BF16)
    keep = pltpu.make_async_copy(out_ref.at[c_at], keep_h, sem.at[0])
    give = pltpu.make_async_copy(out_ref.at[1 - c_at], give_h, sem.at[1])
    give.start()
    keep.start()
    give.wait()
    keep.wait()


def merge_parts(keep_ref, got_ref, b_ref, out_ref):
    first = lax.axis_index("c") == 0
    keep, got = keep_ref[...], got_ref[...]
    out_ref[:, :PROWS] = jnp.where(first, keep, got)
    out_ref[:, PROWS : 2 * PROWS] = jnp.where(first, got, keep)
    sums = jnp.sum(b_ref[...], axis=0)
    high = sums.astype(BF16).astype(F32)
    middle = (sums - high).astype(BF16).astype(F32)
    low = sums - high - middle
    terms = jnp.concatenate([high, middle, low, jnp.zeros((FR, 128), F32)], axis=0).astype(BF16)
    out_ref[:, 2 * PROWS :] = jnp.broadcast_to(terms[None], (NZ, 4 * FR, 128))


def sum_rows(in_ref, out_ref, sums_ref):
    total = jnp.sum(in_ref[...].astype(F32), axis=0)
    at = 2 * PROWS
    sums = (total[at + 2 * FR : at + 3 * FR] + total[at + FR : at + 2 * FR]) + total[at : at + FR]
    sums_ref[...] = sums
    fold_at = lax.broadcasted_iota(jnp.int32, (GROUPS, CH), 0)
    fold_lane = lax.broadcasted_iota(jnp.int32, (GROUPS, CH), 1)
    wide = hdot(sums[:, 2 * GROUPS : 3 * GROUPS], (fold_lane % GROUPS == fold_at).astype(F32))
    row = lax.broadcasted_iota(jnp.int32, (FR, CH), 0)
    lane = lax.broadcasted_iota(jnp.int32, (FR, CH), 1)
    gain = jnp.sum(jnp.where(lane // GROUPS == row, wide, 0.0), axis=0, keepdims=True)
    out_ref[:, :BSL] = total[:PROWS]
    out_ref[:, BSL:] = total[PROWS : 2 * PROWS]
    out_ref[4 * TAPS : 4 * TAPS + 1] = gain


def forward_conv(x_ref, hp_ref, hn_ref, mean_ref, inv_ref, gain_ref, k_ref, live_ref, out_ref, pad_ref):
    s_at = (lax.axis_index("y") * NZ + lax.axis_index("z")) * NC + lax.axis_index("c")
    rows = [hp_ref[0], x_ref[:, 0], x_ref[:, 1], hn_ref[0]]
    mean = mean_ref[...][:, None, :]
    inv = inv_ref[...][:, None, :]
    gain = gain_ref[...][None]
    for r in range(4):
        gated = (rows[r].astype(F32) - mean) * inv * gain
        act = gated * jax.nn.sigmoid(gated)
        if r == 0:
            act = jnp.where(s_at == 0, 0.0, act)
        if r == 3:
            act = jnp.where(s_at == SPACE - 1, 0.0, act)
        for k in range(3):
            pad_ref[k, 2:, r] = shifted(act, k).astype(BF16)
    pad_ref[:, :2] = jnp.zeros((3, 2, 4, COLS, CH), BF16)
    total = jnp.zeros((FR * CELLS, CH), F32)
    for i in range(3):
        for j in range(3):
            for k in range(3):
                window = pad_ref[k, i : i + FR, j : j + 2]
                total = total + jnp.dot(
                    window.reshape(FR * CELLS, CH),
                    k_ref[(i * 3 + j) * 3 + k],
                    preferred_element_type=F32,
                )
    cells = total.reshape(FR, CELLS, CH) + x_ref[...].astype(F32).reshape(FR, CELLS, CH)
    cells = cells * live_ref[...][:, None, :]
    out_ref[...] = cells.astype(BF16).reshape(FR, ROWS, COLS, CH)


def finish_input(sums_ref, sc_ref, x_ref, g_ref, mean_ref, inv_ref, live_ref, out_ref):
    sums = sums_ref[...]
    spread = spread_matrix()
    first = hdot(sums[:, :GROUPS] / COUNT, spread)[:, None, :]
    second = hdot(sums[:, GROUPS : 2 * GROUPS] / COUNT, spread)[:, None, :]
    inv = inv_ref[...][:, None, :]
    xf = x_ref[...].astype(F32).reshape(FR, CELLS, CH)
    normalized = (xf - mean_ref[...][:, None, :]) * inv
    norm_grad = inv * (sc_ref[...] - first - normalized * second)
    grad = g_ref[...].astype(F32).reshape(FR, CELLS, CH) * live_ref[...][:, None, :]
    out_ref[...] = (grad + norm_grad).astype(BF16).reshape(FR, ROWS, COLS, CH)


def sum_clips(own_h, one_h, two_h, three_h, kg_h, gain_h, in_ref, kg_ref, gain_ref, sem):
    x_at = lax.axis_index("x")
    copies = []
    for d, src in enumerate((own_h, one_h, two_h, three_h)):
        copies.append(
            pltpu.make_async_copy(src, in_ref.at[lax.rem(x_at + NX - d, NX)], sem.at[d])
        )
    for copy in copies:
        copy.start()
    for copy in copies:
        copy.wait()
    total = ((in_ref[0] + in_ref[1]) + in_ref[2]) + in_ref[3]
    for tap in range(TAPS):
        kg_ref[tap] = total[4 * tap : 4 * tap + 4]
    gain_ref[...] = total[4 * TAPS : 4 * TAPS + 1]
    out = (
        pltpu.make_async_copy(kg_ref, kg_h, sem.at[4]),
        pltpu.make_async_copy(gain_ref, gain_h, sem.at[5]),
    )
    for copy in out:
        copy.start()
    for copy in out:
        copy.wait()


HBM = pl.BlockSpec(memory_space=pltpu.HBM)
VMEM = pl.BlockSpec(memory_space=pltpu.VMEM)
SMEM = pl.BlockSpec(memory_space=pltpu.SMEM)


def shapes(outs):
    return tuple(jax.ShapeDtypeStruct(s, d) for s, d in outs)


def call(body, outs, args, specs, scratch, flops=0, limit=32):
    return pl.pallas_call(
        body,
        out_shape=shapes(outs),
        in_specs=specs,
        out_specs=tuple(HBM for _ in outs),
        scratch_shapes=list(scratch),
        compiler_params=pltpu.CompilerParams(vmem_limit_bytes=limit * 2**20),
        cost_estimate=pl.CostEstimate(flops=flops, bytes_accessed=2**20, transcendentals=0),
        name=body.__name__,
    )(*args)


def run(body, outs, args, scratch=(), stay=(), smem=(), flops=0):
    count, outputs = len(args), len(outs)
    moved = [at for at in range(count) if at not in stay and at not in smem]

    def kernel(*refs):
        ins, targets = list(refs[:count]), refs[count : count + outputs]
        rest = refs[count + outputs :]
        buffers, rest = rest[: len(moved)], rest[len(moved) :]
        results, rest = rest[:outputs], rest[outputs:]
        sem, extra = rest[0], rest[1:]
        copies = [
            pltpu.make_async_copy(ins[at], buffers[n], sem.at[n]) for n, at in enumerate(moved)
        ]
        for copy in copies:
            copy.start()
        for n, at in enumerate(moved):
            ins[at] = buffers[n]
        for copy in copies:
            copy.wait()
        body(*ins, *results, *extra)
        copies = [
            pltpu.make_async_copy(results[n], targets[n], sem.at[len(moved) + n])
            for n in range(outputs)
        ]
        for copy in copies:
            copy.start()
        for copy in copies:
            copy.wait()

    kernel.__name__ = body.__name__
    specs = [VMEM if at in stay else SMEM if at in smem else HBM for at in range(count)]
    buffers = [pltpu.VMEM(args[at].shape, args[at].dtype) for at in moved]
    buffers += [pltpu.VMEM(s, d) for s, d in outs]
    buffers += [pltpu.SemaphoreType.DMA((len(moved) + outputs,))]
    return call(kernel, outs, args, specs, buffers + list(scratch), flops)


def pack_body(x_h, g_h, hp_h, hn_h, out0, out1, out2, out3, x_ref, g_ref, hp_ref, hn_ref, buf, sem):
    pairs = ((x_h, x_ref), (g_h, g_ref), (hp_h, hp_ref), (hn_h, hn_ref))
    copies = [pltpu.make_async_copy(a, b, sem.at[n]) for n, (a, b) in enumerate(pairs)]
    for copy in copies:
        copy.start()
    for copy in copies:
        copy.wait()
    pack_slices(x_ref, g_ref, hp_ref, hn_ref, buf)
    y_at = lax.axis_index("y")
    copies = [
        pltpu.make_async_copy(buf.at[lax.rem(y_at + d, NY)], out, sem.at[4 + d])
        for d, out in enumerate((out0, out1, out2, out3))
    ]
    for copy in copies:
        copy.start()
    for copy in copies:
        copy.wait()


def local(video_latent, frame_counts, conv_kernel, norm_gain, output_grad):
    x = video_latent.reshape(FR, ROWS, COLS, CH)
    g = output_grad.reshape(FR, ROWS, COLS, CH)
    gain = norm_gain.reshape(1, CH)
    space = ("y", "z", "c")
    cells = (FR, ROWS, COLS, CH)
    wide = (FR, CH)
    halo = (2, FR, COLS, CH)
    swap = [(0, 1), (1, 0)]
    dma = pltpu.SemaphoreType.DMA

    up, dn, stats, live = run(
        edges_and_sums,
        [(halo, BF16), (halo, BF16), ((FR, 128), F32), (wide, F32)],
        (x, g, frame_counts),
        smem=(2,),
    )
    other = lax.ppermute(stats, "c", swap)
    hp = lax.ppermute(dn, space, [(i, i + 1) for i in range(SPACE - 1)])
    hn = lax.ppermute(up, space, [(i + 1, i) for i in range(SPACE - 1)])
    (stats,) = run(pair_sums, [((NY * NZ, FR, 128), F32)], (stats, other))
    stats, hp, hn = lax.optimization_barrier((stats, hp, hn))
    stats = lax.all_to_all(stats, ("y", "z"), 0, 0)
    block = (AROWS + NC * GROWS, BSL)
    packed = call(
        pack_body,
        [(block, BF16)] * NY,
        (x, g, hp, hn),
        [HBM] * 4,
        [pltpu.VMEM(cells, BF16)] * 2
        + [pltpu.VMEM(halo, BF16)] * 2
        + [pltpu.VMEM((NY,) + block, BF16), dma((8,))],
    )
    near = [packed[0]] + [
        lax.ppermute(packed[d], "y", [(i, (i + d) % NY) for i in range(NY)]) for d in range(1, NY)
    ]
    far = [lax.ppermute(a, "c", swap) for a in near]
    conv_flops = 16 * TAPS * FR * CELLS * CH * CH
    padded = pltpu.VMEM((3, FR + 2, 4, COLS, CH), BF16)
    (act_grad,) = run(
        backward_conv,
        [((FR * CELLS, CH), F32)],
        (g, hp, hn, conv_kernel, live),
        scratch=[padded],
        stay=(3,),
        flops=conv_flops,
    )
    terms, scaled, mean, inv = run(
        group_terms,
        [((NY * NC, FR, 128), F32), ((FR, CELLS, CH), F32), (wide, F32), (wide, F32)],
        (stats, x, act_grad, gain),
    )
    terms = lax.all_to_all(terms, ("y", "c"), 0, 0)
    part = (NZ, PROWS, BSL)
    keep, give = call(
        kernel_part,
        [(part, BF16)] * 2,
        (*near, *far, mean, inv, gain, live),
        [HBM] * 12,
        [
            pltpu.VMEM((8, AROWS + GROWS, BSL), BF16),
            pltpu.VMEM(wide, F32),
            pltpu.VMEM(wide, F32),
            pltpu.VMEM((1, CH), F32),
            pltpu.VMEM(wide, F32),
            pltpu.VMEM((NC,) + part, BF16),
            pltpu.VMEM((3, FR + 2, NY, 6, COLS, 2 * ASL), BF16),
            pltpu.VMEM((FR, NY, 4, COLS, BSL), F32),
            pltpu.VMEM((NC,) + part, F32),
            dma((20,)),
        ],
        flops=conv_flops,
    )
    got = lax.ppermute(give, "c", swap)
    (merged,) = run(
        merge_parts, [((NZ, 2 * PROWS + 4 * FR, BSL), BF16)], (keep, got, terms)
    )
    merged, late_mean = lax.optimization_barrier((merged, mean))
    merged = lax.all_to_all(merged, "z", 0, 0)
    (block_output,) = run(
        forward_conv,
        [(cells, BF16)],
        (x, hp, hn, late_mean, inv, gain, conv_kernel, live),
        scratch=[padded],
        stay=(6,),
        flops=conv_flops,
    )
    merged, block_output = lax.optimization_barrier((merged, block_output))
    rows, sums = run(sum_rows, [((PROWS, CH), F32), ((FR, 128), F32)], (merged,))
    others = [
        lax.ppermute(rows, "x", [(i, (i + d) % NX) for i in range(NX)]) for d in range(1, NX)
    ]
    (input_grad,) = run(
        finish_input, [(cells, BF16)], (sums, scaled, x, g, mean, inv, live)
    )
    kernel_grad, gain_grad = call(
        sum_clips,
        [((TAPS, 4, CH), F32), ((1, CH), F32)],
        (rows, *others),
        [HBM] * 4,
        [
            pltpu.VMEM((NX, PROWS, CH), F32),
            pltpu.VMEM((TAPS, 4, CH), F32),
            pltpu.VMEM((1, CH), F32),
            dma((6,)),
        ],
    )
    whole = (1,) + cells
    return (
        block_output.reshape(whole),
        input_grad.reshape(whole),
        jnp.swapaxes(kernel_grad, 0, 1),
        gain_grad.reshape(CH),
    )


def solution(mesh):
    fine = Mesh(mesh.devices.reshape(NX, NY, NZ, NC), ("x", "y", "z", "c"))
    space = ("y", "z", "c")
    cells = P("x", None, space, None, None)
    return jax.shard_map(
        local,
        mesh=fine,
        in_specs=(cells, P("x"), P(), P(), cells),
        out_specs=(cells, cells, P(space, None, None), P()),
        check_vma=False,
    )
```

```python
import jax
import jax.numpy as jnp
from jax import lax
from jax.experimental import pallas as pl
from jax.experimental.pallas import tpu as pltpu
from jax.sharding import Mesh
from jax.sharding import PartitionSpec as P

F32 = jnp.float32
BF16 = jnp.bfloat16
NX, NY, NZ, NC = 4, 4, 8, 2
SPACE = NY * NZ * NC
FR, ROWS, COLS, CH = 8, 2, 16, 256
CELLS = ROWS * COLS
GROUPS = 32
GC = CH // GROUPS
ASL = CH // NY
BSL = CH // NC
EPSILON = 1e-05
COUNT = CELLS * SPACE * GC
AROWS = FR // 2 * 3 * COLS
GROWS = FR * ROWS * COLS
TAPS = 27
PROWS = 112
HI = lax.Precision.HIGHEST


def hdot(a, b):
    return jnp.dot(a, b, preferred_element_type=F32, precision=HI)


def gather_matrix():
    lane = lax.broadcasted_iota(jnp.int32, (CH, GROUPS), 0)
    group = lax.broadcasted_iota(jnp.int32, (CH, GROUPS), 1)
    return (lane // GC == group).astype(F32)


def spread_matrix():
    group = lax.broadcasted_iota(jnp.int32, (GROUPS, CH), 0)
    lane = lax.broadcasted_iota(jnp.int32, (GROUPS, CH), 1)
    return (lane // GC == group).astype(F32)


def shifted(cells, k):
    if k == 1:
        return cells
    zero = jnp.zeros(cells.shape[:-2] + (1, cells.shape[-1]), cells.dtype)
    if k == 0:
        return jnp.concatenate([zero, cells[..., :-1, :]], axis=-2)
    return jnp.concatenate([cells[..., 1:, :], zero], axis=-2)


def edges_and_sums(x_ref, g_ref, n_ref, up_ref, dn_ref, st_ref, live_ref):
    up_ref[0] = x_ref[:, 0]
    up_ref[1] = g_ref[:, 0]
    dn_ref[0] = x_ref[:, 1]
    dn_ref[1] = g_ref[:, 1]
    live_ref[...] = (lax.broadcasted_iota(jnp.int32, (FR, CH), 0) < n_ref[0]).astype(F32)
    xf = x_ref[...].astype(F32).reshape(FR, CELLS, CH)
    gather = gather_matrix()
    mean = hdot(jnp.sum(xf, axis=1), gather) / (CELLS * GC)
    centered = xf - hdot(mean, spread_matrix())[:, None, :]
    squares = hdot(jnp.sum(centered * centered, axis=1), gather)
    st_ref[...] = jnp.concatenate([mean, squares, jnp.zeros((FR, 2 * GROUPS), F32)], axis=1)


def combined(parts, squares, each):
    count = parts.shape[0]
    mean = jnp.sum(parts, axis=0) / count
    apart = parts - mean[None]
    return mean, jnp.sum(squares + each * (apart * apart), axis=0)


def pair_sums(own_ref, other_ref, out_ref):
    both = jnp.stack([own_ref[...], other_ref[...]])
    mean, squares = combined(both[:, :, :GROUPS], both[:, :, GROUPS : 2 * GROUPS], CELLS * GC)
    row = jnp.concatenate([mean, squares, jnp.zeros((FR, 2 * GROUPS), F32)], axis=1)
    out_ref[...] = jnp.broadcast_to(row[None], (NY * NZ, FR, 128))


def pack_slices(x_ref, g_ref, hp_ref, hn_ref, out_ref):
    upper = lax.axis_index("c") == 0
    own = [x_ref[:, 0], x_ref[:, 1]]
    before, after = hp_ref[0], hn_ref[0]
    rows = [
        jnp.where(upper, before, own[0]),
        jnp.where(upper, own[0], own[1]),
        jnp.where(upper, own[1], after),
    ]
    three = jnp.stack(rows, axis=1).reshape(FR // 2, 2, 3, COLS, CH)
    for y in range(NY):
        part = three[..., y * ASL : (y + 1) * ASL]
        pair = jnp.concatenate([part[:, 0], part[:, 1]], axis=-1)
        out_ref[y, :AROWS] = pair.reshape(AROWS, 2 * ASL)
        for c in range(NC):
            at = AROWS + c * GROWS
            out_ref[y, at : at + GROWS] = g_ref[..., c * BSL : (c + 1) * BSL].reshape(GROWS, BSL)


def backward_conv(g_ref, hp_ref, hn_ref, k_ref, live_ref, out_ref, pad_ref, held):
    live = live_ref[...][:, None, :]
    rows = [hp_ref[1], g_ref[:, 0], g_ref[:, 1], hn_ref[1]]
    for r in range(4):
        cells = rows[r].astype(F32) * live
        for k in range(3):
            pad_ref[k, :FR, r] = shifted(cells, k).astype(BF16)
    pad_ref[:, FR:] = jnp.zeros((3, 2, 4, COLS, CH), BF16)
    held.wait()
    total = jnp.zeros((FR * CELLS, CH), F32)
    for i in range(3):
        for j in range(3):
            for k in range(3):
                window = pad_ref[2 - k, 2 - i : 2 - i + FR, 2 - j : 4 - j]
                total = total + lax.dot_general(
                    window.reshape(FR * CELLS, CH),
                    k_ref[(i * 3 + j) * 3 + k],
                    (((1,), (1,)), ((), ())),
                    preferred_element_type=F32,
                )
    out_ref[...] = total


def group_terms(st_ref, x_ref, ag_ref, gain_ref, out_ref, sc_ref, mean_ref, inv_ref):
    mean, whole = combined(
        st_ref[:, :, :GROUPS], st_ref[:, :, GROUPS : 2 * GROUPS], NC * CELLS * GC
    )
    spread = spread_matrix()
    mean_all = hdot(mean, spread)
    inv_all = hdot(lax.rsqrt(whole / COUNT + EPSILON), spread)
    mean_ref[...] = mean_all
    inv_ref[...] = inv_all
    gain = gain_ref[...][None]
    xf = x_ref[...].astype(F32).reshape(FR, CELLS, CH)
    normalized = (xf - mean_all[:, None, :]) * inv_all[:, None, :]
    gated = normalized * gain
    sig = jax.nn.sigmoid(gated)
    pre = ag_ref[...].reshape(FR, CELLS, CH) * sig * (1.0 + gated * (1.0 - sig))
    scaled = pre * gain
    sc_ref[...] = scaled
    gather = gather_matrix()
    first = hdot(jnp.sum(scaled, axis=1), gather)
    by_channel = jnp.sum(pre * normalized, axis=1)
    second = hdot(by_channel * gain_ref[...], gather)
    gain_part = jnp.sum(by_channel, axis=0, keepdims=True)
    row = lax.broadcasted_iota(jnp.int32, (FR, CH), 0)
    lane = lax.broadcasted_iota(jnp.int32, (FR, CH), 1)
    folded = jnp.where(lane // GROUPS == row, jnp.broadcast_to(gain_part, (FR, CH)), 0.0)
    fold_lane = lax.broadcasted_iota(jnp.int32, (CH, GROUPS), 0)
    fold_at = lax.broadcasted_iota(jnp.int32, (CH, GROUPS), 1)
    folded = hdot(folded, (fold_lane % GROUPS == fold_at).astype(F32))
    everything = jnp.concatenate([first, second, folded, jnp.zeros((FR, GROUPS), F32)], axis=1)
    out_ref[...] = jnp.broadcast_to(everything[None], (NY * NC, FR, 128))


def kernel_part(*refs):
    blocks, (mean_h, inv_h, gain_h, live_h, keep_h, give_h) = refs[:8], refs[8:14]
    in_ref, mean_ref, inv_ref, gain_ref, live_ref, out_ref, pad_ref, grad_ref, sum_ref, sem = refs[14:]
    y_at, z_at, c_at = lax.axis_index("y"), lax.axis_index("z"), lax.axis_index("c")
    grads_at = pl.multiple_of(AROWS + c_at * GROWS, 64)
    copies = []
    for n in range(8):
        copies.append(
            pltpu.make_async_copy(blocks[n].at[:AROWS], in_ref.at[n, :AROWS], sem.at[2 * n])
        )
        copies.append(
            pltpu.make_async_copy(
                blocks[n].at[pl.ds(grads_at, GROWS)], in_ref.at[n, AROWS:], sem.at[2 * n + 1]
            )
        )
    for n, (src, dst) in enumerate(
        ((mean_h, mean_ref), (inv_h, inv_ref), (gain_h, gain_ref), (live_h, live_ref))
    ):
        copies.append(pltpu.make_async_copy(src, dst, sem.at[16 + n]))
    for copy in copies:
        copy.start()
    pad_ref[:, 0] = jnp.zeros((3, NY, 6, COLS, 2 * ASL), BF16)
    for copy in copies[16:]:
        copy.wait()
    lane = lax.broadcasted_iota(jnp.int32, (CH, 2 * ASL), 0)
    slot = lax.broadcasted_iota(jnp.int32, (CH, 2 * ASL), 1)
    pick = (lane == y_at * ASL + slot % ASL).astype(F32)
    mean2 = hdot(mean_ref[...], pick)
    inv2 = hdot(inv_ref[...], pick)
    gain2 = hdot(gain_ref[...], pick)
    live = live_ref[:, :BSL][:, None, None, :]
    shape = (3, COLS, 2 * ASL)
    low = lax.broadcasted_iota(jnp.int32, (1, 2 * ASL), 1) < ASL
    lowest = lax.broadcasted_iota(jnp.int32, shape, 2) < ASL
    row = lax.broadcasted_iota(jnp.int32, shape, 0)
    block = 3 * COLS
    for n in range(8):
        copies[2 * n].wait()
        copies[2 * n + 1].wait()
        d = n % 4
        y = lax.rem(y_at + NY - d, NY)
        c = c_at if n < 4 else 1 - c_at
        top = (y == 0) & (z_at == 0) & (c == 0)
        bottom = (y == NY - 1) & (z_at == NZ - 1) & (c == NC - 1)
        edge = jnp.where(top, 0, jnp.where(bottom, 2, 3))
        inside = (row != edge).astype(F32)
        before = jnp.zeros(shape, F32)
        for m in range(FR // 2 + 1):
            if m < FR // 2:
                raw = in_ref[n, m * block : (m + 1) * block].astype(F32)
                center = jnp.where(low, mean2[2 * m : 2 * m + 1], mean2[2 * m + 1 : 2 * m + 2])
                scale = jnp.where(low, inv2[2 * m : 2 * m + 1], inv2[2 * m + 1 : 2 * m + 2])
                gated = (raw - center) * scale * gain2
                act = (gated * jax.nn.sigmoid(gated)).reshape(shape) * inside
            else:
                act = jnp.zeros(shape, F32)
            turned = pltpu.roll(act, ASL, 2)
            odd = jnp.where(lowest, before, turned)
            before = turned
            for k in range(3):
                if m < FR // 2:
                    pad_ref[k, 2 * m + 2, d, pl.ds(3 * c, 3)] = shifted(act, k).astype(BF16)
                pad_ref[k, 2 * m + 1, d, pl.ds(3 * c, 3)] = shifted(odd, k).astype(BF16)
        cells = in_ref[n, AROWS:].astype(F32).reshape(FR, ROWS, COLS, BSL) * live
        grad_ref[:, d, pl.ds(2 * c, 2)] = cells
    turned_grad = grad_ref[...].reshape(FR * NY * 4 * COLS, BSL).T.astype(BF16)
    sum_ref[:, :, 4 * TAPS :] = jnp.zeros((NC, NZ, PROWS - 4 * TAPS, BSL), F32)
    for j in range(3):
        for k in range(3):
            early = pad_ref[k, 0:FR, :, j : j + 4].reshape(FR * NY * 4 * COLS, 2 * ASL)
            late = pad_ref[k, 2 : 2 + FR, :, j : j + 4].reshape(FR * NY * 4 * COLS, 2 * ASL)
            product = jnp.dot(
                turned_grad,
                jnp.concatenate([early, late], axis=1),
                preferred_element_type=F32,
            ).T
            for i in range(3):
                tap = (i * 3 + j) * 3 + k
                piece = product[i * ASL : (i + 1) * ASL].reshape(NZ, ASL // NZ, BSL)
                sum_ref[0, :, tap * 4 : tap * 4 + 4] = piece[:, :4]
                sum_ref[1, :, tap * 4 : tap * 4 + 4] = piece[:, 4:]
    out_ref[...] = sum_ref[...].astype(BF16)
    keep = pltpu.make_async_copy(out_ref.at[c_at], keep_h, sem.at[0])
    give = pltpu.make_async_copy(out_ref.at[1 - c_at], give_h, sem.at[1])
    give.start()
    keep.start()
    give.wait()
    keep.wait()


def merge_parts(keep_ref, got_ref, b_ref, out_ref):
    first = lax.axis_index("c") == 0
    keep, got = keep_ref[...], got_ref[...]
    out_ref[:, :PROWS] = jnp.where(first, keep, got)
    out_ref[:, PROWS : 2 * PROWS] = jnp.where(first, got, keep)
    sums = jnp.sum(b_ref[...], axis=0)
    high = sums.astype(BF16).astype(F32)
    middle = (sums - high).astype(BF16).astype(F32)
    low = sums - high - middle
    terms = jnp.concatenate([high, middle, low, jnp.zeros((FR, 128), F32)], axis=0).astype(BF16)
    out_ref[:, 2 * PROWS :] = jnp.broadcast_to(terms[None], (NZ, 4 * FR, 128))


def sum_rows(in_ref, out_ref, sums_ref):
    total = jnp.sum(in_ref[...].astype(F32), axis=0)
    at = 2 * PROWS
    sums = (total[at + 2 * FR : at + 3 * FR] + total[at + FR : at + 2 * FR]) + total[at : at + FR]
    sums_ref[...] = sums
    fold_at = lax.broadcasted_iota(jnp.int32, (GROUPS, CH), 0)
    fold_lane = lax.broadcasted_iota(jnp.int32, (GROUPS, CH), 1)
    wide = hdot(sums[:, 2 * GROUPS : 3 * GROUPS], (fold_lane % GROUPS == fold_at).astype(F32))
    row = lax.broadcasted_iota(jnp.int32, (FR, CH), 0)
    lane = lax.broadcasted_iota(jnp.int32, (FR, CH), 1)
    gain = jnp.sum(jnp.where(lane // GROUPS == row, wide, 0.0), axis=0, keepdims=True)
    out_ref[:, :BSL] = total[:PROWS]
    out_ref[:, BSL:] = total[PROWS : 2 * PROWS]
    out_ref[4 * TAPS : 4 * TAPS + 1] = gain


def forward_conv(x_ref, hp_ref, hn_ref, mean_ref, inv_ref, gain_ref, k_ref, live_ref, out_ref, pad_ref, held):
    s_at = (lax.axis_index("y") * NZ + lax.axis_index("z")) * NC + lax.axis_index("c")
    rows = [hp_ref[0], x_ref[:, 0], x_ref[:, 1], hn_ref[0]]
    mean = mean_ref[...][:, None, :]
    inv = inv_ref[...][:, None, :]
    gain = gain_ref[...][None]
    for r in range(4):
        gated = (rows[r].astype(F32) - mean) * inv * gain
        act = gated * jax.nn.sigmoid(gated)
        if r == 0:
            act = jnp.where(s_at == 0, 0.0, act)
        if r == 3:
            act = jnp.where(s_at == SPACE - 1, 0.0, act)
        for k in range(3):
            pad_ref[k, 2:, r] = shifted(act, k).astype(BF16)
    pad_ref[:, :2] = jnp.zeros((3, 2, 4, COLS, CH), BF16)
    held.wait()
    total = jnp.zeros((FR * CELLS, CH), F32)
    for i in range(3):
        for j in range(3):
            for k in range(3):
                window = pad_ref[k, i : i + FR, j : j + 2]
                total = total + jnp.dot(
                    window.reshape(FR * CELLS, CH),
                    k_ref[(i * 3 + j) * 3 + k],
                    preferred_element_type=F32,
                )
    cells = total.reshape(FR, CELLS, CH) + x_ref[...].astype(F32).reshape(FR, CELLS, CH)
    cells = cells * live_ref[...][:, None, :]
    out_ref[...] = cells.astype(BF16).reshape(FR, ROWS, COLS, CH)


def finish_input(sums_ref, sc_ref, x_ref, g_ref, mean_ref, inv_ref, live_ref, out_ref):
    sums = sums_ref[...]
    spread = spread_matrix()
    first = hdot(sums[:, :GROUPS] / COUNT, spread)[:, None, :]
    second = hdot(sums[:, GROUPS : 2 * GROUPS] / COUNT, spread)[:, None, :]
    inv = inv_ref[...][:, None, :]
    xf = x_ref[...].astype(F32).reshape(FR, CELLS, CH)
    normalized = (xf - mean_ref[...][:, None, :]) * inv
    norm_grad = inv * (sc_ref[...] - first - normalized * second)
    grad = g_ref[...].astype(F32).reshape(FR, CELLS, CH) * live_ref[...][:, None, :]
    out_ref[...] = (grad + norm_grad).astype(BF16).reshape(FR, ROWS, COLS, CH)


def sum_clips(own_h, one_h, two_h, three_h, kg_h, gain_h, in_ref, kg_ref, gain_ref, sem):
    x_at = lax.axis_index("x")
    copies = []
    for d, src in enumerate((own_h, one_h, two_h, three_h)):
        copies.append(
            pltpu.make_async_copy(src, in_ref.at[lax.rem(x_at + NX - d, NX)], sem.at[d])
        )
    for copy in copies:
        copy.start()
    for copy in copies:
        copy.wait()
    total = ((in_ref[0] + in_ref[1]) + in_ref[2]) + in_ref[3]
    for tap in range(TAPS):
        kg_ref[tap] = total[4 * tap : 4 * tap + 4]
    gain_ref[...] = total[4 * TAPS : 4 * TAPS + 1]
    out = (
        pltpu.make_async_copy(kg_ref, kg_h, sem.at[4]),
        pltpu.make_async_copy(gain_ref, gain_h, sem.at[5]),
    )
    for copy in out:
        copy.start()
    for copy in out:
        copy.wait()


HBM = pl.BlockSpec(memory_space=pltpu.HBM)
SMEM = pl.BlockSpec(memory_space=pltpu.SMEM)


def stay_out(array):
    return pltpu.with_memory_space_constraint(array, pltpu.HBM)


def shapes(outs):
    return tuple(jax.ShapeDtypeStruct(s, d) for s, d in outs)


def call(body, outs, args, specs, scratch, flops=0, limit=32):
    return pl.pallas_call(
        body,
        out_shape=shapes(outs),
        in_specs=specs,
        out_specs=tuple(HBM for _ in outs),
        scratch_shapes=list(scratch),
        compiler_params=pltpu.CompilerParams(vmem_limit_bytes=limit * 2**20),
        cost_estimate=pl.CostEstimate(flops=flops, bytes_accessed=2**20, transcendentals=0),
        name=body.__name__,
    )(*args)


def run(body, outs, args, scratch=(), late=None, smem=(), flops=0):
    count, outputs = len(args), len(outs)
    moved = [at for at in range(count) if at not in smem]

    def kernel(*refs):
        ins, targets = list(refs[:count]), refs[count : count + outputs]
        rest = refs[count + outputs :]
        buffers, rest = rest[: len(moved)], rest[len(moved) :]
        results, rest = rest[:outputs], rest[outputs:]
        sem, extra = rest[0], rest[1:]
        copies = [
            pltpu.make_async_copy(ins[at], buffers[n], sem.at[n]) for n, at in enumerate(moved)
        ]
        for copy in copies:
            copy.start()
        for n, at in enumerate(moved):
            ins[at] = buffers[n]
        held = copies.pop(moved.index(late)) if late is not None else None
        for copy in copies:
            copy.wait()
        if held is None:
            body(*ins, *results, *extra)
        else:
            body(*ins, *results, *extra, held)
        copies = [
            pltpu.make_async_copy(results[n], targets[n], sem.at[len(moved) + n])
            for n in range(outputs)
        ]
        for copy in copies:
            copy.start()
        for copy in copies:
            copy.wait()

    kernel.__name__ = body.__name__
    specs = [SMEM if at in smem else HBM for at in range(count)]
    buffers = [pltpu.VMEM(args[at].shape, args[at].dtype) for at in moved]
    buffers += [pltpu.VMEM(s, d) for s, d in outs]
    buffers += [pltpu.SemaphoreType.DMA((len(moved) + outputs,))]
    return call(kernel, outs, args, specs, buffers + list(scratch), flops)


def pack_body(x_h, g_h, hp_h, hn_h, out0, out1, out2, out3, x_ref, g_ref, hp_ref, hn_ref, buf, sem):
    pairs = ((x_h, x_ref), (g_h, g_ref), (hp_h, hp_ref), (hn_h, hn_ref))
    copies = [pltpu.make_async_copy(a, b, sem.at[n]) for n, (a, b) in enumerate(pairs)]
    for copy in copies:
        copy.start()
    for copy in copies:
        copy.wait()
    pack_slices(x_ref, g_ref, hp_ref, hn_ref, buf)
    y_at = lax.axis_index("y")
    copies = [
        pltpu.make_async_copy(buf.at[lax.rem(y_at + d, NY)], out, sem.at[4 + d])
        for d, out in enumerate((out0, out1, out2, out3))
    ]
    for copy in copies:
        copy.start()
    for copy in copies:
        copy.wait()


def local(video_latent, frame_counts, conv_kernel, norm_gain, output_grad):
    x = stay_out(video_latent.reshape(FR, ROWS, COLS, CH))
    g = stay_out(output_grad.reshape(FR, ROWS, COLS, CH))
    gain = stay_out(norm_gain.reshape(1, CH))
    conv_kernel = stay_out(conv_kernel)
    space = ("y", "z", "c")
    cells = (FR, ROWS, COLS, CH)
    wide = (FR, CH)
    halo = (2, FR, COLS, CH)
    swap = [(0, 1), (1, 0)]
    dma = pltpu.SemaphoreType.DMA

    up, dn, stats, live = run(
        edges_and_sums,
        [(halo, BF16), (halo, BF16), ((FR, 128), F32), (wide, F32)],
        (x, g, frame_counts),
        smem=(2,),
    )
    other = lax.ppermute(stats, "c", swap)
    hp = lax.ppermute(dn, space, [(i, i + 1) for i in range(SPACE - 1)])
    hn = lax.ppermute(up, space, [(i + 1, i) for i in range(SPACE - 1)])
    (stats,) = run(pair_sums, [((NY * NZ, FR, 128), F32)], (stats, other))
    stats, hp, hn = lax.optimization_barrier((stats, hp, hn))
    stats = lax.all_to_all(stats, ("y", "z"), 0, 0)
    block = (AROWS + NC * GROWS, BSL)
    packed = call(
        pack_body,
        [(block, BF16)] * NY,
        (x, g, hp, hn),
        [HBM] * 4,
        [pltpu.VMEM(cells, BF16)] * 2
        + [pltpu.VMEM(halo, BF16)] * 2
        + [pltpu.VMEM((NY,) + block, BF16), dma((8,))],
    )
    near = [packed[0]] + [
        lax.ppermute(packed[d], "y", [(i, (i + d) % NY) for i in range(NY)]) for d in range(1, NY)
    ]
    far = [lax.ppermute(a, "c", swap) for a in near]
    conv_flops = 16 * TAPS * FR * CELLS * CH * CH
    padded = pltpu.VMEM((3, FR + 2, 4, COLS, CH), BF16)
    (act_grad,) = run(
        backward_conv,
        [((FR * CELLS, CH), F32)],
        (g, hp, hn, conv_kernel, live),
        scratch=[padded],
        late=3,
        flops=0,
    )
    terms, scaled, mean, inv = run(
        group_terms,
        [((NY * NC, FR, 128), F32), ((FR, CELLS, CH), F32), (wide, F32), (wide, F32)],
        (stats, x, act_grad, gain),
    )
    terms = lax.all_to_all(terms, ("y", "c"), 0, 0)
    part = (NZ, PROWS, BSL)
    keep, give = call(
        kernel_part,
        [(part, BF16)] * 2,
        (*near, *far, mean, inv, gain, live),
        [HBM] * 12,
        [
            pltpu.VMEM((8, AROWS + GROWS, BSL), BF16),
            pltpu.VMEM(wide, F32),
            pltpu.VMEM(wide, F32),
            pltpu.VMEM((1, CH), F32),
            pltpu.VMEM(wide, F32),
            pltpu.VMEM((NC,) + part, BF16),
            pltpu.VMEM((3, FR + 2, NY, 6, COLS, 2 * ASL), BF16),
            pltpu.VMEM((FR, NY, 4, COLS, BSL), F32),
            pltpu.VMEM((NC,) + part, F32),
            dma((20,)),
        ],
        flops=conv_flops,
    )
    got = lax.ppermute(give, "c", swap)
    (merged,) = run(
        merge_parts, [((NZ, 2 * PROWS + 4 * FR, BSL), BF16)], (keep, got, terms)
    )
    merged, late_mean = lax.optimization_barrier((merged, mean))
    merged = lax.all_to_all(merged, "z", 0, 0)
    (block_output,) = run(
        forward_conv,
        [(cells, BF16)],
        (x, hp, hn, late_mean, inv, gain, conv_kernel, live),
        scratch=[padded],
        late=6,
        flops=conv_flops,
    )
    merged, block_output = lax.optimization_barrier((merged, block_output))
    rows, sums = run(sum_rows, [((PROWS, CH), F32), ((FR, 128), F32)], (merged,))
    others = [
        lax.ppermute(rows, "x", [(i, (i + d) % NX) for i in range(NX)]) for d in range(1, NX)
    ]
    (input_grad,) = run(
        finish_input, [(cells, BF16)], (sums, scaled, x, g, mean, inv, live)
    )
    kernel_grad, gain_grad = call(
        sum_clips,
        [((TAPS, 4, CH), F32), ((1, CH), F32)],
        (rows, *others),
        [HBM] * 4,
        [
            pltpu.VMEM((NX, PROWS, CH), F32),
            pltpu.VMEM((TAPS, 4, CH), F32),
            pltpu.VMEM((1, CH), F32),
            dma((6,)),
        ],
    )
    whole = (1,) + cells
    return (
        block_output.reshape(whole),
        input_grad.reshape(whole),
        jnp.swapaxes(kernel_grad, 0, 1),
        gain_grad.reshape(CH),
    )


def solution(mesh):
    fine = Mesh(mesh.devices.reshape(NX, NY, NZ, NC), ("x", "y", "z", "c"))
    space = ("y", "z", "c")
    cells = P("x", None, space, None, None)
    return jax.shard_map(
        local,
        mesh=fine,
        in_specs=(cells, P("x"), P(), P(), cells),
        out_specs=(cells, cells, P(space, None, None), P()),
        check_vma=False,
    )
```

```python
import jax
import jax.numpy as jnp
from jax import lax
from jax.experimental import pallas as pl
from jax.experimental.pallas import tpu as pltpu
from jax.sharding import Mesh
from jax.sharding import PartitionSpec as P

F32 = jnp.float32
BF16 = jnp.bfloat16
NX, NY, NZ, NC = 4, 4, 8, 2
SPACE = NY * NZ * NC
FR, ROWS, COLS, CH = 8, 2, 16, 256
CELLS = ROWS * COLS
GROUPS = 32
GC = CH // GROUPS
ASL = CH // NY
BSL = CH // NC
EPSILON = 1e-05
COUNT = CELLS * SPACE * GC
AROWS = FR // 2 * 3 * COLS
GROWS = FR * ROWS * COLS
TAPS = 27
PROWS = 224
BLOCK = AROWS + NC * GROWS
TERMS = 32
HI = lax.Precision.HIGHEST


def hdot(a, b):
    return jnp.dot(a, b, preferred_element_type=F32, precision=HI)


def gather_matrix():
    lane = lax.broadcasted_iota(jnp.int32, (CH, GROUPS), 0)
    group = lax.broadcasted_iota(jnp.int32, (CH, GROUPS), 1)
    return (lane // GC == group).astype(F32)


def spread_matrix():
    group = lax.broadcasted_iota(jnp.int32, (GROUPS, CH), 0)
    lane = lax.broadcasted_iota(jnp.int32, (GROUPS, CH), 1)
    return (lane // GC == group).astype(F32)


def shifted(cells, k):
    if k == 1:
        return cells
    zero = jnp.zeros(cells.shape[:-2] + (1, cells.shape[-1]), cells.dtype)
    if k == 0:
        return jnp.concatenate([zero, cells[..., :-1, :]], axis=-2)
    return jnp.concatenate([cells[..., 1:, :], zero], axis=-2)


def edges_and_sums(x_ref, g_ref, n_ref, up_ref, dn_ref, st_ref, live_ref):
    up_ref[0] = x_ref[:, 0]
    up_ref[1] = g_ref[:, 0]
    dn_ref[0] = x_ref[:, 1]
    dn_ref[1] = g_ref[:, 1]
    live_ref[...] = (lax.broadcasted_iota(jnp.int32, (FR, CH), 0) < n_ref[0]).astype(F32)
    xf = x_ref[...].astype(F32).reshape(FR, CELLS, CH)
    gather = gather_matrix()
    mean = hdot(jnp.sum(xf, axis=1), gather) / (CELLS * GC)
    centered = xf - hdot(mean, spread_matrix())[:, None, :]
    squares = hdot(jnp.sum(centered * centered, axis=1), gather)
    row = jnp.concatenate([mean, squares, jnp.zeros((FR, 2 * GROUPS), F32)], axis=1)
    st_ref[...] = jnp.broadcast_to(row[None], (NZ * NC, FR, 128))


def combined(parts, squares, each):
    count = parts.shape[0]
    mean = jnp.sum(parts, axis=0) / count
    apart = parts - mean[None]
    return mean, jnp.sum(squares + each * (apart * apart), axis=0)


def as_terms(values):
    high = values.astype(BF16).astype(F32)
    middle = (values - high).astype(BF16).astype(F32)
    low = values - high - middle
    return jnp.concatenate([high, middle, low, jnp.zeros((FR, 128), F32)], axis=0).astype(BF16)


def from_terms(terms):
    terms = terms.astype(F32)
    return (terms[2 * FR : 3 * FR] + terms[FR : 2 * FR]) + terms[:FR]


def pack_slices(x_ref, g_ref, hp_ref, hn_ref, st_ref, out_ref):
    mean, squares = combined(
        st_ref[:, :, :GROUPS], st_ref[:, :, GROUPS : 2 * GROUPS], CELLS * GC
    )
    sums = as_terms(
        jnp.concatenate([mean, squares, jnp.zeros((FR, 2 * GROUPS), F32)], axis=1)
    )
    upper = lax.axis_index("c") == 0
    own = [x_ref[:, 0], x_ref[:, 1]]
    before, after = hp_ref[0], hn_ref[0]
    rows = [
        jnp.where(upper, before, own[0]),
        jnp.where(upper, own[0], own[1]),
        jnp.where(upper, own[1], after),
    ]
    three = jnp.stack(rows, axis=1).reshape(FR // 2, 2, 3, COLS, CH)
    for y in range(NY):
        part = three[..., y * ASL : (y + 1) * ASL]
        pair = jnp.concatenate([part[:, 0], part[:, 1]], axis=-1)
        out_ref[y, :AROWS] = pair.reshape(AROWS, 2 * ASL)
        for c in range(NC):
            at = AROWS + c * GROWS
            out_ref[y, at : at + GROWS] = g_ref[..., c * BSL : (c + 1) * BSL].reshape(GROWS, BSL)
        out_ref[y, BLOCK:] = sums


def backward_conv(g_ref, hp_ref, hn_ref, k_ref, live_ref, out_ref, pad_ref, held):
    live = live_ref[...][:, None, :]
    rows = [hp_ref[1], g_ref[:, 0], g_ref[:, 1], hn_ref[1]]
    for r in range(4):
        cells = rows[r].astype(F32) * live
        for k in range(3):
            pad_ref[k, :FR, r] = shifted(cells, k).astype(BF16)
    pad_ref[:, FR:] = jnp.zeros((3, 2, 4, COLS, CH), BF16)
    held.wait()
    total = jnp.zeros((FR * CELLS, CH), F32)
    for i in range(3):
        for j in range(3):
            for k in range(3):
                window = pad_ref[2 - k, 2 - i : 2 - i + FR, 2 - j : 4 - j]
                total = total + lax.dot_general(
                    window.reshape(FR * CELLS, CH),
                    k_ref[(i * 3 + j) * 3 + k],
                    (((1,), (1,)), ((), ())),
                    preferred_element_type=F32,
                )
    out_ref[...] = total


def group_terms(a_ref, b_ref, c_ref, d_ref, x_ref, ag_ref, gain_ref, out_ref, sc_ref, mean_ref, inv_ref):
    parts = jnp.stack([from_terms(ref[...]) for ref in (a_ref, b_ref, c_ref, d_ref)])
    mean, whole = combined(
        parts[:, :, :GROUPS], parts[:, :, GROUPS : 2 * GROUPS], NZ * NC * CELLS * GC
    )
    spread = spread_matrix()
    mean_all = hdot(mean, spread)
    inv_all = hdot(lax.rsqrt(whole / COUNT + EPSILON), spread)
    mean_ref[...] = mean_all
    inv_ref[...] = inv_all
    gain = gain_ref[...][None]
    xf = x_ref[...].astype(F32).reshape(FR, CELLS, CH)
    normalized = (xf - mean_all[:, None, :]) * inv_all[:, None, :]
    gated = normalized * gain
    sig = jax.nn.sigmoid(gated)
    pre = ag_ref[...].reshape(FR, CELLS, CH) * sig * (1.0 + gated * (1.0 - sig))
    scaled = pre * gain
    sc_ref[...] = scaled
    gather = gather_matrix()
    first = hdot(jnp.sum(scaled, axis=1), gather)
    by_channel = jnp.sum(pre * normalized, axis=1)
    second = hdot(by_channel * gain_ref[...], gather)
    gain_part = jnp.sum(by_channel, axis=0, keepdims=True)
    row = lax.broadcasted_iota(jnp.int32, (FR, CH), 0)
    lane = lax.broadcasted_iota(jnp.int32, (FR, CH), 1)
    folded = jnp.where(lane // GROUPS == row, jnp.broadcast_to(gain_part, (FR, CH)), 0.0)
    fold_lane = lax.broadcasted_iota(jnp.int32, (CH, GROUPS), 0)
    fold_at = lax.broadcasted_iota(jnp.int32, (CH, GROUPS), 1)
    folded = hdot(folded, (fold_lane % GROUPS == fold_at).astype(F32))
    everything = jnp.concatenate([first, second, folded, jnp.zeros((FR, GROUPS), F32)], axis=1)
    out_ref[...] = jnp.broadcast_to(everything[None], (NY * NC, FR, 128))


def kernel_part(*refs):
    blocks, (mean_h, inv_h, gain_h, live_h, out_h) = refs[:8], refs[8:13]
    in_ref, mean_ref, inv_ref, gain_ref, live_ref, out_ref, pad_ref, grad_ref, sum_ref, sem = refs[13:]
    y_at, z_at, c_at = lax.axis_index("y"), lax.axis_index("z"), lax.axis_index("c")
    grads_at = pl.multiple_of(AROWS + c_at * GROWS, 64)
    copies = []
    for n in range(8):
        copies.append(
            pltpu.make_async_copy(blocks[n].at[:AROWS], in_ref.at[n, :AROWS], sem.at[2 * n])
        )
        copies.append(
            pltpu.make_async_copy(
                blocks[n].at[pl.ds(grads_at, GROWS)], in_ref.at[n, AROWS:], sem.at[2 * n + 1]
            )
        )
    for n, (src, dst) in enumerate(
        ((mean_h, mean_ref), (inv_h, inv_ref), (gain_h, gain_ref), (live_h, live_ref))
    ):
        copies.append(pltpu.make_async_copy(src, dst, sem.at[16 + n]))
    for copy in copies:
        copy.start()
    pad_ref[:, 0] = jnp.zeros((3, NY, 6, COLS, 2 * ASL), BF16)
    for copy in copies[16:]:
        copy.wait()
    lane = lax.broadcasted_iota(jnp.int32, (CH, 2 * ASL), 0)
    slot = lax.broadcasted_iota(jnp.int32, (CH, 2 * ASL), 1)
    pick = (lane == y_at * ASL + slot % ASL).astype(F32)
    mean2 = hdot(mean_ref[...], pick)
    inv2 = hdot(inv_ref[...], pick)
    gain2 = hdot(gain_ref[...], pick)
    live = live_ref[:, :BSL][:, None, None, :]
    shape = (3, COLS, 2 * ASL)
    low = lax.broadcasted_iota(jnp.int32, (1, 2 * ASL), 1) < ASL
    lowest = lax.broadcasted_iota(jnp.int32, shape, 2) < ASL
    row = lax.broadcasted_iota(jnp.int32, shape, 0)
    block = 3 * COLS
    for n in range(8):
        copies[2 * n].wait()
        copies[2 * n + 1].wait()
        d = n % 4
        y = lax.rem(y_at + NY - d, NY)
        c = c_at if n < 4 else 1 - c_at
        top = (y == 0) & (z_at == 0) & (c == 0)
        bottom = (y == NY - 1) & (z_at == NZ - 1) & (c == NC - 1)
        edge = jnp.where(top, 0, jnp.where(bottom, 2, 3))
        inside = (row != edge).astype(F32)
        before = jnp.zeros(shape, F32)
        for m in range(FR // 2 + 1):
            if m < FR // 2:
                raw = in_ref[n, m * block : (m + 1) * block].astype(F32)
                center = jnp.where(low, mean2[2 * m : 2 * m + 1], mean2[2 * m + 1 : 2 * m + 2])
                scale = jnp.where(low, inv2[2 * m : 2 * m + 1], inv2[2 * m + 1 : 2 * m + 2])
                gated = (raw - center) * scale * gain2
                act = (gated * jax.nn.sigmoid(gated)).reshape(shape) * inside
            else:
                act = jnp.zeros(shape, F32)
            turned = pltpu.roll(act, ASL, 2)
            odd = jnp.where(lowest, before, turned)
            before = turned
            for k in range(3):
                if m < FR // 2:
                    pad_ref[k, 2 * m + 2, d, pl.ds(3 * c, 3)] = shifted(act, k).astype(BF16)
                pad_ref[k, 2 * m + 1, d, pl.ds(3 * c, 3)] = shifted(odd, k).astype(BF16)
        cells = in_ref[n, AROWS:].astype(F32).reshape(FR, ROWS, COLS, BSL) * live
        grad_ref[:, d, pl.ds(2 * c, 2)] = cells
    turned_grad = grad_ref[...].reshape(FR * NY * 4 * COLS, BSL).T.astype(BF16)
    sum_ref[:, 8 * TAPS :] = jnp.zeros((NZ, PROWS - 8 * TAPS, BSL), F32)
    for j in range(3):
        for k in range(3):
            early = pad_ref[k, 0:FR, :, j : j + 4].reshape(FR * NY * 4 * COLS, 2 * ASL)
            late = pad_ref[k, 2 : 2 + FR, :, j : j + 4].reshape(FR * NY * 4 * COLS, 2 * ASL)
            product = jnp.dot(
                turned_grad,
                jnp.concatenate([early, late], axis=1),
                preferred_element_type=F32,
            ).T
            for i in range(3):
                tap = (i * 3 + j) * 3 + k
                piece = product[i * ASL : (i + 1) * ASL].reshape(NZ, ASL // NZ, BSL)
                sum_ref[:, tap * 8 : tap * 8 + 8] = piece
    out_ref[...] = sum_ref[...].astype(BF16)
    copy = pltpu.make_async_copy(out_ref, out_h.at[:, :PROWS], sem.at[0])
    copy.start()
    copy.wait()


def add_sums(part_h, b_h, out_h, b_ref, out_ref, sem):
    copy = pltpu.make_async_copy(b_h, b_ref, sem.at[0])
    copy.start()
    copy.wait()
    terms = as_terms(jnp.sum(b_ref[...], axis=0))
    out_ref[...] = jnp.broadcast_to(terms[None], (NZ, TERMS, 128))
    copy = pltpu.make_async_copy(out_ref, out_h.at[:, PROWS:], sem.at[1])
    copy.start()
    copy.wait()


def sum_rows(in_ref, out_ref, sums_ref):
    total = jnp.sum(in_ref[...].astype(F32), axis=0)
    sums = from_terms(total[PROWS:])
    sums_ref[...] = sums
    fold_at = lax.broadcasted_iota(jnp.int32, (GROUPS, CH), 0)
    fold_lane = lax.broadcasted_iota(jnp.int32, (GROUPS, CH), 1)
    wide = hdot(sums[:, 2 * GROUPS : 3 * GROUPS], (fold_lane % GROUPS == fold_at).astype(F32))
    row = lax.broadcasted_iota(jnp.int32, (FR, CH), 0)
    lane = lax.broadcasted_iota(jnp.int32, (FR, CH), 1)
    gain = jnp.sum(jnp.where(lane // GROUPS == row, wide, 0.0), axis=0, keepdims=True)
    out_ref[...] = total[:PROWS]
    out_ref[8 * TAPS : 8 * TAPS + 1] = gain[:, :BSL]
    out_ref[8 * TAPS + 1 : 8 * TAPS + 2] = gain[:, BSL:]


def forward_conv(x_ref, hp_ref, hn_ref, mean_ref, inv_ref, gain_ref, k_ref, live_ref, out_ref, pad_ref, held):
    s_at = (lax.axis_index("y") * NZ + lax.axis_index("z")) * NC + lax.axis_index("c")
    rows = [hp_ref[0], x_ref[:, 0], x_ref[:, 1], hn_ref[0]]
    mean = mean_ref[...][:, None, :]
    inv = inv_ref[...][:, None, :]
    gain = gain_ref[...][None]
    for r in range(4):
        gated = (rows[r].astype(F32) - mean) * inv * gain
        act = gated * jax.nn.sigmoid(gated)
        if r == 0:
            act = jnp.where(s_at == 0, 0.0, act)
        if r == 3:
            act = jnp.where(s_at == SPACE - 1, 0.0, act)
        for k in range(3):
            pad_ref[k, 2:, r] = shifted(act, k).astype(BF16)
    pad_ref[:, :2] = jnp.zeros((3, 2, 4, COLS, CH), BF16)
    held.wait()
    total = jnp.zeros((FR * CELLS, CH), F32)
    for i in range(3):
        for j in range(3):
            for k in range(3):
                window = pad_ref[k, i : i + FR, j : j + 2]
                total = total + jnp.dot(
                    window.reshape(FR * CELLS, CH),
                    k_ref[(i * 3 + j) * 3 + k],
                    preferred_element_type=F32,
                )
    cells = total.reshape(FR, CELLS, CH) + x_ref[...].astype(F32).reshape(FR, CELLS, CH)
    cells = cells * live_ref[...][:, None, :]
    out_ref[...] = cells.astype(BF16).reshape(FR, ROWS, COLS, CH)


def finish_input(sums_ref, sc_ref, x_ref, g_ref, mean_ref, inv_ref, live_ref, out_ref):
    sums = sums_ref[...]
    spread = spread_matrix()
    first = hdot(sums[:, :GROUPS] / COUNT, spread)[:, None, :]
    second = hdot(sums[:, GROUPS : 2 * GROUPS] / COUNT, spread)[:, None, :]
    inv = inv_ref[...][:, None, :]
    xf = x_ref[...].astype(F32).reshape(FR, CELLS, CH)
    normalized = (xf - mean_ref[...][:, None, :]) * inv
    norm_grad = inv * (sc_ref[...] - first - normalized * second)
    grad = g_ref[...].astype(F32).reshape(FR, CELLS, CH) * live_ref[...][:, None, :]
    out_ref[...] = (grad + norm_grad).astype(BF16).reshape(FR, ROWS, COLS, CH)


def sum_clips(*refs):
    kg_h, gain_h, in_ref, kg_ref, gain_ref, sem = refs[8:]
    x_at, c_at = lax.axis_index("x"), lax.axis_index("c")
    copies = []
    for n, src in enumerate(refs[:8]):
        c = c_at if n < 4 else 1 - c_at
        slot = in_ref.at[c, lax.rem(x_at + NX - n % 4, NX)]
        copies.append(pltpu.make_async_copy(src, slot, sem.at[n]))
    for copy in copies:
        copy.start()
    for copy in copies:
        copy.wait()
    for c in range(NC):
        total = ((in_ref[c, 0] + in_ref[c, 1]) + in_ref[c, 2]) + in_ref[c, 3]
        total = total.reshape(TAPS + 1, 8, BSL)
        kg_ref[:, :, c * BSL : (c + 1) * BSL] = jnp.where(c_at == 0, total[:TAPS, :4], total[:TAPS, 4:])
        if c == 0:
            gain_ref[:, :BSL] = total[TAPS, 0:1]
            gain_ref[:, BSL:] = total[TAPS, 1:2]
    out = (
        pltpu.make_async_copy(kg_ref, kg_h, sem.at[8]),
        pltpu.make_async_copy(gain_ref, gain_h, sem.at[9]),
    )
    for copy in out:
        copy.start()
    for copy in out:
        copy.wait()


HBM = pl.BlockSpec(memory_space=pltpu.HBM)
SMEM = pl.BlockSpec(memory_space=pltpu.SMEM)


def stay_out(array):
    return pltpu.with_memory_space_constraint(array, pltpu.HBM)


def shapes(outs):
    return tuple(jax.ShapeDtypeStruct(s, d) for s, d in outs)


def call(body, outs, args, specs, scratch, flops=0, limit=32, aliases={}):
    return pl.pallas_call(
        body,
        out_shape=shapes(outs),
        in_specs=specs,
        out_specs=tuple(HBM for _ in outs),
        scratch_shapes=list(scratch),
        input_output_aliases=aliases,
        compiler_params=pltpu.CompilerParams(vmem_limit_bytes=limit * 2**20),
        cost_estimate=pl.CostEstimate(flops=flops, bytes_accessed=2**20, transcendentals=0),
        name=body.__name__,
    )(*args)


def run(body, outs, args, scratch=(), late=None, smem=(), flops=0, rows={}):
    count, outputs = len(args), len(outs)
    moved = [at for at in range(count) if at not in smem]

    def kernel(*refs):
        ins, targets = list(refs[:count]), refs[count : count + outputs]
        rest = refs[count + outputs :]
        buffers, rest = rest[: len(moved)], rest[len(moved) :]
        results, rest = rest[:outputs], rest[outputs:]
        sem, extra = rest[0], rest[1:]
        copies = [
            pltpu.make_async_copy(
                ins[at].at[rows[at][0] : rows[at][1]] if at in rows else ins[at], buffers[n], sem.at[n]
            )
            for n, at in enumerate(moved)
        ]
        for copy in copies:
            copy.start()
        for n, at in enumerate(moved):
            ins[at] = buffers[n]
        held = copies.pop(moved.index(late)) if late is not None else None
        for copy in copies:
            copy.wait()
        if held is None:
            body(*ins, *results, *extra)
        else:
            body(*ins, *results, *extra, held)
        copies = [
            pltpu.make_async_copy(results[n], targets[n], sem.at[len(moved) + n])
            for n in range(outputs)
        ]
        for copy in copies:
            copy.start()
        for copy in copies:
            copy.wait()

    kernel.__name__ = body.__name__
    specs = [SMEM if at in smem else HBM for at in range(count)]
    buffers = []
    for at in moved:
        shape = args[at].shape
        if at in rows:
            shape = (rows[at][1] - rows[at][0],) + shape[1:]
        buffers.append(pltpu.VMEM(shape, args[at].dtype))
    buffers += [pltpu.VMEM(s, d) for s, d in outs]
    buffers += [pltpu.SemaphoreType.DMA((len(moved) + outputs,))]
    return call(kernel, outs, args, specs, buffers + list(scratch), flops)


def pack_body(*refs):
    sources, outs = refs[:5], refs[5:9]
    x_ref, g_ref, hp_ref, hn_ref, st_ref, buf, sem = refs[9:]
    pairs = tuple(zip(sources, (x_ref, g_ref, hp_ref, hn_ref, st_ref)))
    copies = [pltpu.make_async_copy(a, b, sem.at[n]) for n, (a, b) in enumerate(pairs)]
    for copy in copies:
        copy.start()
    for copy in copies:
        copy.wait()
    pack_slices(x_ref, g_ref, hp_ref, hn_ref, st_ref, buf)
    y_at = lax.axis_index("y")
    copies = [
        pltpu.make_async_copy(buf.at[lax.rem(y_at + d, NY)], out, sem.at[5 + d])
        for d, out in enumerate(outs)
    ]
    for copy in copies:
        copy.start()
    for copy in copies:
        copy.wait()


def local(video_latent, frame_counts, conv_kernel, norm_gain, output_grad):
    x = stay_out(video_latent.reshape(FR, ROWS, COLS, CH))
    g = stay_out(output_grad.reshape(FR, ROWS, COLS, CH))
    gain = stay_out(norm_gain.reshape(1, CH))
    conv_kernel = stay_out(conv_kernel)
    space = ("y", "z", "c")
    cells = (FR, ROWS, COLS, CH)
    wide = (FR, CH)
    halo = (2, FR, COLS, CH)
    swap = [(0, 1), (1, 0)]
    dma = pltpu.SemaphoreType.DMA

    up, dn, stats, live = run(
        edges_and_sums,
        [(halo, BF16), (halo, BF16), ((NZ * NC, FR, 128), F32), (wide, F32)],
        (x, g, frame_counts),
        smem=(2,),
    )
    hp = lax.ppermute(dn, space, [(i, i + 1) for i in range(SPACE - 1)])
    hn = lax.ppermute(up, space, [(i + 1, i) for i in range(SPACE - 1)])
    stats = lax.all_to_all(stats, ("z", "c"), 0, 0)
    conv_flops = 16 * TAPS * FR * CELLS * CH * CH
    padded = pltpu.VMEM((3, FR + 2, 4, COLS, CH), BF16)
    (act_grad,) = run(
        backward_conv,
        [((FR * CELLS, CH), F32)],
        (g, hp, hn, conv_kernel, live),
        scratch=[padded],
        late=3,
        flops=0,
    )
    act_grad, hp, hn = lax.optimization_barrier((act_grad, hp, hn))
    block = (BLOCK + TERMS, BSL)
    packed = call(
        pack_body,
        [(block, BF16)] * NY,
        (x, g, hp, hn, stats),
        [HBM] * 5,
        [pltpu.VMEM(cells, BF16)] * 2
        + [pltpu.VMEM(halo, BF16)] * 2
        + [pltpu.VMEM((NZ * NC, FR, 128), F32), pltpu.VMEM((NY,) + block, BF16), dma((9,))],
    )
    near = [packed[0]] + [
        lax.ppermute(packed[d], "y", [(i, (i + d) % NY) for i in range(NY)]) for d in range(1, NY)
    ]
    far = [lax.ppermute(a, "c", swap) for a in near]
    terms, scaled, mean, inv = run(
        group_terms,
        [((NY * NC, FR, 128), F32), ((FR, CELLS, CH), F32), (wide, F32), (wide, F32)],
        (*near, x, act_grad, gain),
        rows={at: (BLOCK, BLOCK + TERMS) for at in range(NY)},
    )
    terms = lax.all_to_all(terms, ("y", "c"), 0, 0)
    part = (NZ, PROWS, BSL)
    whole_part = (NZ, PROWS + TERMS, BSL)
    (partial,) = call(
        kernel_part,
        [(whole_part, BF16)],
        (*near, *far, mean, inv, gain, live),
        [HBM] * 12,
        [
            pltpu.VMEM((8, AROWS + GROWS, BSL), BF16),
            pltpu.VMEM(wide, F32),
            pltpu.VMEM(wide, F32),
            pltpu.VMEM((1, CH), F32),
            pltpu.VMEM(wide, F32),
            pltpu.VMEM(part, BF16),
            pltpu.VMEM((3, FR + 2, NY, 6, COLS, 2 * ASL), BF16),
            pltpu.VMEM((FR, NY, 4, COLS, BSL), F32),
            pltpu.VMEM(part, F32),
            dma((20,)),
        ],
        flops=conv_flops,
    )
    (merged,) = call(
        add_sums,
        [(whole_part, BF16)],
        (partial, terms),
        [HBM] * 2,
        [pltpu.VMEM((NY * NC, FR, 128), F32), pltpu.VMEM((NZ, TERMS, 128), BF16), dma((2,))],
        aliases={0: 0},
    )
    merged, late_mean = lax.optimization_barrier((merged, mean))
    merged = lax.all_to_all(merged, "z", 0, 0)
    (block_output,) = run(
        forward_conv,
        [(cells, BF16)],
        (x, hp, hn, late_mean, inv, gain, conv_kernel, live),
        scratch=[padded],
        late=6,
        flops=conv_flops,
    )
    merged, block_output = lax.optimization_barrier((merged, block_output))
    rows, sums = run(sum_rows, [((PROWS, BSL), F32), ((FR, 128), F32)], (merged,))
    others = [rows] + [
        lax.ppermute(rows, "x", [(i, (i + d) % NX) for i in range(NX)]) for d in range(1, NX)
    ]
    (input_grad,) = run(
        finish_input, [(cells, BF16)], (sums, scaled, x, g, mean, inv, live)
    )
    *others, input_grad = lax.optimization_barrier((*others, input_grad))
    swapped = [lax.ppermute(a, "c", swap) for a in others]
    kernel_grad, gain_grad = call(
        sum_clips,
        [((TAPS, 4, CH), F32), ((1, CH), F32)],
        (*others, *swapped),
        [HBM] * 8,
        [
            pltpu.VMEM((NC, NX, PROWS, BSL), F32),
            pltpu.VMEM((TAPS, 4, CH), F32),
            pltpu.VMEM((1, CH), F32),
            dma((10,)),
        ],
    )
    whole = (1,) + cells
    return (
        block_output.reshape(whole),
        input_grad.reshape(whole),
        jnp.swapaxes(kernel_grad, 0, 1),
        gain_grad.reshape(CH),
    )


def solution(mesh):
    fine = Mesh(mesh.devices.reshape(NX, NY, NZ, NC), ("x", "y", "z", "c"))
    space = ("y", "z", "c")
    cells = P("x", None, space, None, None)
    return jax.shard_map(
        local,
        mesh=fine,
        in_specs=(cells, P("x"), P(), P(), cells),
        out_specs=(cells, cells, P(space, None, None), P()),
        check_vma=False,
    )
```

```python
import jax
import jax.numpy as jnp
from jax import lax
from jax.experimental import pallas as pl
from jax.experimental.pallas import tpu as pltpu
from jax.sharding import Mesh
from jax.sharding import PartitionSpec as P

F32 = jnp.float32
BF16 = jnp.bfloat16
NX, NY, NZ, NC = 4, 4, 8, 2
SPACE = NY * NZ * NC
FR, ROWS, COLS, CH = 8, 2, 16, 256
CELLS = ROWS * COLS
GROUPS = 32
GC = CH // GROUPS
ASL = CH // NY
BSL = CH // NC
EPSILON = 1e-05
COUNT = CELLS * SPACE * GC
AROWS = FR // 2 * 3 * COLS
GROWS = FR * ROWS * COLS
TAPS = 27
PROWS = 112
Q = 4
APART = ASL // NC
BLOCK = AROWS + NC * GROWS
TERMS = 16
HI = lax.Precision.HIGHEST


def hdot(a, b):
    return jnp.dot(a, b, preferred_element_type=F32, precision=HI)


def gather_matrix():
    lane = lax.broadcasted_iota(jnp.int32, (CH, GROUPS), 0)
    group = lax.broadcasted_iota(jnp.int32, (CH, GROUPS), 1)
    return (lane // GC == group).astype(F32)


def spread_matrix():
    group = lax.broadcasted_iota(jnp.int32, (GROUPS, CH), 0)
    lane = lax.broadcasted_iota(jnp.int32, (GROUPS, CH), 1)
    return (lane // GC == group).astype(F32)


def shifted(cells, k):
    if k == 1:
        return cells
    zero = jnp.zeros(cells.shape[:-2] + (1, cells.shape[-1]), cells.dtype)
    if k == 0:
        return jnp.concatenate([zero, cells[..., :-1, :]], axis=-2)
    return jnp.concatenate([cells[..., 1:, :], zero], axis=-2)


def edges_and_sums(x_ref, g_ref, n_ref, up_ref, dn_ref, st_ref, live_ref):
    up_ref[0] = x_ref[:, 0]
    up_ref[1] = g_ref[:, 0]
    dn_ref[0] = x_ref[:, 1]
    dn_ref[1] = g_ref[:, 1]
    live_ref[...] = (lax.broadcasted_iota(jnp.int32, (FR, CH), 0) < n_ref[0]).astype(F32)
    xf = x_ref[...].astype(F32).reshape(FR, CELLS, CH)
    gather = gather_matrix()
    mean = hdot(jnp.sum(xf, axis=1), gather) / (CELLS * GC)
    centered = xf - hdot(mean, spread_matrix())[:, None, :]
    squares = hdot(jnp.sum(centered * centered, axis=1), gather)
    st_ref[...] = jnp.concatenate([mean, squares, jnp.zeros((FR, 2 * GROUPS), F32)], axis=1)


def combined(parts, squares, each):
    count = parts.shape[0]
    mean = jnp.sum(parts, axis=0) / count
    apart = parts - mean[None]
    return mean, jnp.sum(squares + each * (apart * apart), axis=0)


def pair_sums(own_ref, other_ref, out_ref):
    both = jnp.stack([own_ref[...], other_ref[...]])
    mean, squares = combined(both[:, :, :GROUPS], both[:, :, GROUPS : 2 * GROUPS], CELLS * GC)
    row = jnp.concatenate([mean, squares, jnp.zeros((FR, 2 * GROUPS), F32)], axis=1)
    row = jnp.concatenate([row] * 2, axis=0)
    out_ref[...] = jnp.broadcast_to(row[None], (NY * NZ, 16, 128))


def as_terms(values):
    high = values.astype(BF16).astype(F32)
    middle = (values - high).astype(BF16).astype(F32)
    low = values - high - middle
    upper = jnp.concatenate([high, middle], axis=1)
    lower = jnp.concatenate([low, jnp.zeros((FR, 128), F32)], axis=1)
    return jnp.concatenate([upper, lower], axis=0).astype(BF16)


def from_terms(terms):
    return (terms[FR:, :128] + terms[:FR, 128:]) + terms[:FR, :128]


def pack_slices(x_ref, g_ref, hp_ref, hn_ref, out_ref):
    upper = lax.axis_index("c") == 0
    own = [x_ref[:, 0], x_ref[:, 1]]
    before, after = hp_ref[0], hn_ref[0]
    rows = [
        jnp.where(upper, before, own[0]),
        jnp.where(upper, own[0], own[1]),
        jnp.where(upper, own[1], after),
    ]
    three = jnp.stack(rows, axis=1).reshape(FR // 2, 2, 3, COLS, CH)
    for y in range(NY):
        part = three[..., y * ASL : (y + 1) * ASL]
        pair = jnp.concatenate([part[:, 0], part[:, 1]], axis=-1)
        out_ref[y, :AROWS] = pair.reshape(AROWS, 2 * ASL)
        for c in range(NC):
            at = AROWS + c * GROWS
            out_ref[y, at : at + GROWS] = g_ref[..., c * BSL : (c + 1) * BSL].reshape(GROWS, BSL)


def backward_conv(g_ref, hp_ref, hn_ref, k_ref, live_ref, out_ref, pad_ref, held):
    live = live_ref[...][:, None, :]
    rows = [hp_ref[1], g_ref[:, 0], g_ref[:, 1], hn_ref[1]]
    for r in range(4):
        cells = rows[r].astype(F32) * live
        for k in range(3):
            pad_ref[k, :FR, r] = shifted(cells, k).astype(BF16)
    pad_ref[:, FR:] = jnp.zeros((3, 2, 4, COLS, CH), BF16)
    held.wait()
    total = jnp.zeros((FR * CELLS, CH), F32)
    for i in range(3):
        for j in range(3):
            for k in range(3):
                window = pad_ref[2 - k, 2 - i : 2 - i + FR, 2 - j : 4 - j]
                total = total + lax.dot_general(
                    window.reshape(FR * CELLS, CH),
                    k_ref[(i * 3 + j) * 3 + k],
                    (((1,), (1,)), ((), ())),
                    preferred_element_type=F32,
                )
    out_ref[...] = total


def group_terms(st_ref, x_ref, ag_ref, gain_ref, out_ref, sc_ref, mean_ref, inv_ref):
    mean, whole = combined(
        st_ref[:, :FR, :GROUPS], st_ref[:, :FR, GROUPS : 2 * GROUPS], NC * CELLS * GC
    )
    spread = spread_matrix()
    mean_all = hdot(mean, spread)
    inv_all = hdot(lax.rsqrt(whole / COUNT + EPSILON), spread)
    mean_ref[...] = mean_all
    inv_ref[...] = inv_all
    gain = gain_ref[...][None]
    xf = x_ref[...].astype(F32).reshape(FR, CELLS, CH)
    normalized = (xf - mean_all[:, None, :]) * inv_all[:, None, :]
    gated = normalized * gain
    sig = jax.nn.sigmoid(gated)
    pre = ag_ref[...].reshape(FR, CELLS, CH) * sig * (1.0 + gated * (1.0 - sig))
    scaled = pre * gain
    sc_ref[...] = scaled
    gather = gather_matrix()
    first = hdot(jnp.sum(scaled, axis=1), gather)
    by_channel = jnp.sum(pre * normalized, axis=1)
    second = hdot(by_channel * gain_ref[...], gather)
    gain_part = jnp.sum(by_channel, axis=0, keepdims=True)
    row = lax.broadcasted_iota(jnp.int32, (FR, CH), 0)
    lane = lax.broadcasted_iota(jnp.int32, (FR, CH), 1)
    folded = jnp.where(lane // GROUPS == row, jnp.broadcast_to(gain_part, (FR, CH)), 0.0)
    fold_lane = lax.broadcasted_iota(jnp.int32, (CH, GROUPS), 0)
    fold_at = lax.broadcasted_iota(jnp.int32, (CH, GROUPS), 1)
    folded = hdot(folded, (fold_lane % GROUPS == fold_at).astype(F32))
    everything = jnp.concatenate([first, second, folded, jnp.zeros((FR, GROUPS), F32)], axis=1)
    out_ref[...] = jnp.broadcast_to(everything[None], (NY * NC, FR, 128))


def kernel_part(*refs):
    blocks, (mean_h, inv_h, gain_h, live_h, out_h) = refs[:8], refs[8:13]
    in_ref, mean_ref, inv_ref, gain_ref, live_ref, out_ref, pad_ref, grad_ref, sum_ref, sem = refs[13:]
    y_at, z_at, c_at = lax.axis_index("y"), lax.axis_index("z"), lax.axis_index("c")
    pairs = [(blocks[n], in_ref.at[n]) for n in range(8)]
    pairs += [(mean_h, mean_ref), (inv_h, inv_ref), (gain_h, gain_ref), (live_h, live_ref)]
    copies = [pltpu.make_async_copy(a, b, sem.at[n]) for n, (a, b) in enumerate(pairs)]
    for copy in copies:
        copy.start()
    for copy in copies[8:]:
        copy.wait()
    width = Q * APART
    lane = lax.broadcasted_iota(jnp.int32, (CH, width), 0)
    slot = lax.broadcasted_iota(jnp.int32, (CH, width), 1)
    channel = GC * ((slot % APART) // 4) + 4 * c_at + slot % 4
    pick = (lane == y_at * ASL + channel).astype(F32)
    mean2 = hdot(mean_ref[...], pick)
    inv2 = hdot(inv_ref[...], pick)
    gain2 = hdot(gain_ref[...], pick)
    live = live_ref[:, :BSL][:, None, None, :]
    quarter = lax.broadcasted_iota(jnp.int32, (1, width), 1) // APART
    centers, scales = [], []
    for u in range(2):
        center, scale = mean2[4 * u : 4 * u + 1], inv2[4 * u : 4 * u + 1]
        for q in range(1, Q):
            center = jnp.where(quarter == q, mean2[4 * u + q : 4 * u + q + 1], center)
            scale = jnp.where(quarter == q, inv2[4 * u + q : 4 * u + q + 1], scale)
        centers.append(center)
        scales.append(scale * gain2)
    lane = lax.broadcasted_iota(jnp.int32, (2 * ASL, width), 0)
    slot = lax.broadcasted_iota(jnp.int32, (2 * ASL, width), 1)
    channel = GC * ((slot % APART) // 4) + 4 * c_at + slot % 4
    chosen = [
        (lane == (slot // APART - 2 * half) * ASL + channel).astype(BF16) for half in range(2)
    ]
    shape = (3, COLS, width)
    place = lax.broadcasted_iota(jnp.int32, shape, 2) // APART
    row = lax.broadcasted_iota(jnp.int32, shape, 0)
    block = 3 * COLS
    for n in range(8):
        copies[n].wait()
        d = n % 4
        y = lax.rem(y_at + NY - d, NY)
        c = c_at if n < 4 else 1 - c_at
        top = (y == 0) & (z_at == 0) & (c == 0)
        bottom = (y == NY - 1) & (z_at == NZ - 1) & (c == NC - 1)
        edge = jnp.where(top, 0, jnp.where(bottom, 2, 3))
        inside = (row != edge).astype(F32)
        acts = []
        for u in range(2):
            at = 2 * u * block
            raw = jnp.dot(
                in_ref[n, at : at + block], chosen[0], preferred_element_type=F32
            ) + jnp.dot(
                in_ref[n, at + block : at + 2 * block], chosen[1], preferred_element_type=F32
            )
            gated = (raw - centers[u]) * scales[u]
            acts.append((gated * jax.nn.sigmoid(gated)).reshape(shape) * inside)
        a, b = acts
        a1, a2, b1 = pltpu.roll(a, 32, 2), pltpu.roll(a, 64, 2), pltpu.roll(b, 32, 2)
        b2 = pltpu.roll(b, 64, 2)
        frames = [
            jnp.where(place < 2, 0.0, a2),
            jnp.where(place < 1, 0.0, a1),
            a,
            pltpu.roll(a, 96, 2),
            jnp.where(place < 2, a2, b2),
            jnp.where(place < 1, a1, b1),
            b,
            pltpu.roll(b, 96, 2),
        ]
        for f in range(FR):
            for k in range(3):
                pad_ref[k, f, d, pl.ds(3 * c, 3)] = shifted(frames[f], k).astype(BF16)
        for h in range(NC):
            at = AROWS + h * GROWS
            cells = in_ref[n, at : at + GROWS].astype(F32).reshape(FR, ROWS, COLS, BSL) * live
            grad_ref[:, d, pl.ds(2 * c, 2), :, h * BSL : (h + 1) * BSL] = cells
    cells = FR * NY * 4 * COLS
    turned_grad = grad_ref[...].reshape(cells, CH).T.astype(BF16)
    sum_ref[:, 4 * TAPS :] = jnp.zeros((NZ, PROWS - 4 * TAPS, CH), F32)
    combos = [(j, k) for j in range(3) for k in range(3)]
    for first in range(0, 9, 2):
        group = combos[first : first + 2]
        windows = [pad_ref[k, :, :, j : j + 4].reshape(cells, width) for j, k in group]
        window = windows[0] if len(windows) == 1 else jnp.concatenate(windows, axis=1)
        product = jnp.dot(turned_grad, window, preferred_element_type=F32).T
        for n, (j, k) in enumerate(group):
            for i in range(3):
                tap = (i * 3 + j) * 3 + k
                at = n * width + i * APART
                piece = product[at : at + APART].reshape(NZ, 4, CH)
                sum_ref[:, tap * 4 : tap * 4 + 4] = piece
    out_ref[...] = sum_ref[...].astype(BF16)
    copy = pltpu.make_async_copy(out_ref, out_h.at[:, :PROWS], sem.at[0])
    copy.start()
    copy.wait()


def add_sums(part_h, b_h, out_h, b_ref, out_ref, sem):
    copy = pltpu.make_async_copy(b_h, b_ref, sem.at[0])
    copy.start()
    copy.wait()
    terms = as_terms(jnp.sum(b_ref[...], axis=0))
    out_ref[...] = jnp.broadcast_to(terms[None], (NZ, TERMS, CH))
    copy = pltpu.make_async_copy(out_ref, out_h.at[:, PROWS:], sem.at[1])
    copy.start()
    copy.wait()


def sum_rows(in_ref, out_ref, sums_ref):
    total = jnp.sum(in_ref[...].astype(F32), axis=0)
    sums = from_terms(total[PROWS:])
    sums_ref[...] = sums
    fold_at = lax.broadcasted_iota(jnp.int32, (GROUPS, CH), 0)
    fold_lane = lax.broadcasted_iota(jnp.int32, (GROUPS, CH), 1)
    wide = hdot(sums[:, 2 * GROUPS : 3 * GROUPS], (fold_lane % GROUPS == fold_at).astype(F32))
    row = lax.broadcasted_iota(jnp.int32, (FR, CH), 0)
    lane = lax.broadcasted_iota(jnp.int32, (FR, CH), 1)
    gain = jnp.sum(jnp.where(lane // GROUPS == row, wide, 0.0), axis=0, keepdims=True)
    out_ref[...] = total[:PROWS]
    out_ref[4 * TAPS : 4 * TAPS + 1] = gain


def forward_conv(x_ref, hp_ref, hn_ref, mean_ref, inv_ref, gain_ref, k_ref, live_ref, out_ref, pad_ref, held):
    s_at = (lax.axis_index("y") * NZ + lax.axis_index("z")) * NC + lax.axis_index("c")
    rows = [hp_ref[0], x_ref[:, 0], x_ref[:, 1], hn_ref[0]]
    mean = mean_ref[...][:, None, :]
    inv = inv_ref[...][:, None, :]
    gain = gain_ref[...][None]
    for r in range(4):
        gated = (rows[r].astype(F32) - mean) * inv * gain
        act = gated * jax.nn.sigmoid(gated)
        if r == 0:
            act = jnp.where(s_at == 0, 0.0, act)
        if r == 3:
            act = jnp.where(s_at == SPACE - 1, 0.0, act)
        for k in range(3):
            pad_ref[k, 2:, r] = shifted(act, k).astype(BF16)
    pad_ref[:, :2] = jnp.zeros((3, 2, 4, COLS, CH), BF16)
    held.wait()
    total = jnp.zeros((FR * CELLS, CH), F32)
    for i in range(3):
        for j in range(3):
            for k in range(3):
                window = pad_ref[k, i : i + FR, j : j + 2]
                total = total + jnp.dot(
                    window.reshape(FR * CELLS, CH),
                    k_ref[(i * 3 + j) * 3 + k],
                    preferred_element_type=F32,
                )
    cells = total.reshape(FR, CELLS, CH) + x_ref[...].astype(F32).reshape(FR, CELLS, CH)
    cells = cells * live_ref[...][:, None, :]
    out_ref[...] = cells.astype(BF16).reshape(FR, ROWS, COLS, CH)


def finish_input(sums_ref, sc_ref, x_ref, g_ref, mean_ref, inv_ref, live_ref, out_ref):
    sums = sums_ref[...]
    spread = spread_matrix()
    first = hdot(sums[:, :GROUPS] / COUNT, spread)[:, None, :]
    second = hdot(sums[:, GROUPS : 2 * GROUPS] / COUNT, spread)[:, None, :]
    inv = inv_ref[...][:, None, :]
    xf = x_ref[...].astype(F32).reshape(FR, CELLS, CH)
    normalized = (xf - mean_ref[...][:, None, :]) * inv
    norm_grad = inv * (sc_ref[...] - first - normalized * second)
    grad = g_ref[...].astype(F32).reshape(FR, CELLS, CH) * live_ref[...][:, None, :]
    out_ref[...] = (grad + norm_grad).astype(BF16).reshape(FR, ROWS, COLS, CH)


def sum_clips(own_h, one_h, two_h, three_h, kg_h, gain_h, in_ref, kg_ref, gain_ref, sem):
    x_at = lax.axis_index("x")
    copies = []
    for d, src in enumerate((own_h, one_h, two_h, three_h)):
        copies.append(
            pltpu.make_async_copy(src, in_ref.at[lax.rem(x_at + NX - d, NX)], sem.at[d])
        )
    for copy in copies:
        copy.start()
    for copy in copies:
        copy.wait()
    total = ((in_ref[0] + in_ref[1]) + in_ref[2]) + in_ref[3]
    for tap in range(TAPS):
        kg_ref[tap] = total[4 * tap : 4 * tap + 4]
    gain_ref[...] = total[4 * TAPS : 4 * TAPS + 1]
    out = (
        pltpu.make_async_copy(kg_ref, kg_h, sem.at[4]),
        pltpu.make_async_copy(gain_ref, gain_h, sem.at[5]),
    )
    for copy in out:
        copy.start()
    for copy in out:
        copy.wait()


HBM = pl.BlockSpec(memory_space=pltpu.HBM)
SMEM = pl.BlockSpec(memory_space=pltpu.SMEM)


def stay_out(array):
    return pltpu.with_memory_space_constraint(array, pltpu.HBM)


def shapes(outs):
    return tuple(jax.ShapeDtypeStruct(s, d) for s, d in outs)


def call(body, outs, args, specs, scratch, flops=0, limit=32, aliases={}):
    return pl.pallas_call(
        body,
        out_shape=shapes(outs),
        in_specs=specs,
        out_specs=tuple(HBM for _ in outs),
        scratch_shapes=list(scratch),
        input_output_aliases=aliases,
        compiler_params=pltpu.CompilerParams(vmem_limit_bytes=limit * 2**20),
        cost_estimate=pl.CostEstimate(flops=flops, bytes_accessed=2**20, transcendentals=0),
        name=body.__name__,
    )(*args)


def run(body, outs, args, scratch=(), late=None, smem=(), flops=0, rows={}):
    count, outputs = len(args), len(outs)
    moved = [at for at in range(count) if at not in smem]

    def kernel(*refs):
        ins, targets = list(refs[:count]), refs[count : count + outputs]
        rest = refs[count + outputs :]
        buffers, rest = rest[: len(moved)], rest[len(moved) :]
        results, rest = rest[:outputs], rest[outputs:]
        sem, extra = rest[0], rest[1:]
        copies = [
            pltpu.make_async_copy(
                ins[at].at[rows[at][0] : rows[at][1]] if at in rows else ins[at], buffers[n], sem.at[n]
            )
            for n, at in enumerate(moved)
        ]
        for copy in copies:
            copy.start()
        for n, at in enumerate(moved):
            ins[at] = buffers[n]
        held = copies.pop(moved.index(late)) if late is not None else None
        for copy in copies:
            copy.wait()
        if held is None:
            body(*ins, *results, *extra)
        else:
            body(*ins, *results, *extra, held)
        copies = [
            pltpu.make_async_copy(results[n], targets[n], sem.at[len(moved) + n])
            for n in range(outputs)
        ]
        for copy in copies:
            copy.start()
        for copy in copies:
            copy.wait()

    kernel.__name__ = body.__name__
    specs = [SMEM if at in smem else HBM for at in range(count)]
    buffers = []
    for at in moved:
        shape = args[at].shape
        if at in rows:
            shape = (rows[at][1] - rows[at][0],) + shape[1:]
        buffers.append(pltpu.VMEM(shape, args[at].dtype))
    buffers += [pltpu.VMEM(s, d) for s, d in outs]
    buffers += [pltpu.SemaphoreType.DMA((len(moved) + outputs,))]
    return call(kernel, outs, args, specs, buffers + list(scratch), flops)


def pack_body(*refs):
    sources, outs = refs[:4], refs[4:8]
    x_ref, g_ref, hp_ref, hn_ref, buf, sem = refs[8:]
    pairs = tuple(zip(sources, (x_ref, g_ref, hp_ref, hn_ref)))
    copies = [pltpu.make_async_copy(a, b, sem.at[n]) for n, (a, b) in enumerate(pairs)]
    for copy in copies:
        copy.start()
    for copy in copies:
        copy.wait()
    pack_slices(x_ref, g_ref, hp_ref, hn_ref, buf)
    y_at = lax.axis_index("y")
    copies = [
        pltpu.make_async_copy(buf.at[lax.rem(y_at + d, NY)], out, sem.at[4 + d])
        for d, out in enumerate(outs)
    ]
    for copy in copies:
        copy.start()
    for copy in copies:
        copy.wait()


def local(video_latent, frame_counts, conv_kernel, norm_gain, output_grad):
    x = stay_out(video_latent.reshape(FR, ROWS, COLS, CH))
    g = stay_out(output_grad.reshape(FR, ROWS, COLS, CH))
    gain = stay_out(norm_gain.reshape(1, CH))
    conv_kernel = stay_out(conv_kernel)
    space = ("y", "z", "c")
    cells = (FR, ROWS, COLS, CH)
    wide = (FR, CH)
    halo = (2, FR, COLS, CH)
    swap = [(0, 1), (1, 0)]
    dma = pltpu.SemaphoreType.DMA

    up, dn, stats, live = run(
        edges_and_sums,
        [(halo, BF16), (halo, BF16), ((FR, 128), F32), (wide, F32)],
        (x, g, frame_counts),
        smem=(2,),
    )
    other = lax.ppermute(stats, "c", swap)
    (stats,) = run(pair_sums, [((NY * NZ, 16, 128), F32)], (stats, other))
    stats, up, dn = lax.optimization_barrier((stats, up, dn))
    hp = lax.ppermute(dn, space, [(i, i + 1) for i in range(SPACE - 1)])
    hn = lax.ppermute(up, space, [(i + 1, i) for i in range(SPACE - 1)])
    stats = lax.all_to_all(stats, ("y", "z"), 0, 0)
    block = (BLOCK, BSL)
    packed = call(
        pack_body,
        [(block, BF16)] * NY,
        (x, g, hp, hn),
        [HBM] * 4,
        [pltpu.VMEM(cells, BF16)] * 2
        + [pltpu.VMEM(halo, BF16)] * 2
        + [pltpu.VMEM((NY,) + block, BF16), dma((8,))],
    )
    near = [packed[0]] + [
        lax.ppermute(packed[d], "y", [(i, (i + d) % NY) for i in range(NY)]) for d in range(1, NY)
    ]
    far = [lax.ppermute(a, "c", swap) for a in near]
    conv_flops = 16 * TAPS * FR * CELLS * CH * CH
    padded = pltpu.VMEM((3, FR + 2, 4, COLS, CH), BF16)
    (act_grad,) = run(
        backward_conv,
        [((FR * CELLS, CH), F32)],
        (g, hp, hn, conv_kernel, live),
        scratch=[padded],
        late=3,
        flops=0,
    )
    terms, scaled, mean, inv = run(
        group_terms,
        [((NY * NC, FR, 128), F32), ((FR, CELLS, CH), F32), (wide, F32), (wide, F32)],
        (stats, x, act_grad, gain),
    )
    terms = lax.all_to_all(terms, ("y", "c"), 0, 0)
    part = (NZ, PROWS, CH)
    whole_part = (NZ, PROWS + TERMS, CH)
    (partial,) = call(
        kernel_part,
        [(whole_part, BF16)],
        (*near, *far, mean, inv, gain, live),
        [HBM] * 12,
        [
            pltpu.VMEM((8, BLOCK, BSL), BF16),
            pltpu.VMEM(wide, F32),
            pltpu.VMEM(wide, F32),
            pltpu.VMEM((1, CH), F32),
            pltpu.VMEM(wide, F32),
            pltpu.VMEM(part, BF16),
            pltpu.VMEM((3, FR, NY, 6, COLS, Q * APART), BF16),
            pltpu.VMEM((FR, NY, 4, COLS, CH), F32),
            pltpu.VMEM(part, F32),
            dma((12,)),
        ],
        flops=conv_flops,
    )
    (merged,) = call(
        add_sums,
        [(whole_part, BF16)],
        (partial, terms),
        [HBM] * 2,
        [pltpu.VMEM((NY * NC, FR, 128), F32), pltpu.VMEM((NZ, TERMS, CH), BF16), dma((2,))],
        aliases={0: 0},
    )
    merged, late_mean = lax.optimization_barrier((merged, mean))
    merged = lax.all_to_all(merged, "z", 0, 0)
    (block_output,) = run(
        forward_conv,
        [(cells, BF16)],
        (x, hp, hn, late_mean, inv, gain, conv_kernel, live),
        scratch=[padded],
        late=6,
        flops=conv_flops,
    )
    merged, block_output = lax.optimization_barrier((merged, block_output))
    rows, sums = run(sum_rows, [((PROWS, CH), F32), ((FR, 128), F32)], (merged,))
    others = [rows] + [
        lax.ppermute(rows, "x", [(i, (i + d) % NX) for i in range(NX)]) for d in range(1, NX)
    ]
    (input_grad,) = run(
        finish_input, [(cells, BF16)], (sums, scaled, x, g, mean, inv, live)
    )
    kernel_grad, gain_grad = call(
        sum_clips,
        [((TAPS, 4, CH), F32), ((1, CH), F32)],
        others,
        [HBM] * 4,
        [
            pltpu.VMEM((NX, PROWS, CH), F32),
            pltpu.VMEM((TAPS, 4, CH), F32),
            pltpu.VMEM((1, CH), F32),
            dma((6,)),
        ],
    )
    whole = (1,) + cells
    return (
        block_output.reshape(whole),
        input_grad.reshape(whole),
        jnp.swapaxes(kernel_grad, 0, 1),
        gain_grad.reshape(CH),
    )


def solution(mesh):
    fine = Mesh(mesh.devices.reshape(NX, NY, NZ, NC), ("x", "y", "z", "c"))
    space = ("y", "z", "c")
    cells = P("x", None, space, None, None)
    return jax.shard_map(
        local,
        mesh=fine,
        in_specs=(cells, P("x"), P(), P(), cells),
        out_specs=(cells, cells, P(space, None, None), P()),
        check_vma=False,
    )
```

```python
import jax
import jax.numpy as jnp
from jax import lax
from jax.experimental import pallas as pl
from jax.experimental.pallas import tpu as pltpu
from jax.sharding import Mesh
from jax.sharding import PartitionSpec as P

F32 = jnp.float32
BF16 = jnp.bfloat16
NX, NY, NZ, NC = 4, 4, 8, 2
SPACE = NY * NZ * NC
FR, ROWS, COLS, CH = 8, 2, 16, 256
CELLS = ROWS * COLS
GROUPS = 32
GC = CH // GROUPS
ASL = CH // NY
BSL = CH // NC
EPSILON = 1e-05
COUNT = CELLS * SPACE * GC
AROWS = FR // 2 * 3 * COLS
GROWS = FR * ROWS * COLS
TAPS = 27
PROWS = 112
Q = 4
APART = ASL // NC
BLOCK = AROWS + NC * GROWS
TERMS = 16
HALO = FR * COLS
HI = lax.Precision.HIGHEST


def hdot(a, b):
    return jnp.dot(a, b, preferred_element_type=F32, precision=HI)


def gather_matrix():
    lane = lax.broadcasted_iota(jnp.int32, (CH, GROUPS), 0)
    group = lax.broadcasted_iota(jnp.int32, (CH, GROUPS), 1)
    return (lane // GC == group).astype(F32)


def spread_matrix():
    group = lax.broadcasted_iota(jnp.int32, (GROUPS, CH), 0)
    lane = lax.broadcasted_iota(jnp.int32, (GROUPS, CH), 1)
    return (lane // GC == group).astype(F32)


def shifted(cells, k):
    if k == 1:
        return cells
    zero = jnp.zeros(cells.shape[:-2] + (1, cells.shape[-1]), cells.dtype)
    if k == 0:
        return jnp.concatenate([zero, cells[..., :-1, :]], axis=-2)
    return jnp.concatenate([cells[..., 1:, :], zero], axis=-2)


def edges_and_sums(x_ref, g_ref, n_ref, in_ref, out_ref, st_ref, live_ref):
    first = lax.axis_index("c") == 0
    for n, ref in enumerate((x_ref, g_ref)):
        low, high = ref[:, 0], ref[:, 1]
        inner, outer = jnp.where(first, high, low), jnp.where(first, low, high)
        in_ref[n * HALO : (n + 1) * HALO] = inner.reshape(HALO, CH)
        out_ref[n * HALO : (n + 1) * HALO] = outer.reshape(HALO, CH)
    live_ref[...] = (lax.broadcasted_iota(jnp.int32, (FR, CH), 0) < n_ref[0]).astype(F32)
    xf = x_ref[...].astype(F32).reshape(FR, CELLS, CH)
    gather = gather_matrix()
    mean = hdot(jnp.sum(xf, axis=1), gather) / (CELLS * GC)
    centered = xf - hdot(mean, spread_matrix())[:, None, :]
    squares = hdot(jnp.sum(centered * centered, axis=1), gather)
    sums = jnp.concatenate([mean, squares, jnp.zeros((FR, 2 * GROUPS), F32)], axis=1)
    st_ref[...] = sums
    in_ref[2 * HALO :] = as_terms(sums)


def outside(in_ref, out_ref):
    first = lax.axis_index("c") == 0
    inner = in_ref[...].reshape(FR, COLS, CH)
    outer = out_ref[...].reshape(FR, COLS, CH)
    return jnp.where(first, outer, inner), jnp.where(first, inner, outer)


def combined(parts, squares, each):
    count = parts.shape[0]
    mean = jnp.sum(parts, axis=0) / count
    apart = parts - mean[None]
    return mean, jnp.sum(squares + each * (apart * apart), axis=0)


def pair_sums(own_ref, other_ref, out_ref):
    both = jnp.stack([own_ref[...], from_terms(other_ref[...].astype(F32))])
    mean, squares = combined(both[:, :, :GROUPS], both[:, :, GROUPS : 2 * GROUPS], CELLS * GC)
    row = jnp.concatenate([mean, squares, jnp.zeros((FR, 2 * GROUPS), F32)], axis=1)
    out_ref[...] = jnp.broadcast_to(row[None], (NY * NZ, FR, 128))


def as_terms(values):
    high = values.astype(BF16).astype(F32)
    middle = (values - high).astype(BF16).astype(F32)
    low = values - high - middle
    upper = jnp.concatenate([high, middle], axis=1)
    lower = jnp.concatenate([low, jnp.zeros((FR, 128), F32)], axis=1)
    return jnp.concatenate([upper, lower], axis=0).astype(BF16)


def from_terms(terms):
    return (terms[FR:, :128] + terms[:FR, 128:]) + terms[:FR, :128]


def pack_slices(x_ref, g_ref, hp_ref, hn_ref, out_ref):
    upper = lax.axis_index("c") == 0
    own = [x_ref[:, 0], x_ref[:, 1]]
    before, after = outside(hp_ref, hn_ref)
    rows = [
        jnp.where(upper, before, own[0]),
        jnp.where(upper, own[0], own[1]),
        jnp.where(upper, own[1], after),
    ]
    three = jnp.stack(rows, axis=1).reshape(FR // 2, 2, 3, COLS, CH)
    for y in range(NY):
        part = three[..., y * ASL : (y + 1) * ASL]
        pair = jnp.concatenate([part[:, 0], part[:, 1]], axis=-1)
        out_ref[y, :AROWS] = pair.reshape(AROWS, 2 * ASL)
        for c in range(NC):
            at = AROWS + c * GROWS
            out_ref[y, at : at + GROWS] = g_ref[..., c * BSL : (c + 1) * BSL].reshape(GROWS, BSL)


def backward_conv(g_ref, hp_ref, hn_ref, k_ref, live_ref, out_ref, pad_ref, held):
    live = live_ref[...][:, None, :]
    before, after = outside(hp_ref, hn_ref)
    rows = [before, g_ref[:, 0], g_ref[:, 1], after]
    for r in range(4):
        cells = rows[r].astype(F32) * live
        for k in range(3):
            pad_ref[k, :FR, r] = shifted(cells, k).astype(BF16)
    pad_ref[:, FR:] = jnp.zeros((3, 2, 4, COLS, CH), BF16)
    held.wait()
    total = jnp.zeros((FR * CELLS, CH), F32)
    for i in range(3):
        for j in range(3):
            for k in range(3):
                window = pad_ref[2 - k, 2 - i : 2 - i + FR, 2 - j : 4 - j]
                total = total + lax.dot_general(
                    window.reshape(FR * CELLS, CH),
                    k_ref[(i * 3 + j) * 3 + k],
                    (((1,), (1,)), ((), ())),
                    preferred_element_type=F32,
                )
    out_ref[...] = total


def group_terms(st_ref, x_ref, ag_ref, gain_ref, out_ref, sc_ref, mean_ref, inv_ref):
    mean, whole = combined(
        st_ref[:, :FR, :GROUPS], st_ref[:, :FR, GROUPS : 2 * GROUPS], NC * CELLS * GC
    )
    spread = spread_matrix()
    mean_all = hdot(mean, spread)
    inv_all = hdot(lax.rsqrt(whole / COUNT + EPSILON), spread)
    mean_ref[...] = mean_all
    inv_ref[...] = inv_all
    gain = gain_ref[...][None]
    xf = x_ref[...].astype(F32).reshape(FR, CELLS, CH)
    normalized = (xf - mean_all[:, None, :]) * inv_all[:, None, :]
    gated = normalized * gain
    sig = jax.nn.sigmoid(gated)
    pre = ag_ref[...].reshape(FR, CELLS, CH) * sig * (1.0 + gated * (1.0 - sig))
    scaled = pre * gain
    sc_ref[...] = scaled
    gather = gather_matrix()
    first = hdot(jnp.sum(scaled, axis=1), gather)
    by_channel = jnp.sum(pre * normalized, axis=1)
    second = hdot(by_channel * gain_ref[...], gather)
    gain_part = jnp.sum(by_channel, axis=0, keepdims=True)
    row = lax.broadcasted_iota(jnp.int32, (FR, CH), 0)
    lane = lax.broadcasted_iota(jnp.int32, (FR, CH), 1)
    folded = jnp.where(lane // GROUPS == row, jnp.broadcast_to(gain_part, (FR, CH)), 0.0)
    fold_lane = lax.broadcasted_iota(jnp.int32, (CH, GROUPS), 0)
    fold_at = lax.broadcasted_iota(jnp.int32, (CH, GROUPS), 1)
    folded = hdot(folded, (fold_lane % GROUPS == fold_at).astype(F32))
    everything = jnp.concatenate([first, second, folded, jnp.zeros((FR, GROUPS), F32)], axis=1)
    out_ref[...] = jnp.broadcast_to(everything[None], (NY * NC, FR, 128))


def kernel_part(*refs):
    blocks, (mean_h, inv_h, gain_h, live_h, out_h) = refs[:8], refs[8:13]
    in_ref, mean_ref, inv_ref, gain_ref, live_ref, out_ref, pad_ref, grad_ref, sum_ref, sem = refs[13:]
    y_at, z_at, c_at = lax.axis_index("y"), lax.axis_index("z"), lax.axis_index("c")
    pairs = [(blocks[n], in_ref.at[n]) for n in range(8)]
    pairs += [(mean_h, mean_ref), (inv_h, inv_ref), (gain_h, gain_ref), (live_h, live_ref)]
    copies = [pltpu.make_async_copy(a, b, sem.at[n]) for n, (a, b) in enumerate(pairs)]
    for copy in copies:
        copy.start()
    for copy in copies[8:]:
        copy.wait()
    width = Q * APART
    lane = lax.broadcasted_iota(jnp.int32, (CH, width), 0)
    slot = lax.broadcasted_iota(jnp.int32, (CH, width), 1)
    channel = GC * ((slot % APART) // 4) + 4 * c_at + slot % 4
    pick = (lane == y_at * ASL + channel).astype(F32)
    mean2 = hdot(mean_ref[...], pick)
    inv2 = hdot(inv_ref[...], pick)
    gain2 = hdot(gain_ref[...], pick)
    live = live_ref[:, :BSL][:, None, None, :]
    quarter = lax.broadcasted_iota(jnp.int32, (1, width), 1) // APART
    centers, scales = [], []
    for u in range(2):
        center, scale = mean2[4 * u : 4 * u + 1], inv2[4 * u : 4 * u + 1]
        for q in range(1, Q):
            center = jnp.where(quarter == q, mean2[4 * u + q : 4 * u + q + 1], center)
            scale = jnp.where(quarter == q, inv2[4 * u + q : 4 * u + q + 1], scale)
        centers.append(center)
        scales.append(scale * gain2)
    lane = lax.broadcasted_iota(jnp.int32, (2 * ASL, width), 0)
    slot = lax.broadcasted_iota(jnp.int32, (2 * ASL, width), 1)
    channel = GC * ((slot % APART) // 4) + 4 * c_at + slot % 4
    chosen = [
        (lane == (slot // APART - 2 * half) * ASL + channel).astype(BF16) for half in range(2)
    ]
    shape = (3, COLS, width)
    place = lax.broadcasted_iota(jnp.int32, shape, 2) // APART
    row = lax.broadcasted_iota(jnp.int32, shape, 0)
    block = 3 * COLS
    for n in range(8):
        copies[n].wait()
        d = n % 4
        y = lax.rem(y_at + NY - d, NY)
        c = c_at if n < 4 else 1 - c_at
        top = (y == 0) & (z_at == 0) & (c == 0)
        bottom = (y == NY - 1) & (z_at == NZ - 1) & (c == NC - 1)
        edge = jnp.where(top, 0, jnp.where(bottom, 2, 3))
        inside = (row != edge).astype(F32)
        acts = []
        for u in range(2):
            at = 2 * u * block
            raw = jnp.dot(
                in_ref[n, at : at + block], chosen[0], preferred_element_type=F32
            ) + jnp.dot(
                in_ref[n, at + block : at + 2 * block], chosen[1], preferred_element_type=F32
            )
            gated = (raw - centers[u]) * scales[u]
            acts.append((gated * jax.nn.sigmoid(gated)).reshape(shape) * inside)
        a, b = acts
        a1, a2, b1 = pltpu.roll(a, 32, 2), pltpu.roll(a, 64, 2), pltpu.roll(b, 32, 2)
        b2 = pltpu.roll(b, 64, 2)
        frames = [
            jnp.where(place < 2, 0.0, a2),
            jnp.where(place < 1, 0.0, a1),
            a,
            pltpu.roll(a, 96, 2),
            jnp.where(place < 2, a2, b2),
            jnp.where(place < 1, a1, b1),
            b,
            pltpu.roll(b, 96, 2),
        ]
        for f in range(FR):
            for k in range(3):
                pad_ref[k, f, d, pl.ds(3 * c, 3)] = shifted(frames[f], k).astype(BF16)
        for h in range(NC):
            at = AROWS + h * GROWS
            cells = in_ref[n, at : at + GROWS].astype(F32).reshape(FR, ROWS, COLS, BSL) * live
            grad_ref[:, d, pl.ds(2 * c, 2), :, h * BSL : (h + 1) * BSL] = cells
    cells = FR * NY * 4 * COLS
    turned_grad = grad_ref[...].reshape(cells, CH).T.astype(BF16)
    sum_ref[:, 4 * TAPS :] = jnp.zeros((NZ, PROWS - 4 * TAPS, CH), F32)
    combos = [(j, k) for j in range(3) for k in range(3)]
    for first in range(0, 9, 2):
        group = combos[first : first + 2]
        windows = [pad_ref[k, :, :, j : j + 4].reshape(cells, width) for j, k in group]
        window = windows[0] if len(windows) == 1 else jnp.concatenate(windows, axis=1)
        product = jnp.dot(turned_grad, window, preferred_element_type=F32).T
        for n, (j, k) in enumerate(group):
            for i in range(3):
                tap = (i * 3 + j) * 3 + k
                at = n * width + i * APART
                piece = product[at : at + APART].reshape(NZ, 4, CH)
                sum_ref[:, tap * 4 : tap * 4 + 4] = piece
    out_ref[...] = sum_ref[...].astype(BF16)
    copy = pltpu.make_async_copy(out_ref, out_h.at[:, :PROWS], sem.at[0])
    copy.start()
    copy.wait()


def add_sums(part_h, b_h, out_h, b_ref, out_ref, sem):
    copy = pltpu.make_async_copy(b_h, b_ref, sem.at[0])
    copy.start()
    copy.wait()
    terms = as_terms(jnp.sum(b_ref[...], axis=0))
    out_ref[...] = jnp.broadcast_to(terms[None], (NZ, TERMS, CH))
    copy = pltpu.make_async_copy(out_ref, out_h.at[:, PROWS:], sem.at[1])
    copy.start()
    copy.wait()


def sum_rows(in_ref, out_ref, sums_ref):
    total = jnp.sum(in_ref[...].astype(F32), axis=0)
    sums = from_terms(total[PROWS:])
    sums_ref[...] = sums
    fold_at = lax.broadcasted_iota(jnp.int32, (GROUPS, CH), 0)
    fold_lane = lax.broadcasted_iota(jnp.int32, (GROUPS, CH), 1)
    wide = hdot(sums[:, 2 * GROUPS : 3 * GROUPS], (fold_lane % GROUPS == fold_at).astype(F32))
    row = lax.broadcasted_iota(jnp.int32, (FR, CH), 0)
    lane = lax.broadcasted_iota(jnp.int32, (FR, CH), 1)
    gain = jnp.sum(jnp.where(lane // GROUPS == row, wide, 0.0), axis=0, keepdims=True)
    out_ref[...] = total[:PROWS]
    out_ref[4 * TAPS : 4 * TAPS + 1] = gain


def forward_conv(x_ref, hp_ref, hn_ref, mean_ref, inv_ref, gain_ref, k_ref, live_ref, out_ref, pad_ref, held):
    s_at = (lax.axis_index("y") * NZ + lax.axis_index("z")) * NC + lax.axis_index("c")
    before, after = outside(hp_ref, hn_ref)
    rows = [before, x_ref[:, 0], x_ref[:, 1], after]
    mean = mean_ref[...][:, None, :]
    inv = inv_ref[...][:, None, :]
    gain = gain_ref[...][None]
    for r in range(4):
        gated = (rows[r].astype(F32) - mean) * inv * gain
        act = gated * jax.nn.sigmoid(gated)
        if r == 0:
            act = jnp.where(s_at == 0, 0.0, act)
        if r == 3:
            act = jnp.where(s_at == SPACE - 1, 0.0, act)
        for k in range(3):
            pad_ref[k, 2:, r] = shifted(act, k).astype(BF16)
    pad_ref[:, :2] = jnp.zeros((3, 2, 4, COLS, CH), BF16)
    held.wait()
    total = jnp.zeros((FR * CELLS, CH), F32)
    for i in range(3):
        for j in range(3):
            for k in range(3):
                window = pad_ref[k, i : i + FR, j : j + 2]
                total = total + jnp.dot(
                    window.reshape(FR * CELLS, CH),
                    k_ref[(i * 3 + j) * 3 + k],
                    preferred_element_type=F32,
                )
    cells = total.reshape(FR, CELLS, CH) + x_ref[...].astype(F32).reshape(FR, CELLS, CH)
    cells = cells * live_ref[...][:, None, :]
    out_ref[...] = cells.astype(BF16).reshape(FR, ROWS, COLS, CH)


def finish_input(sums_ref, sc_ref, x_ref, g_ref, mean_ref, inv_ref, live_ref, out_ref):
    sums = sums_ref[...]
    spread = spread_matrix()
    first = hdot(sums[:, :GROUPS] / COUNT, spread)[:, None, :]
    second = hdot(sums[:, GROUPS : 2 * GROUPS] / COUNT, spread)[:, None, :]
    inv = inv_ref[...][:, None, :]
    xf = x_ref[...].astype(F32).reshape(FR, CELLS, CH)
    normalized = (xf - mean_ref[...][:, None, :]) * inv
    norm_grad = inv * (sc_ref[...] - first - normalized * second)
    grad = g_ref[...].astype(F32).reshape(FR, CELLS, CH) * live_ref[...][:, None, :]
    out_ref[...] = (grad + norm_grad).astype(BF16).reshape(FR, ROWS, COLS, CH)


def sum_clips(own_h, one_h, two_h, three_h, kg_h, gain_h, in_ref, kg_ref, gain_ref, sem):
    x_at = lax.axis_index("x")
    copies = []
    for d, src in enumerate((own_h, one_h, two_h, three_h)):
        copies.append(
            pltpu.make_async_copy(src, in_ref.at[lax.rem(x_at + NX - d, NX)], sem.at[d])
        )
    for copy in copies:
        copy.start()
    for copy in copies:
        copy.wait()
    total = ((in_ref[0] + in_ref[1]) + in_ref[2]) + in_ref[3]
    for tap in range(TAPS):
        kg_ref[tap] = total[4 * tap : 4 * tap + 4]
    gain_ref[...] = total[4 * TAPS : 4 * TAPS + 1]
    out = (
        pltpu.make_async_copy(kg_ref, kg_h, sem.at[4]),
        pltpu.make_async_copy(gain_ref, gain_h, sem.at[5]),
    )
    for copy in out:
        copy.start()
    for copy in out:
        copy.wait()


HBM = pl.BlockSpec(memory_space=pltpu.HBM)
SMEM = pl.BlockSpec(memory_space=pltpu.SMEM)


def stay_out(array):
    return pltpu.with_memory_space_constraint(array, pltpu.HBM)


def shapes(outs):
    return tuple(jax.ShapeDtypeStruct(s, d) for s, d in outs)


def call(body, outs, args, specs, scratch, flops=0, limit=32, aliases={}):
    return pl.pallas_call(
        body,
        out_shape=shapes(outs),
        in_specs=specs,
        out_specs=tuple(HBM for _ in outs),
        scratch_shapes=list(scratch),
        input_output_aliases=aliases,
        compiler_params=pltpu.CompilerParams(vmem_limit_bytes=limit * 2**20),
        cost_estimate=pl.CostEstimate(flops=flops, bytes_accessed=2**20, transcendentals=0),
        name=body.__name__,
    )(*args)


def run(body, outs, args, scratch=(), late=None, smem=(), flops=0, rows={}):
    count, outputs = len(args), len(outs)
    moved = [at for at in range(count) if at not in smem]

    def kernel(*refs):
        ins, targets = list(refs[:count]), refs[count : count + outputs]
        rest = refs[count + outputs :]
        buffers, rest = rest[: len(moved)], rest[len(moved) :]
        results, rest = rest[:outputs], rest[outputs:]
        sem, extra = rest[0], rest[1:]
        copies = [
            pltpu.make_async_copy(
                ins[at].at[rows[at][0] : rows[at][1]] if at in rows else ins[at], buffers[n], sem.at[n]
            )
            for n, at in enumerate(moved)
        ]
        for copy in copies:
            copy.start()
        for n, at in enumerate(moved):
            ins[at] = buffers[n]
        held = copies.pop(moved.index(late)) if late is not None else None
        for copy in copies:
            copy.wait()
        if held is None:
            body(*ins, *results, *extra)
        else:
            body(*ins, *results, *extra, held)
        copies = [
            pltpu.make_async_copy(results[n], targets[n], sem.at[len(moved) + n])
            for n in range(outputs)
        ]
        for copy in copies:
            copy.start()
        for copy in copies:
            copy.wait()

    kernel.__name__ = body.__name__
    specs = [SMEM if at in smem else HBM for at in range(count)]
    buffers = []
    for at in moved:
        shape = args[at].shape
        if at in rows:
            shape = (rows[at][1] - rows[at][0],) + shape[1:]
        buffers.append(pltpu.VMEM(shape, args[at].dtype))
    buffers += [pltpu.VMEM(s, d) for s, d in outs]
    buffers += [pltpu.SemaphoreType.DMA((len(moved) + outputs,))]
    return call(kernel, outs, args, specs, buffers + list(scratch), flops)


def pack_body(*refs):
    sources, outs = refs[:4], refs[4:8]
    x_ref, g_ref, hp_ref, hn_ref, buf, sem = refs[8:]
    sources = (sources[0], sources[1], sources[2].at[:HALO], sources[3].at[:HALO])
    pairs = tuple(zip(sources, (x_ref, g_ref, hp_ref, hn_ref)))
    copies = [pltpu.make_async_copy(a, b, sem.at[n]) for n, (a, b) in enumerate(pairs)]
    for copy in copies:
        copy.start()
    for copy in copies:
        copy.wait()
    pack_slices(x_ref, g_ref, hp_ref, hn_ref, buf)
    y_at = lax.axis_index("y")
    copies = [
        pltpu.make_async_copy(buf.at[lax.rem(y_at + d, NY)], out, sem.at[4 + d])
        for d, out in enumerate(outs)
    ]
    for copy in copies:
        copy.start()
    for copy in copies:
        copy.wait()


def local(video_latent, frame_counts, conv_kernel, norm_gain, output_grad):
    x = stay_out(video_latent.reshape(FR, ROWS, COLS, CH))
    g = stay_out(output_grad.reshape(FR, ROWS, COLS, CH))
    gain = stay_out(norm_gain.reshape(1, CH))
    conv_kernel = stay_out(conv_kernel)
    space = ("y", "z", "c")
    cells = (FR, ROWS, COLS, CH)
    wide = (FR, CH)
    swap = [(0, 1), (1, 0)]
    dma = pltpu.SemaphoreType.DMA

    inner, outer, stats, live = run(
        edges_and_sums,
        [
            ((2 * HALO + TERMS, CH), BF16),
            ((2 * HALO, CH), BF16),
            ((FR, 128), F32),
            (wide, F32),
        ],
        (x, g, frame_counts),
        smem=(2,),
    )
    hp = lax.ppermute(inner, "c", swap)
    hn = lax.ppermute(
        outer,
        space,
        [(i, i - 1 if i % 2 == 0 else i + 1) for i in range(1, SPACE - 1)],
    )
    (stats,) = run(
        pair_sums,
        [((NY * NZ, FR, 128), F32)],
        (stats, hp),
        rows={1: (2 * HALO, 2 * HALO + TERMS)},
    )
    stats = lax.all_to_all(stats, ("y", "z"), 0, 0)
    block = (BLOCK, BSL)
    packed = call(
        pack_body,
        [(block, BF16)] * NY,
        (x, g, hp, hn),
        [HBM] * 4,
        [pltpu.VMEM(cells, BF16)] * 2
        + [pltpu.VMEM((HALO, CH), BF16)] * 2
        + [pltpu.VMEM((NY,) + block, BF16), dma((8,))],
    )
    near = [packed[0]] + [
        lax.ppermute(packed[d], "y", [(i, (i + d) % NY) for i in range(NY)]) for d in range(1, NY)
    ]
    conv_flops = 16 * TAPS * FR * CELLS * CH * CH
    padded = pltpu.VMEM((3, FR + 2, 4, COLS, CH), BF16)
    (act_grad,) = run(
        backward_conv,
        [((FR * CELLS, CH), F32)],
        (g, hp, hn, conv_kernel, live),
        rows={1: (HALO, 2 * HALO), 2: (HALO, 2 * HALO)},
        scratch=[padded],
        late=3,
        flops=0,
    )
    terms, scaled, mean, inv = run(
        group_terms,
        [((NY * NC, FR, 128), F32), ((FR, CELLS, CH), F32), (wide, F32), (wide, F32)],
        (stats, x, act_grad, gain),
    )
    *near, terms = lax.optimization_barrier((*near, terms))
    terms = lax.all_to_all(terms, ("y", "c"), 0, 0)
    far = [lax.ppermute(a, "c", swap) for a in near]
    part = (NZ, PROWS, CH)
    whole_part = (NZ, PROWS + TERMS, CH)
    (partial,) = call(
        kernel_part,
        [(whole_part, BF16)],
        (*near, *far, mean, inv, gain, live),
        [HBM] * 12,
        [
            pltpu.VMEM((8, BLOCK, BSL), BF16),
            pltpu.VMEM(wide, F32),
            pltpu.VMEM(wide, F32),
            pltpu.VMEM((1, CH), F32),
            pltpu.VMEM(wide, F32),
            pltpu.VMEM(part, BF16),
            pltpu.VMEM((3, FR, NY, 6, COLS, Q * APART), BF16),
            pltpu.VMEM((FR, NY, 4, COLS, CH), F32),
            pltpu.VMEM(part, F32),
            dma((12,)),
        ],
        flops=conv_flops,
    )
    (merged,) = call(
        add_sums,
        [(whole_part, BF16)],
        (partial, terms),
        [HBM] * 2,
        [pltpu.VMEM((NY * NC, FR, 128), F32), pltpu.VMEM((NZ, TERMS, CH), BF16), dma((2,))],
        aliases={0: 0},
    )
    merged, late_mean = lax.optimization_barrier((merged, mean))
    merged = lax.all_to_all(merged, "z", 0, 0)
    (block_output,) = run(
        forward_conv,
        [(cells, BF16)],
        (x, hp, hn, late_mean, inv, gain, conv_kernel, live),
        rows={1: (0, HALO), 2: (0, HALO)},
        scratch=[padded],
        late=6,
        flops=conv_flops,
    )
    merged, block_output = lax.optimization_barrier((merged, block_output))
    rows, sums = run(sum_rows, [((PROWS, CH), F32), ((FR, 128), F32)], (merged,))
    others = [rows] + [
        lax.ppermute(rows, "x", [(i, (i + d) % NX) for i in range(NX)]) for d in range(1, NX)
    ]
    (input_grad,) = run(
        finish_input, [(cells, BF16)], (sums, scaled, x, g, mean, inv, live)
    )
    kernel_grad, gain_grad = call(
        sum_clips,
        [((TAPS, 4, CH), F32), ((1, CH), F32)],
        others,
        [HBM] * 4,
        [
            pltpu.VMEM((NX, PROWS, CH), F32),
            pltpu.VMEM((TAPS, 4, CH), F32),
            pltpu.VMEM((1, CH), F32),
            dma((6,)),
        ],
    )
    whole = (1,) + cells
    return (
        block_output.reshape(whole),
        input_grad.reshape(whole),
        jnp.swapaxes(kernel_grad, 0, 1),
        gain_grad.reshape(CH),
    )


def solution(mesh):
    fine = Mesh(mesh.devices.reshape(NX, NY, NZ, NC), ("x", "y", "z", "c"))
    space = ("y", "z", "c")
    cells = P("x", None, space, None, None)
    return jax.shard_map(
        local,
        mesh=fine,
        in_specs=(cells, P("x"), P(), P(), cells),
        out_specs=(cells, cells, P(space, None, None), P()),
        check_vma=False,
    )
```

```python
import jax
import jax.numpy as jnp
from jax import lax
from jax.experimental import pallas as pl
from jax.experimental.pallas import tpu as pltpu
from jax.sharding import Mesh
from jax.sharding import PartitionSpec as P

F32 = jnp.float32
BF16 = jnp.bfloat16
NX, NY, NZ, NC = 4, 4, 8, 2
SPACE = NY * NZ * NC
FR, ROWS, COLS, CH = 8, 2, 16, 256
CELLS = ROWS * COLS
GROUPS = 32
GC = CH // GROUPS
ASL = CH // NY
BSL = CH // NC
EPSILON = 1e-05
COUNT = CELLS * SPACE * GC
AROWS = FR // 2 * 3 * COLS
GROWS = FR * ROWS * COLS
TAPS = 27
PROWS = 112
Q = 4
APART = ASL // NC
BLOCK = AROWS + NC * GROWS
TERMS = 16
HALO = FR * COLS
HI = lax.Precision.HIGHEST


def hdot(a, b):
    return jnp.dot(a, b, preferred_element_type=F32, precision=HI)


def gather_matrix():
    lane = lax.broadcasted_iota(jnp.int32, (CH, GROUPS), 0)
    group = lax.broadcasted_iota(jnp.int32, (CH, GROUPS), 1)
    return (lane // GC == group).astype(F32)


def spread_matrix():
    group = lax.broadcasted_iota(jnp.int32, (GROUPS, CH), 0)
    lane = lax.broadcasted_iota(jnp.int32, (GROUPS, CH), 1)
    return (lane // GC == group).astype(F32)


def shifted(cells, k):
    if k == 1:
        return cells
    zero = jnp.zeros(cells.shape[:-2] + (1, cells.shape[-1]), cells.dtype)
    if k == 0:
        return jnp.concatenate([zero, cells[..., :-1, :]], axis=-2)
    return jnp.concatenate([cells[..., 1:, :], zero], axis=-2)


def edges_and_sums(x_ref, g_ref, in_ref, out_ref, st_ref):
    first = lax.axis_index("c") == 0
    for n, ref in enumerate((x_ref, g_ref)):
        low, high = ref[:, 0], ref[:, 1]
        inner, outer = jnp.where(first, high, low), jnp.where(first, low, high)
        in_ref[n * HALO : (n + 1) * HALO] = inner.reshape(HALO, CH)
        out_ref[n * HALO : (n + 1) * HALO] = outer.reshape(HALO, CH)
    xf = x_ref[...].astype(F32).reshape(FR, CELLS, CH)
    gather = gather_matrix()
    mean = hdot(jnp.sum(xf, axis=1), gather) / (CELLS * GC)
    centered = xf - hdot(mean, spread_matrix())[:, None, :]
    squares = hdot(jnp.sum(centered * centered, axis=1), gather)
    sums = jnp.concatenate([mean, squares, jnp.zeros((FR, 2 * GROUPS), F32)], axis=1)
    st_ref[...] = sums
    in_ref[2 * HALO :] = as_terms(sums)


def outside(in_ref, out_ref):
    first = lax.axis_index("c") == 0
    inner = in_ref[...].reshape(FR, COLS, CH)
    outer = out_ref[...].reshape(FR, COLS, CH)
    return jnp.where(first, outer, inner), jnp.where(first, inner, outer)


def combined(parts, squares, each):
    count = parts.shape[0]
    mean = jnp.sum(parts, axis=0) / count
    apart = parts - mean[None]
    return mean, jnp.sum(squares + each * (apart * apart), axis=0)


def pair_sums(own_ref, other_ref, out_ref):
    both = jnp.stack([own_ref[...], from_terms(other_ref[...].astype(F32))])
    mean, squares = combined(both[:, :, :GROUPS], both[:, :, GROUPS : 2 * GROUPS], CELLS * GC)
    row = jnp.concatenate([mean, squares, jnp.zeros((FR, 2 * GROUPS), F32)], axis=1)
    out_ref[...] = jnp.broadcast_to(row[None], (NY * NZ, FR, 128))


def as_terms(values):
    high = values.astype(BF16).astype(F32)
    middle = (values - high).astype(BF16).astype(F32)
    low = values - high - middle
    upper = jnp.concatenate([high, middle], axis=1)
    lower = jnp.concatenate([low, jnp.zeros((FR, 128), F32)], axis=1)
    return jnp.concatenate([upper, lower], axis=0).astype(BF16)


def from_terms(terms):
    return (terms[FR:, :128] + terms[:FR, 128:]) + terms[:FR, :128]


def pack_slices(x_ref, g_ref, hp_ref, hn_ref, out_ref):
    upper = lax.axis_index("c") == 0
    own = [x_ref[:, 0], x_ref[:, 1]]
    before, after = outside(hp_ref, hn_ref)
    rows = [
        jnp.where(upper, before, own[0]),
        jnp.where(upper, own[0], own[1]),
        jnp.where(upper, own[1], after),
    ]
    three = jnp.stack(rows, axis=1).reshape(FR // 2, 2, 3, COLS, CH)
    for y in range(NY):
        part = three[..., y * ASL : (y + 1) * ASL]
        pair = jnp.concatenate([part[:, 0], part[:, 1]], axis=-1)
        out_ref[y, :AROWS] = pair.reshape(AROWS, 2 * ASL)
        for c in range(NC):
            at = AROWS + c * GROWS
            out_ref[y, at : at + GROWS] = g_ref[..., c * BSL : (c + 1) * BSL].reshape(GROWS, BSL)


def backward_conv(g_ref, hp_ref, hn_ref, k_ref, live_ref, pad_ref, held):
    live = live_ref[...][:, None, :]
    before, after = outside(hp_ref, hn_ref)
    rows = [before, g_ref[:, 0], g_ref[:, 1], after]
    for r in range(4):
        cells = rows[r].astype(F32) * live
        for k in range(3):
            pad_ref[k, :FR, r] = shifted(cells, k).astype(BF16)
    pad_ref[:, FR:] = jnp.zeros((3, 2, 4, COLS, CH), BF16)
    held.wait()
    total = jnp.zeros((FR * CELLS, CH), F32)
    for i in range(3):
        for j in range(3):
            for k in range(3):
                window = pad_ref[2 - k, 2 - i : 2 - i + FR, 2 - j : 4 - j]
                total = total + lax.dot_general(
                    window.reshape(FR * CELLS, CH),
                    k_ref[(i * 3 + j) * 3 + k],
                    (((1,), (1,)), ((), ())),
                    preferred_element_type=F32,
                )
    return total


def backward_terms(
    g_ref, hp_ref, hn_ref, k_ref, live_ref, st_ref, x_ref, gain_ref,
    out_ref, sc_ref, mean_ref, inv_ref, pad_ref, held,
):
    act_grad = backward_conv(g_ref, hp_ref, hn_ref, k_ref, live_ref, pad_ref, held)
    mean, whole = combined(
        st_ref[:, :FR, :GROUPS], st_ref[:, :FR, GROUPS : 2 * GROUPS], NC * CELLS * GC
    )
    spread = spread_matrix()
    mean_all = hdot(mean, spread)
    inv_all = hdot(lax.rsqrt(whole / COUNT + EPSILON), spread)
    mean_ref[...] = mean_all
    inv_ref[...] = inv_all
    gain = gain_ref[...][None]
    xf = x_ref[...].astype(F32).reshape(FR, CELLS, CH)
    normalized = (xf - mean_all[:, None, :]) * inv_all[:, None, :]
    gated = normalized * gain
    sig = jax.nn.sigmoid(gated)
    pre = act_grad.reshape(FR, CELLS, CH) * sig * (1.0 + gated * (1.0 - sig))
    scaled = pre * gain
    sc_ref[...] = scaled
    gather = gather_matrix()
    first = hdot(jnp.sum(scaled, axis=1), gather)
    by_channel = jnp.sum(pre * normalized, axis=1)
    second = hdot(by_channel * gain_ref[...], gather)
    gain_part = jnp.sum(by_channel, axis=0, keepdims=True)
    row = lax.broadcasted_iota(jnp.int32, (FR, CH), 0)
    lane = lax.broadcasted_iota(jnp.int32, (FR, CH), 1)
    folded = jnp.where(lane // GROUPS == row, jnp.broadcast_to(gain_part, (FR, CH)), 0.0)
    fold_lane = lax.broadcasted_iota(jnp.int32, (CH, GROUPS), 0)
    fold_at = lax.broadcasted_iota(jnp.int32, (CH, GROUPS), 1)
    folded = hdot(folded, (fold_lane % GROUPS == fold_at).astype(F32))
    everything = jnp.concatenate([first, second, folded, jnp.zeros((FR, GROUPS), F32)], axis=1)
    out_ref[...] = jnp.broadcast_to(everything[None], (NY * NC, FR, 128))


def kernel_part(*refs):
    blocks, (mean_h, inv_h, gain_h, live_h, out_h) = refs[:8], refs[8:13]
    in_ref, mean_ref, inv_ref, gain_ref, live_ref, out_ref, pad_ref, grad_ref, sum_ref, sem = refs[13:]
    y_at, z_at, c_at = lax.axis_index("y"), lax.axis_index("z"), lax.axis_index("c")
    pairs = [(blocks[n], in_ref.at[n]) for n in range(8)]
    pairs += [(mean_h, mean_ref), (inv_h, inv_ref), (gain_h, gain_ref), (live_h, live_ref)]
    copies = [pltpu.make_async_copy(a, b, sem.at[n]) for n, (a, b) in enumerate(pairs)]
    for copy in copies:
        copy.start()
    for copy in copies[8:]:
        copy.wait()
    width = Q * APART
    lane = lax.broadcasted_iota(jnp.int32, (CH, width), 0)
    slot = lax.broadcasted_iota(jnp.int32, (CH, width), 1)
    channel = GC * ((slot % APART) // 4) + 4 * c_at + slot % 4
    pick = (lane == y_at * ASL + channel).astype(F32)
    mean2 = hdot(mean_ref[...], pick)
    inv2 = hdot(inv_ref[...], pick)
    gain2 = hdot(gain_ref[...], pick)
    live = live_ref[:, :BSL].astype(BF16)[:, None, None, :]
    quarter = lax.broadcasted_iota(jnp.int32, (1, width), 1) // APART
    centers, scales = [], []
    for u in range(2):
        center, scale = mean2[4 * u : 4 * u + 1], inv2[4 * u : 4 * u + 1]
        for q in range(1, Q):
            center = jnp.where(quarter == q, mean2[4 * u + q : 4 * u + q + 1], center)
            scale = jnp.where(quarter == q, inv2[4 * u + q : 4 * u + q + 1], scale)
        centers.append(center)
        scales.append(scale * gain2)
    lane = lax.broadcasted_iota(jnp.int32, (2 * ASL, width), 0)
    slot = lax.broadcasted_iota(jnp.int32, (2 * ASL, width), 1)
    channel = GC * ((slot % APART) // 4) + 4 * c_at + slot % 4
    chosen = [
        (lane == (slot // APART - 2 * half) * ASL + channel).astype(BF16) for half in range(2)
    ]
    shape = (3, COLS, width)
    place = lax.broadcasted_iota(jnp.int32, shape, 2) // APART
    row = lax.broadcasted_iota(jnp.int32, shape, 0)
    block = 3 * COLS
    for n in range(8):
        copies[n].wait()
        d = n % 4
        y = lax.rem(y_at + NY - d, NY)
        c = c_at if n < 4 else 1 - c_at
        top = (y == 0) & (z_at == 0) & (c == 0)
        bottom = (y == NY - 1) & (z_at == NZ - 1) & (c == NC - 1)
        edge = jnp.where(top, 0, jnp.where(bottom, 2, 3))
        inside = (row != edge).astype(F32)
        acts = []
        for u in range(2):
            at = 2 * u * block
            raw = jnp.dot(
                in_ref[n, at : at + block], chosen[0], preferred_element_type=F32
            ) + jnp.dot(
                in_ref[n, at + block : at + 2 * block], chosen[1], preferred_element_type=F32
            )
            gated = (raw - centers[u]) * scales[u]
            acts.append((gated * jax.nn.sigmoid(gated)).reshape(shape) * inside)
        a, b = acts
        a1, a2, b1 = pltpu.roll(a, 32, 2), pltpu.roll(a, 64, 2), pltpu.roll(b, 32, 2)
        b2 = pltpu.roll(b, 64, 2)
        frames = [
            jnp.where(place < 2, 0.0, a2),
            jnp.where(place < 1, 0.0, a1),
            a,
            pltpu.roll(a, 96, 2),
            jnp.where(place < 2, a2, b2),
            jnp.where(place < 1, a1, b1),
            b,
            pltpu.roll(b, 96, 2),
        ]
        for f in range(FR):
            for k in range(3):
                pad_ref[k, f, d, pl.ds(3 * c, 3)] = shifted(frames[f], k).astype(BF16)
        for h in range(NC):
            at = AROWS + h * GROWS
            cells = in_ref[n, at : at + GROWS].reshape(FR, ROWS, COLS, BSL) * live
            grad_ref[:, d, pl.ds(2 * c, 2), :, h * BSL : (h + 1) * BSL] = cells
    cells = FR * NY * 4 * COLS
    turned_grad = grad_ref[...].reshape(cells, CH).T
    sum_ref[:, 4 * TAPS :] = jnp.zeros((NZ, PROWS - 4 * TAPS, CH), F32)
    combos = [(j, k) for j in range(3) for k in range(3)]
    for first in range(0, 9, 2):
        group = combos[first : first + 2]
        windows = [pad_ref[k, :, :, j : j + 4].reshape(cells, width) for j, k in group]
        window = windows[0] if len(windows) == 1 else jnp.concatenate(windows, axis=1)
        product = jnp.dot(turned_grad, window, preferred_element_type=F32)
        product = product.astype(BF16).T.astype(F32)
        for n, (j, k) in enumerate(group):
            for i in range(3):
                tap = (i * 3 + j) * 3 + k
                at = n * width + i * APART
                piece = product[at : at + APART].reshape(NZ, 4, CH)
                sum_ref[:, tap * 4 : tap * 4 + 4] = piece
    out_ref[...] = sum_ref[...].astype(BF16)
    copy = pltpu.make_async_copy(out_ref, out_h.at[:, :PROWS], sem.at[0])
    copy.start()
    copy.wait()


def add_sums(part_h, b_h, out_h, b_ref, out_ref, sem):
    copy = pltpu.make_async_copy(b_h, b_ref, sem.at[0])
    copy.start()
    copy.wait()
    terms = as_terms(jnp.sum(b_ref[...], axis=0))
    out_ref[...] = jnp.broadcast_to(terms[None], (NZ, TERMS, CH))
    copy = pltpu.make_async_copy(out_ref, out_h.at[:, PROWS:], sem.at[1])
    copy.start()
    copy.wait()


def sum_rows(in_ref, out_ref, sums_ref):
    total = jnp.sum(in_ref[...].astype(F32), axis=0)
    sums = from_terms(total[PROWS:])
    sums_ref[...] = sums
    fold_at = lax.broadcasted_iota(jnp.int32, (GROUPS, CH), 0)
    fold_lane = lax.broadcasted_iota(jnp.int32, (GROUPS, CH), 1)
    wide = hdot(sums[:, 2 * GROUPS : 3 * GROUPS], (fold_lane % GROUPS == fold_at).astype(F32))
    row = lax.broadcasted_iota(jnp.int32, (FR, CH), 0)
    lane = lax.broadcasted_iota(jnp.int32, (FR, CH), 1)
    gain = jnp.sum(jnp.where(lane // GROUPS == row, wide, 0.0), axis=0, keepdims=True)
    out_ref[...] = total[:PROWS]
    out_ref[4 * TAPS : 4 * TAPS + 1] = gain


def forward_conv(x_ref, hp_ref, hn_ref, mean_ref, inv_ref, gain_ref, k_ref, live_ref, out_ref, pad_ref, held):
    s_at = (lax.axis_index("y") * NZ + lax.axis_index("z")) * NC + lax.axis_index("c")
    before, after = outside(hp_ref, hn_ref)
    rows = [before, x_ref[:, 0], x_ref[:, 1], after]
    mean = mean_ref[...][:, None, :]
    inv = inv_ref[...][:, None, :]
    gain = gain_ref[...][None]
    for r in range(4):
        gated = (rows[r].astype(F32) - mean) * inv * gain
        act = gated * jax.nn.sigmoid(gated)
        if r == 0:
            act = jnp.where(s_at == 0, 0.0, act)
        if r == 3:
            act = jnp.where(s_at == SPACE - 1, 0.0, act)
        for k in range(3):
            pad_ref[k, 2:, r] = shifted(act, k).astype(BF16)
    pad_ref[:, :2] = jnp.zeros((3, 2, 4, COLS, CH), BF16)
    held.wait()
    total = jnp.zeros((FR * CELLS, CH), F32)
    for i in range(3):
        for j in range(3):
            for k in range(3):
                window = pad_ref[k, i : i + FR, j : j + 2]
                total = total + jnp.dot(
                    window.reshape(FR * CELLS, CH),
                    k_ref[(i * 3 + j) * 3 + k],
                    preferred_element_type=F32,
                )
    cells = total.reshape(FR, CELLS, CH) + x_ref[...].astype(F32).reshape(FR, CELLS, CH)
    cells = cells * live_ref[...][:, None, :]
    out_ref[...] = cells.astype(BF16).reshape(FR, ROWS, COLS, CH)


def finish_input(sums_ref, sc_ref, x_ref, g_ref, mean_ref, inv_ref, live_ref, out_ref):
    sums = sums_ref[...]
    spread = spread_matrix()
    first = hdot(sums[:, :GROUPS] / COUNT, spread)[:, None, :]
    second = hdot(sums[:, GROUPS : 2 * GROUPS] / COUNT, spread)[:, None, :]
    inv = inv_ref[...][:, None, :]
    xf = x_ref[...].astype(F32).reshape(FR, CELLS, CH)
    normalized = (xf - mean_ref[...][:, None, :]) * inv
    norm_grad = inv * (sc_ref[...] - first - normalized * second)
    grad = g_ref[...].astype(F32).reshape(FR, CELLS, CH) * live_ref[...][:, None, :]
    out_ref[...] = (grad + norm_grad).astype(BF16).reshape(FR, ROWS, COLS, CH)


def sum_clips(own_h, one_h, two_h, three_h, kg_h, gain_h, in_ref, kg_ref, gain_ref, sem):
    x_at = lax.axis_index("x")
    copies = []
    for d, src in enumerate((own_h, one_h, two_h, three_h)):
        copies.append(
            pltpu.make_async_copy(src, in_ref.at[lax.rem(x_at + NX - d, NX)], sem.at[d])
        )
    for copy in copies:
        copy.start()
    for copy in copies:
        copy.wait()
    total = ((in_ref[0] + in_ref[1]) + in_ref[2]) + in_ref[3]
    for tap in range(TAPS):
        kg_ref[tap] = total[4 * tap : 4 * tap + 4]
    gain_ref[...] = total[4 * TAPS : 4 * TAPS + 1]
    out = (
        pltpu.make_async_copy(kg_ref, kg_h, sem.at[4]),
        pltpu.make_async_copy(gain_ref, gain_h, sem.at[5]),
    )
    for copy in out:
        copy.start()
    for copy in out:
        copy.wait()


HBM = pl.BlockSpec(memory_space=pltpu.HBM)
SMEM = pl.BlockSpec(memory_space=pltpu.SMEM)


def stay_out(array):
    return pltpu.with_memory_space_constraint(array, pltpu.HBM)


def shapes(outs):
    return tuple(jax.ShapeDtypeStruct(s, d) for s, d in outs)


def call(body, outs, args, specs, scratch, flops=0, limit=32, aliases={}):
    return pl.pallas_call(
        body,
        out_shape=shapes(outs),
        in_specs=specs,
        out_specs=tuple(HBM for _ in outs),
        scratch_shapes=list(scratch),
        input_output_aliases=aliases,
        compiler_params=pltpu.CompilerParams(vmem_limit_bytes=limit * 2**20),
        cost_estimate=pl.CostEstimate(flops=flops, bytes_accessed=2**20, transcendentals=0),
        name=body.__name__,
    )(*args)


def run(body, outs, args, scratch=(), late=None, smem=(), flops=0, rows={}):
    count, outputs = len(args), len(outs)
    moved = [at for at in range(count) if at not in smem]

    def kernel(*refs):
        ins, targets = list(refs[:count]), refs[count : count + outputs]
        rest = refs[count + outputs :]
        buffers, rest = rest[: len(moved)], rest[len(moved) :]
        results, rest = rest[:outputs], rest[outputs:]
        sem, extra = rest[0], rest[1:]
        copies = [
            pltpu.make_async_copy(
                ins[at].at[rows[at][0] : rows[at][1]] if at in rows else ins[at], buffers[n], sem.at[n]
            )
            for n, at in enumerate(moved)
        ]
        for copy in copies:
            copy.start()
        for n, at in enumerate(moved):
            ins[at] = buffers[n]
        held = copies.pop(moved.index(late)) if late is not None else None
        for copy in copies:
            copy.wait()
        if held is None:
            body(*ins, *results, *extra)
        else:
            body(*ins, *results, *extra, held)
        copies = [
            pltpu.make_async_copy(results[n], targets[n], sem.at[len(moved) + n])
            for n in range(outputs)
        ]
        for copy in copies:
            copy.start()
        for copy in copies:
            copy.wait()

    kernel.__name__ = body.__name__
    specs = [SMEM if at in smem else HBM for at in range(count)]
    buffers = []
    for at in moved:
        shape = args[at].shape
        if at in rows:
            shape = (rows[at][1] - rows[at][0],) + shape[1:]
        buffers.append(pltpu.VMEM(shape, args[at].dtype))
    buffers += [pltpu.VMEM(s, d) for s, d in outs]
    buffers += [pltpu.SemaphoreType.DMA((len(moved) + outputs,))]
    return call(kernel, outs, args, specs, buffers + list(scratch), flops)


def pack_body(*refs):
    sources, outs = refs[:4], refs[4:8]
    x_ref, g_ref, hp_ref, hn_ref, buf, sem = refs[8:]
    sources = (sources[0], sources[1], sources[2].at[:HALO], sources[3].at[:HALO])
    pairs = tuple(zip(sources, (x_ref, g_ref, hp_ref, hn_ref)))
    copies = [pltpu.make_async_copy(a, b, sem.at[n]) for n, (a, b) in enumerate(pairs)]
    for copy in copies:
        copy.start()
    for copy in copies:
        copy.wait()
    pack_slices(x_ref, g_ref, hp_ref, hn_ref, buf)
    y_at = lax.axis_index("y")
    copies = [
        pltpu.make_async_copy(buf.at[lax.rem(y_at + d, NY)], out, sem.at[4 + d])
        for d, out in enumerate(outs)
    ]
    for copy in copies:
        copy.start()
    for copy in copies:
        copy.wait()


def local(video_latent, frame_counts, conv_kernel, norm_gain, output_grad):
    x = stay_out(video_latent.reshape(FR, ROWS, COLS, CH))
    g = stay_out(output_grad.reshape(FR, ROWS, COLS, CH))
    gain = stay_out(norm_gain.reshape(1, CH))
    conv_kernel = stay_out(conv_kernel)
    space = ("y", "z", "c")
    cells = (FR, ROWS, COLS, CH)
    wide = (FR, CH)
    swap = [(0, 1), (1, 0)]
    dma = pltpu.SemaphoreType.DMA

    inner, outer, stats = run(
        edges_and_sums,
        [
            ((2 * HALO + TERMS, CH), BF16),
            ((2 * HALO, CH), BF16),
            ((FR, 128), F32),
        ],
        (x, g),
    )
    stats, counts = lax.optimization_barrier((stats, frame_counts))
    live = jnp.broadcast_to(jnp.arange(FR)[:, None] < counts[0], wide).astype(F32)
    hp = lax.ppermute(inner, "c", swap)
    hn = lax.ppermute(
        outer,
        space,
        [(i, i - 1 if i % 2 == 0 else i + 1) for i in range(1, SPACE - 1)],
    )
    (stats,) = run(
        pair_sums,
        [((NY * NZ, FR, 128), F32)],
        (stats, hp),
        rows={1: (2 * HALO, 2 * HALO + TERMS)},
    )
    stats = lax.all_to_all(stats, ("y", "z"), 0, 0)
    block = (BLOCK, BSL)
    packed = call(
        pack_body,
        [(block, BF16)] * NY,
        (x, g, hp, hn),
        [HBM] * 4,
        [pltpu.VMEM(cells, BF16)] * 2
        + [pltpu.VMEM((HALO, CH), BF16)] * 2
        + [pltpu.VMEM((NY,) + block, BF16), dma((8,))],
    )
    near = [packed[0]] + [
        lax.ppermute(packed[d], "y", [(i, (i + d) % NY) for i in range(NY)]) for d in range(1, NY)
    ]
    conv_flops = 16 * TAPS * FR * CELLS * CH * CH
    padded = pltpu.VMEM((3, FR + 2, 4, COLS, CH), BF16)
    terms, scaled, mean, inv = run(
        backward_terms,
        [((NY * NC, FR, 128), F32), ((FR, CELLS, CH), F32), (wide, F32), (wide, F32)],
        (g, hp, hn, conv_kernel, live, stats, x, gain),
        rows={1: (HALO, 2 * HALO), 2: (HALO, 2 * HALO)},
        scratch=[padded],
        late=3,
    )
    *near, terms = lax.optimization_barrier((*near, terms))
    terms = lax.all_to_all(terms, ("y", "c"), 0, 0)
    far = [lax.ppermute(a, "c", swap) for a in near]
    part = (NZ, PROWS, CH)
    whole_part = (NZ, PROWS + TERMS, CH)
    (partial,) = call(
        kernel_part,
        [(whole_part, BF16)],
        (*near, *far, mean, inv, gain, live),
        [HBM] * 12,
        [
            pltpu.VMEM((8, BLOCK, BSL), BF16),
            pltpu.VMEM(wide, F32),
            pltpu.VMEM(wide, F32),
            pltpu.VMEM((1, CH), F32),
            pltpu.VMEM(wide, F32),
            pltpu.VMEM(part, BF16),
            pltpu.VMEM((3, FR, NY, 6, COLS, Q * APART), BF16),
            pltpu.VMEM((FR, NY, 4, COLS, CH), BF16),
            pltpu.VMEM(part, F32),
            dma((12,)),
        ],
        flops=conv_flops,
    )
    (merged,) = call(
        add_sums,
        [(whole_part, BF16)],
        (partial, terms),
        [HBM] * 2,
        [pltpu.VMEM((NY * NC, FR, 128), F32), pltpu.VMEM((NZ, TERMS, CH), BF16), dma((2,))],
        aliases={0: 0},
    )
    merged, late_mean = lax.optimization_barrier((merged, mean))
    merged = lax.all_to_all(merged, "z", 0, 0)
    (block_output,) = run(
        forward_conv,
        [(cells, BF16)],
        (x, hp, hn, late_mean, inv, gain, conv_kernel, live),
        rows={1: (0, HALO), 2: (0, HALO)},
        scratch=[padded],
        late=6,
        flops=conv_flops,
    )
    merged, block_output = lax.optimization_barrier((merged, block_output))
    rows, sums = run(sum_rows, [((PROWS, CH), F32), ((FR, 128), F32)], (merged,))
    others = [rows] + [
        lax.ppermute(rows, "x", [(i, (i + d) % NX) for i in range(NX)]) for d in range(1, NX)
    ]
    (input_grad,) = run(
        finish_input, [(cells, BF16)], (sums, scaled, x, g, mean, inv, live)
    )
    kernel_grad, gain_grad = call(
        sum_clips,
        [((TAPS, 4, CH), F32), ((1, CH), F32)],
        others,
        [HBM] * 4,
        [
            pltpu.VMEM((NX, PROWS, CH), F32),
            pltpu.VMEM((TAPS, 4, CH), F32),
            pltpu.VMEM((1, CH), F32),
            dma((6,)),
        ],
    )
    whole = (1,) + cells
    return (
        block_output.reshape(whole),
        input_grad.reshape(whole),
        jnp.swapaxes(kernel_grad, 0, 1),
        gain_grad.reshape(CH),
    )


def solution(mesh):
    fine = Mesh(mesh.devices.reshape(NX, NY, NZ, NC), ("x", "y", "z", "c"))
    space = ("y", "z", "c")
    cells = P("x", None, space, None, None)
    return jax.shard_map(
        local,
        mesh=fine,
        in_specs=(cells, P("x"), P(), P(), cells),
        out_specs=(cells, cells, P(space, None, None), P()),
        check_vma=False,
    )
```

```python
import jax
import jax.numpy as jnp
from jax import lax
from jax.experimental import pallas as pl
from jax.experimental.pallas import tpu as pltpu
from jax.sharding import Mesh
from jax.sharding import PartitionSpec as P

F32 = jnp.float32
BF16 = jnp.bfloat16
NX, NY, NZ, NC = 4, 4, 8, 2
SPACE = NY * NZ * NC
FR, ROWS, COLS, CH = 8, 2, 16, 256
CELLS = ROWS * COLS
GROUPS = 32
GC = CH // GROUPS
ASL = CH // NY
BSL = CH // NC
EPSILON = 1e-05
COUNT = CELLS * SPACE * GC
AROWS = FR // 2 * 3 * COLS
GROWS = FR * ROWS * COLS
TAPS = 27
PROWS = 112
Q = 4
APART = ASL // NC
BLOCK = AROWS + NC * GROWS
TERMS = 16
HALO = FR * COLS
HI = lax.Precision.HIGHEST


def hdot(a, b):
    return jnp.dot(a, b, preferred_element_type=F32, precision=HI)


def gather_matrix():
    lane = lax.broadcasted_iota(jnp.int32, (CH, GROUPS), 0)
    group = lax.broadcasted_iota(jnp.int32, (CH, GROUPS), 1)
    return (lane // GC == group).astype(F32)


def spread_matrix():
    group = lax.broadcasted_iota(jnp.int32, (GROUPS, CH), 0)
    lane = lax.broadcasted_iota(jnp.int32, (GROUPS, CH), 1)
    return (lane // GC == group).astype(F32)


def shifted(cells, k):
    if k == 1:
        return cells
    zero = jnp.zeros(cells.shape[:-2] + (1, cells.shape[-1]), cells.dtype)
    if k == 0:
        return jnp.concatenate([zero, cells[..., :-1, :]], axis=-2)
    return jnp.concatenate([cells[..., 1:, :], zero], axis=-2)


def edges_and_sums(x_ref, g_ref, in_ref, out_ref, st_ref):
    first = lax.axis_index("c") == 0
    for n, ref in enumerate((x_ref, g_ref)):
        low, high = ref[:, 0], ref[:, 1]
        inner, outer = jnp.where(first, high, low), jnp.where(first, low, high)
        in_ref[n * HALO : (n + 1) * HALO] = inner.reshape(HALO, CH)
        out_ref[n * HALO : (n + 1) * HALO] = outer.reshape(HALO, CH)
    xf = x_ref[...].astype(F32).reshape(FR, CELLS, CH)
    gather = gather_matrix()
    mean = hdot(jnp.sum(xf, axis=1), gather) / (CELLS * GC)
    centered = xf - hdot(mean, spread_matrix())[:, None, :]
    squares = hdot(jnp.sum(centered * centered, axis=1), gather)
    sums = jnp.concatenate([mean, squares, jnp.zeros((FR, 2 * GROUPS), F32)], axis=1)
    st_ref[...] = sums
    in_ref[2 * HALO :] = as_terms(sums)


def outside(in_ref, out_ref):
    first = lax.axis_index("c") == 0
    inner = in_ref[...].reshape(FR, COLS, CH)
    outer = out_ref[...].reshape(FR, COLS, CH)
    return jnp.where(first, outer, inner), jnp.where(first, inner, outer)


def combined(parts, squares, each):
    count = parts.shape[0]
    mean = jnp.sum(parts, axis=0) / count
    apart = parts - mean[None]
    return mean, jnp.sum(squares + each * (apart * apart), axis=0)


def pair_sums(own_ref, other_ref, out_ref):
    both = jnp.stack([own_ref[...], from_terms(other_ref[...].astype(F32))])
    mean, squares = combined(both[:, :, :GROUPS], both[:, :, GROUPS : 2 * GROUPS], CELLS * GC)
    row = jnp.concatenate([mean, squares, jnp.zeros((FR, 2 * GROUPS), F32)], axis=1)
    out_ref[...] = jnp.broadcast_to(row[None], (NY * NZ, FR, 128))


def as_terms(values):
    high = values.astype(BF16).astype(F32)
    middle = (values - high).astype(BF16).astype(F32)
    low = values - high - middle
    upper = jnp.concatenate([high, middle], axis=1)
    lower = jnp.concatenate([low, jnp.zeros((FR, 128), F32)], axis=1)
    return jnp.concatenate([upper, lower], axis=0).astype(BF16)


def from_terms(terms):
    return (terms[FR:, :128] + terms[:FR, 128:]) + terms[:FR, :128]


def pack_slices(x_ref, hp_ref, hn_ref, out_ref):
    upper = lax.axis_index("c") == 0
    own = [x_ref[:, 0], x_ref[:, 1]]
    before, after = outside(hp_ref, hn_ref)
    rows = [
        jnp.where(upper, before, own[0]),
        jnp.where(upper, own[0], own[1]),
        jnp.where(upper, own[1], after),
    ]
    three = jnp.stack(rows, axis=1).reshape(FR // 2, 2, 3, COLS, CH)
    for y in range(NY):
        part = three[..., y * ASL : (y + 1) * ASL]
        pair = jnp.concatenate([part[:, 0], part[:, 1]], axis=-1)
        out_ref[y] = pair.reshape(AROWS, 2 * ASL)


def backward_conv(g_ref, hp_ref, hn_ref, k_ref, live_ref, pad_ref, held):
    live = live_ref[...][:, None, :]
    before, after = outside(hp_ref, hn_ref)
    rows = [before, g_ref[:, 0], g_ref[:, 1], after]
    for r in range(4):
        cells = rows[r].astype(F32) * live
        for k in range(3):
            pad_ref[k, :FR, r] = shifted(cells, k).astype(BF16)
    pad_ref[:, FR:] = jnp.zeros((3, 2, 4, COLS, CH), BF16)
    held.wait()
    total = jnp.zeros((FR * CELLS, CH), F32)
    for i in range(3):
        for j in range(3):
            for k in range(3):
                window = pad_ref[2 - k, 2 - i : 2 - i + FR, 2 - j : 4 - j]
                total = total + lax.dot_general(
                    window.reshape(FR * CELLS, CH),
                    k_ref[(i * 3 + j) * 3 + k],
                    (((1,), (1,)), ((), ())),
                    preferred_element_type=F32,
                )
    return total


def backward_terms(
    g_ref, hp_ref, hn_ref, k_ref, live_ref, st_ref, x_ref, gain_ref,
    out_ref, sc_ref, mean_ref, inv_ref, pad_ref, held,
):
    act_grad = backward_conv(g_ref, hp_ref, hn_ref, k_ref, live_ref, pad_ref, held)
    mean, whole = combined(
        st_ref[:, :FR, :GROUPS], st_ref[:, :FR, GROUPS : 2 * GROUPS], NC * CELLS * GC
    )
    spread = spread_matrix()
    mean_all = hdot(mean, spread)
    inv_all = hdot(lax.rsqrt(whole / COUNT + EPSILON), spread)
    mean_ref[...] = mean_all
    inv_ref[...] = inv_all
    gain = gain_ref[...][None]
    xf = x_ref[...].astype(F32).reshape(FR, CELLS, CH)
    normalized = (xf - mean_all[:, None, :]) * inv_all[:, None, :]
    gated = normalized * gain
    sig = jax.nn.sigmoid(gated)
    pre = act_grad.reshape(FR, CELLS, CH) * sig * (1.0 + gated * (1.0 - sig))
    scaled = pre * gain
    sc_ref[...] = scaled
    gather = gather_matrix()
    first = hdot(jnp.sum(scaled, axis=1), gather)
    by_channel = jnp.sum(pre * normalized, axis=1)
    second = hdot(by_channel * gain_ref[...], gather)
    gain_part = jnp.sum(by_channel, axis=0, keepdims=True)
    row = lax.broadcasted_iota(jnp.int32, (FR, CH), 0)
    lane = lax.broadcasted_iota(jnp.int32, (FR, CH), 1)
    folded = jnp.where(lane // GROUPS == row, jnp.broadcast_to(gain_part, (FR, CH)), 0.0)
    fold_lane = lax.broadcasted_iota(jnp.int32, (CH, GROUPS), 0)
    fold_at = lax.broadcasted_iota(jnp.int32, (CH, GROUPS), 1)
    folded = hdot(folded, (fold_lane % GROUPS == fold_at).astype(F32))
    everything = jnp.concatenate([first, second, folded, jnp.zeros((FR, GROUPS), F32)], axis=1)
    out_ref[...] = jnp.broadcast_to(everything[None], (NY * NC, FR, 128))


def kernel_part(*refs):
    blocks, (mean_h, inv_h, gain_h, live_h, out_h) = refs[:8], refs[8:13]
    in_ref, mean_ref, inv_ref, gain_ref, live_ref, out_ref, pad_ref, grad_ref, sum_ref, sem = refs[13:]
    y_at, z_at, c_at = lax.axis_index("y"), lax.axis_index("z"), lax.axis_index("c")
    pairs = [(blocks[n], in_ref.at[n]) for n in range(8)]
    pairs += [(mean_h, mean_ref), (inv_h, inv_ref), (gain_h, gain_ref), (live_h, live_ref)]
    copies = [pltpu.make_async_copy(a, b, sem.at[n]) for n, (a, b) in enumerate(pairs)]
    for copy in copies:
        copy.start()
    for copy in copies[8:]:
        copy.wait()
    width = Q * APART
    lane = lax.broadcasted_iota(jnp.int32, (CH, width), 0)
    slot = lax.broadcasted_iota(jnp.int32, (CH, width), 1)
    channel = GC * ((slot % APART) // 4) + 4 * c_at + slot % 4
    pick = (lane == y_at * ASL + channel).astype(F32)
    mean2 = hdot(mean_ref[...], pick)
    inv2 = hdot(inv_ref[...], pick)
    gain2 = hdot(gain_ref[...], pick)
    live = live_ref[:, :BSL].astype(BF16)[:, None, None, :]
    quarter = lax.broadcasted_iota(jnp.int32, (1, width), 1) // APART
    centers, scales = [], []
    for u in range(2):
        center, scale = mean2[4 * u : 4 * u + 1], inv2[4 * u : 4 * u + 1]
        for q in range(1, Q):
            center = jnp.where(quarter == q, mean2[4 * u + q : 4 * u + q + 1], center)
            scale = jnp.where(quarter == q, inv2[4 * u + q : 4 * u + q + 1], scale)
        centers.append(center)
        scales.append(scale * gain2)
    lane = lax.broadcasted_iota(jnp.int32, (2 * ASL, width), 0)
    slot = lax.broadcasted_iota(jnp.int32, (2 * ASL, width), 1)
    channel = GC * ((slot % APART) // 4) + 4 * c_at + slot % 4
    chosen = [
        (lane == (slot // APART - 2 * half) * ASL + channel).astype(BF16) for half in range(2)
    ]
    shape = (3, COLS, width)
    place = lax.broadcasted_iota(jnp.int32, shape, 2) // APART
    row = lax.broadcasted_iota(jnp.int32, shape, 0)
    block = 3 * COLS
    for copy in copies[:8]:
        copy.wait()
    for n in range(8):
        d = n % 4
        y = lax.rem(y_at + NY - d, NY)
        c = c_at if n < 4 else 1 - c_at
        top = (y == 0) & (z_at == 0) & (c == 0)
        bottom = (y == NY - 1) & (z_at == NZ - 1) & (c == NC - 1)
        edge = jnp.where(top, 0, jnp.where(bottom, 2, 3))
        inside = (row != edge).astype(F32)
        acts = []
        for u in range(2):
            at = 2 * u * block
            raw = jnp.dot(
                in_ref[n, at : at + block], chosen[0], preferred_element_type=F32
            ) + jnp.dot(
                in_ref[n, at + block : at + 2 * block], chosen[1], preferred_element_type=F32
            )
            gated = (raw - centers[u]) * scales[u]
            acts.append((gated * jax.nn.sigmoid(gated)).reshape(shape) * inside)
        a, b = acts
        a1, a2, b1 = pltpu.roll(a, 32, 2), pltpu.roll(a, 64, 2), pltpu.roll(b, 32, 2)
        b2 = pltpu.roll(b, 64, 2)
        frames = [
            jnp.where(place < 2, 0.0, a2),
            jnp.where(place < 1, 0.0, a1),
            a,
            pltpu.roll(a, 96, 2),
            jnp.where(place < 2, a2, b2),
            jnp.where(place < 1, a1, b1),
            b,
            pltpu.roll(b, 96, 2),
        ]
        for f in range(FR):
            for k in range(3):
                pad_ref[k, f, d, pl.ds(3 * c, 3)] = shifted(frames[f], k).astype(BF16)
        for h in range(NC):
            at = AROWS + h * GROWS
            cells = in_ref[n, at : at + GROWS].reshape(FR, ROWS, COLS, BSL) * live
            grad_ref[:, d, pl.ds(2 * c, 2), :, h * BSL : (h + 1) * BSL] = cells
    cells = FR * NY * 4 * COLS
    turned_grad = grad_ref[...].reshape(cells, CH).T
    sum_ref[:, 4 * TAPS :] = jnp.zeros((NZ, PROWS - 4 * TAPS, CH), F32)
    combos = [(j, k) for j in range(3) for k in range(3)]
    for first in range(0, 9, 2):
        group = combos[first : first + 2]
        windows = [pad_ref[k, :, :, j : j + 4].reshape(cells, width) for j, k in group]
        window = windows[0] if len(windows) == 1 else jnp.concatenate(windows, axis=1)
        product = jnp.dot(turned_grad, window, preferred_element_type=F32)
        product = product.astype(BF16).T.astype(F32)
        for n, (j, k) in enumerate(group):
            for i in range(3):
                tap = (i * 3 + j) * 3 + k
                at = n * width + i * APART
                piece = product[at : at + APART].reshape(NZ, 4, CH)
                sum_ref[:, tap * 4 : tap * 4 + 4] = piece
    out_ref[...] = sum_ref[...].astype(BF16)
    copy = pltpu.make_async_copy(out_ref, out_h.at[:, :PROWS], sem.at[0])
    copy.start()
    copy.wait()


def add_sums(part_h, b_h, out_h, b_ref, out_ref, sem):
    copy = pltpu.make_async_copy(b_h, b_ref, sem.at[0])
    copy.start()
    copy.wait()
    terms = as_terms(jnp.sum(b_ref[...], axis=0))
    out_ref[...] = jnp.broadcast_to(terms[None], (NZ, TERMS, CH))
    copy = pltpu.make_async_copy(out_ref, out_h.at[:, PROWS:], sem.at[1])
    copy.start()
    copy.wait()


def sum_rows(in_ref, out_ref, sums_ref):
    total = jnp.sum(in_ref[...].astype(F32), axis=0)
    sums = from_terms(total[PROWS:])
    sums_ref[...] = sums
    fold_at = lax.broadcasted_iota(jnp.int32, (GROUPS, CH), 0)
    fold_lane = lax.broadcasted_iota(jnp.int32, (GROUPS, CH), 1)
    wide = hdot(sums[:, 2 * GROUPS : 3 * GROUPS], (fold_lane % GROUPS == fold_at).astype(F32))
    row = lax.broadcasted_iota(jnp.int32, (FR, CH), 0)
    lane = lax.broadcasted_iota(jnp.int32, (FR, CH), 1)
    gain = jnp.sum(jnp.where(lane // GROUPS == row, wide, 0.0), axis=0, keepdims=True)
    out_ref[...] = total[:PROWS]
    out_ref[4 * TAPS : 4 * TAPS + 1] = gain


def forward_conv(x_ref, hp_ref, hn_ref, mean_ref, inv_ref, gain_ref, k_ref, live_ref, out_ref, pad_ref, held):
    s_at = (lax.axis_index("y") * NZ + lax.axis_index("z")) * NC + lax.axis_index("c")
    before, after = outside(hp_ref, hn_ref)
    rows = [before, x_ref[:, 0], x_ref[:, 1], after]
    mean = mean_ref[...][:, None, :]
    inv = inv_ref[...][:, None, :]
    gain = gain_ref[...][None]
    for r in range(4):
        gated = (rows[r].astype(F32) - mean) * inv * gain
        act = gated * jax.nn.sigmoid(gated)
        if r == 0:
            act = jnp.where(s_at == 0, 0.0, act)
        if r == 3:
            act = jnp.where(s_at == SPACE - 1, 0.0, act)
        for k in range(3):
            pad_ref[k, 2:, r] = shifted(act, k).astype(BF16)
    pad_ref[:, :2] = jnp.zeros((3, 2, 4, COLS, CH), BF16)
    held.wait()
    total = jnp.zeros((FR * CELLS, CH), F32)
    for i in range(3):
        for j in range(3):
            for k in range(3):
                window = pad_ref[k, i : i + FR, j : j + 2]
                total = total + jnp.dot(
                    window.reshape(FR * CELLS, CH),
                    k_ref[(i * 3 + j) * 3 + k],
                    preferred_element_type=F32,
                )
    cells = total.reshape(FR, CELLS, CH) + x_ref[...].astype(F32).reshape(FR, CELLS, CH)
    cells = cells * live_ref[...][:, None, :]
    out_ref[...] = cells.astype(BF16).reshape(FR, ROWS, COLS, CH)


def finish_input(sums_ref, sc_ref, x_ref, g_ref, mean_ref, inv_ref, live_ref, out_ref):
    sums = sums_ref[...]
    spread = spread_matrix()
    first = hdot(sums[:, :GROUPS] / COUNT, spread)[:, None, :]
    second = hdot(sums[:, GROUPS : 2 * GROUPS] / COUNT, spread)[:, None, :]
    inv = inv_ref[...][:, None, :]
    xf = x_ref[...].astype(F32).reshape(FR, CELLS, CH)
    normalized = (xf - mean_ref[...][:, None, :]) * inv
    norm_grad = inv * (sc_ref[...] - first - normalized * second)
    grad = g_ref[...].astype(F32).reshape(FR, CELLS, CH) * live_ref[...][:, None, :]
    out_ref[...] = (grad + norm_grad).astype(BF16).reshape(FR, ROWS, COLS, CH)


def sum_clips(own_h, one_h, two_h, three_h, kg_h, gain_h, in_ref, kg_ref, gain_ref, sem):
    x_at = lax.axis_index("x")
    copies = []
    for d, src in enumerate((own_h, one_h, two_h, three_h)):
        copies.append(
            pltpu.make_async_copy(src, in_ref.at[lax.rem(x_at + NX - d, NX)], sem.at[d])
        )
    for copy in copies:
        copy.start()
    for copy in copies:
        copy.wait()
    total = ((in_ref[0] + in_ref[1]) + in_ref[2]) + in_ref[3]
    for tap in range(TAPS):
        kg_ref[tap] = total[4 * tap : 4 * tap + 4]
    gain_ref[...] = total[4 * TAPS : 4 * TAPS + 1]
    out = (
        pltpu.make_async_copy(kg_ref, kg_h, sem.at[4]),
        pltpu.make_async_copy(gain_ref, gain_h, sem.at[5]),
    )
    for copy in out:
        copy.start()
    for copy in out:
        copy.wait()


HBM = pl.BlockSpec(memory_space=pltpu.HBM)
SMEM = pl.BlockSpec(memory_space=pltpu.SMEM)


def stay_out(array):
    return pltpu.with_memory_space_constraint(array, pltpu.HBM)


def shapes(outs):
    return tuple(jax.ShapeDtypeStruct(s, d) for s, d in outs)


def call(body, outs, args, specs, scratch, flops=0, limit=32, aliases={}):
    return pl.pallas_call(
        body,
        out_shape=shapes(outs),
        in_specs=specs,
        out_specs=tuple(HBM for _ in outs),
        scratch_shapes=list(scratch),
        input_output_aliases=aliases,
        compiler_params=pltpu.CompilerParams(vmem_limit_bytes=limit * 2**20),
        cost_estimate=pl.CostEstimate(flops=flops, bytes_accessed=2**20, transcendentals=0),
        name=body.__name__,
    )(*args)


def run(body, outs, args, scratch=(), late=None, smem=(), flops=0, rows={}):
    count, outputs = len(args), len(outs)
    moved = [at for at in range(count) if at not in smem]

    def kernel(*refs):
        ins, targets = list(refs[:count]), refs[count : count + outputs]
        rest = refs[count + outputs :]
        buffers, rest = rest[: len(moved)], rest[len(moved) :]
        results, rest = rest[:outputs], rest[outputs:]
        sem, extra = rest[0], rest[1:]
        copies = [
            pltpu.make_async_copy(
                ins[at].at[rows[at][0] : rows[at][1]] if at in rows else ins[at], buffers[n], sem.at[n]
            )
            for n, at in enumerate(moved)
        ]
        held = copies.pop(moved.index(late)) if late is not None else None
        for copy in copies + ([held] if held is not None else []):
            copy.start()
        for n, at in enumerate(moved):
            ins[at] = buffers[n]
        for copy in copies:
            copy.wait()
        if held is None:
            body(*ins, *results, *extra)
        else:
            body(*ins, *results, *extra, held)
        copies = [
            pltpu.make_async_copy(results[n], targets[n], sem.at[len(moved) + n])
            for n in range(outputs)
        ]
        for copy in copies:
            copy.start()
        for copy in copies:
            copy.wait()

    kernel.__name__ = body.__name__
    specs = [SMEM if at in smem else HBM for at in range(count)]
    buffers = []
    for at in moved:
        shape = args[at].shape
        if at in rows:
            shape = (rows[at][1] - rows[at][0],) + shape[1:]
        buffers.append(pltpu.VMEM(shape, args[at].dtype))
    buffers += [pltpu.VMEM(s, d) for s, d in outs]
    buffers += [pltpu.SemaphoreType.DMA((len(moved) + outputs,))]
    return call(kernel, outs, args, specs, buffers + list(scratch), flops)


def pack_body(x_h, g_h, hp_h, hn_h, *refs):
    outs = refs[:NY]
    x_ref, hp_ref, hn_ref, buf, sem = refs[NY:]
    pairs = ((x_h, x_ref), (hp_h.at[:HALO], hp_ref), (hn_h.at[:HALO], hn_ref))
    copies = [pltpu.make_async_copy(a, b, sem.at[n]) for n, (a, b) in enumerate(pairs)]
    for copy in copies:
        copy.start()
    straight = []
    for d, out in enumerate(outs):
        for c in range(NC):
            at = AROWS + c * GROWS
            straight.append(
                pltpu.make_async_copy(
                    g_h.at[:, c * BSL : (c + 1) * BSL],
                    out.at[at : at + GROWS],
                    sem.at[3 + NC * d + c],
                )
            )
    for copy in straight:
        copy.start()
    for copy in copies:
        copy.wait()
    pack_slices(x_ref, hp_ref, hn_ref, buf)
    y_at = lax.axis_index("y")
    copies = [
        pltpu.make_async_copy(
            buf.at[lax.rem(y_at + d, NY)], out.at[:AROWS], sem.at[3 + NC * NY + d]
        )
        for d, out in enumerate(outs)
    ]
    for copy in copies:
        copy.start()
    for copy in straight + copies:
        copy.wait()


def local(video_latent, frame_counts, conv_kernel, norm_gain, output_grad):
    x = stay_out(video_latent.reshape(FR, ROWS, COLS, CH))
    g = stay_out(output_grad.reshape(FR, ROWS, COLS, CH))
    gain = stay_out(norm_gain.reshape(1, CH))
    conv_kernel = stay_out(conv_kernel)
    space = ("y", "z", "c")
    cells = (FR, ROWS, COLS, CH)
    wide = (FR, CH)
    swap = [(0, 1), (1, 0)]
    dma = pltpu.SemaphoreType.DMA

    inner, outer, stats = run(
        edges_and_sums,
        [
            ((2 * HALO + TERMS, CH), BF16),
            ((2 * HALO, CH), BF16),
            ((FR, 128), F32),
        ],
        (x, g),
    )
    stats, counts = lax.optimization_barrier((stats, frame_counts))
    live = jnp.broadcast_to(jnp.arange(FR)[:, None] < counts[0], wide).astype(F32)
    hp = lax.ppermute(inner, "c", swap)
    hn = lax.ppermute(
        outer,
        space,
        [(i, i - 1 if i % 2 == 0 else i + 1) for i in range(1, SPACE - 1)],
    )
    (stats,) = run(
        pair_sums,
        [((NY * NZ, FR, 128), F32)],
        (stats, hp),
        rows={1: (2 * HALO, 2 * HALO + TERMS)},
    )
    stats = lax.all_to_all(stats, ("y", "z"), 0, 0)
    block = (BLOCK, BSL)
    packed = call(
        pack_body,
        [(block, BF16)] * NY,
        (x, stay_out(output_grad.reshape(GROWS, CH)), hp, hn),
        [HBM] * 4,
        [pltpu.VMEM(cells, BF16)]
        + [pltpu.VMEM((HALO, CH), BF16)] * 2
        + [pltpu.VMEM((NY, AROWS, BSL), BF16), dma((3 + NC * NY + NY,))],
    )
    near = [packed[0]] + [
        lax.ppermute(packed[d], "y", [(i, (i + d) % NY) for i in range(NY)]) for d in range(1, NY)
    ]
    conv_flops = 16 * TAPS * FR * CELLS * CH * CH
    padded = pltpu.VMEM((3, FR + 2, 4, COLS, CH), BF16)
    terms, scaled, mean, inv = run(
        backward_terms,
        [((NY * NC, FR, 128), F32), ((FR, CELLS, CH), F32), (wide, F32), (wide, F32)],
        (g, hp, hn, conv_kernel, live, stats, x, gain),
        rows={1: (HALO, 2 * HALO), 2: (HALO, 2 * HALO)},
        scratch=[padded],
        late=3,
    )
    *near, terms = lax.optimization_barrier((*near, terms))
    terms = lax.all_to_all(terms, ("y", "c"), 0, 0)
    far = [lax.ppermute(a, "c", swap) for a in near]
    part = (NZ, PROWS, CH)
    whole_part = (NZ, PROWS + TERMS, CH)
    (partial,) = call(
        kernel_part,
        [(whole_part, BF16)],
        (*near, *far, mean, inv, gain, live),
        [HBM] * 12,
        [
            pltpu.VMEM((8, BLOCK, BSL), BF16),
            pltpu.VMEM(wide, F32),
            pltpu.VMEM(wide, F32),
            pltpu.VMEM((1, CH), F32),
            pltpu.VMEM(wide, F32),
            pltpu.VMEM(part, BF16),
            pltpu.VMEM((3, FR, NY, 6, COLS, Q * APART), BF16),
            pltpu.VMEM((FR, NY, 4, COLS, CH), BF16),
            pltpu.VMEM(part, F32),
            dma((12,)),
        ],
        flops=conv_flops,
    )
    (merged,) = call(
        add_sums,
        [(whole_part, BF16)],
        (partial, terms),
        [HBM] * 2,
        [pltpu.VMEM((NY * NC, FR, 128), F32), pltpu.VMEM((NZ, TERMS, CH), BF16), dma((2,))],
        aliases={0: 0},
    )
    merged, late_mean = lax.optimization_barrier((merged, mean))
    merged = lax.all_to_all(merged, "z", 0, 0)
    (block_output,) = run(
        forward_conv,
        [(cells, BF16)],
        (x, hp, hn, late_mean, inv, gain, conv_kernel, live),
        rows={1: (0, HALO), 2: (0, HALO)},
        scratch=[padded],
        late=6,
        flops=conv_flops,
    )
    merged, block_output = lax.optimization_barrier((merged, block_output))
    rows, sums = run(sum_rows, [((PROWS, CH), F32), ((FR, 128), F32)], (merged,))
    others = [rows] + [
        lax.ppermute(rows, "x", [(i, (i + d) % NX) for i in range(NX)]) for d in range(1, NX)
    ]
    (input_grad,) = run(
        finish_input, [(cells, BF16)], (sums, scaled, x, g, mean, inv, live)
    )
    kernel_grad, gain_grad = call(
        sum_clips,
        [((TAPS, 4, CH), F32), ((1, CH), F32)],
        others,
        [HBM] * 4,
        [
            pltpu.VMEM((NX, PROWS, CH), F32),
            pltpu.VMEM((TAPS, 4, CH), F32),
            pltpu.VMEM((1, CH), F32),
            dma((6,)),
        ],
    )
    whole = (1,) + cells
    return (
        block_output.reshape(whole),
        input_grad.reshape(whole),
        jnp.swapaxes(kernel_grad, 0, 1),
        gain_grad.reshape(CH),
    )


def solution(mesh):
    fine = Mesh(mesh.devices.reshape(NX, NY, NZ, NC), ("x", "y", "z", "c"))
    space = ("y", "z", "c")
    cells = P("x", None, space, None, None)
    return jax.shard_map(
        local,
        mesh=fine,
        in_specs=(cells, P("x"), P(), P(), cells),
        out_specs=(cells, cells, P(space, None, None), P()),
        check_vma=False,
    )
```

```python
import jax
import jax.numpy as jnp
from jax import lax
from jax.experimental import pallas as pl
from jax.experimental.pallas import tpu as pltpu
from jax.sharding import Mesh
from jax.sharding import PartitionSpec as P

F32 = jnp.float32
BF16 = jnp.bfloat16
NX, NY, NZ, NC = 4, 4, 8, 2
SPACE = NY * NZ * NC
FR, ROWS, COLS, CH = 8, 2, 16, 256
CELLS = ROWS * COLS
GROUPS = 32
GC = CH // GROUPS
ASL = CH // NY
BSL = CH // NC
EPSILON = 1e-05
COUNT = CELLS * SPACE * GC
AROWS = FR // 2 * 3 * COLS
GROWS = FR * ROWS * COLS
TAPS = 27
PROWS = 112
Q = 4
APART = ASL // NC
BLOCK = AROWS + NC * GROWS
TERMS = 16
STEPS = 32000.0
HALO = FR * COLS
HI = lax.Precision.HIGHEST


def hdot(a, b):
    return jnp.dot(a, b, preferred_element_type=F32, precision=HI)


def gather_matrix():
    lane = lax.broadcasted_iota(jnp.int32, (CH, GROUPS), 0)
    group = lax.broadcasted_iota(jnp.int32, (CH, GROUPS), 1)
    return (lane // GC == group).astype(F32)


def spread_matrix():
    group = lax.broadcasted_iota(jnp.int32, (GROUPS, CH), 0)
    lane = lax.broadcasted_iota(jnp.int32, (GROUPS, CH), 1)
    return (lane // GC == group).astype(F32)


def shifted(cells, k):
    if k == 1:
        return cells
    zero = jnp.zeros(cells.shape[:-2] + (1, cells.shape[-1]), cells.dtype)
    if k == 0:
        return jnp.concatenate([zero, cells[..., :-1, :]], axis=-2)
    return jnp.concatenate([cells[..., 1:, :], zero], axis=-2)


def edges_and_sums(x_ref, g_ref, in_ref, out_ref, st_ref):
    first = lax.axis_index("c") == 0
    for n, ref in enumerate((x_ref, g_ref)):
        low, high = ref[:, 0], ref[:, 1]
        inner, outer = jnp.where(first, high, low), jnp.where(first, low, high)
        in_ref[n * HALO : (n + 1) * HALO] = inner.reshape(HALO, CH)
        out_ref[n * HALO : (n + 1) * HALO] = outer.reshape(HALO, CH)
    xf = x_ref[...].astype(F32).reshape(FR, CELLS, CH)
    gather = gather_matrix()
    mean = hdot(jnp.sum(xf, axis=1), gather) / (CELLS * GC)
    centered = xf - hdot(mean, spread_matrix())[:, None, :]
    squares = hdot(jnp.sum(centered * centered, axis=1), gather)
    sums = jnp.concatenate([mean, squares, jnp.zeros((FR, 2 * GROUPS), F32)], axis=1)
    st_ref[...] = sums
    in_ref[2 * HALO :] = as_terms(sums)


def outside(in_ref, out_ref):
    first = lax.axis_index("c") == 0
    inner = in_ref[...].reshape(FR, COLS, CH)
    outer = out_ref[...].reshape(FR, COLS, CH)
    return jnp.where(first, outer, inner), jnp.where(first, inner, outer)


def combined(parts, squares, each):
    count = parts.shape[0]
    mean = jnp.sum(parts, axis=0) / count
    apart = parts - mean[None]
    return mean, jnp.sum(squares + each * (apart * apart), axis=0)


def pair_sums(own_ref, other_ref, out_ref):
    both = jnp.stack([own_ref[...], from_terms(other_ref[...].astype(F32))])
    mean, squares = combined(both[:, :, :GROUPS], both[:, :, GROUPS : 2 * GROUPS], CELLS * GC)
    row = jnp.concatenate([mean, squares, jnp.zeros((FR, 2 * GROUPS), F32)], axis=1)
    out_ref[...] = jnp.broadcast_to(row[None], (NY * NZ, FR, 128))


def as_terms(values):
    high = values.astype(BF16).astype(F32)
    middle = (values - high).astype(BF16).astype(F32)
    low = values - high - middle
    upper = jnp.concatenate([high, middle], axis=1)
    lower = jnp.concatenate([low, jnp.zeros((FR, 128), F32)], axis=1)
    return jnp.concatenate([upper, lower], axis=0).astype(BF16)


def from_terms(terms):
    return (terms[FR:, :128] + terms[:FR, 128:]) + terms[:FR, :128]


def pack_slices(x_ref, hp_ref, hn_ref, out_ref):
    upper = lax.axis_index("c") == 0
    own = [x_ref[:, 0], x_ref[:, 1]]
    before, after = outside(hp_ref, hn_ref)
    rows = [
        jnp.where(upper, before, own[0]),
        jnp.where(upper, own[0], own[1]),
        jnp.where(upper, own[1], after),
    ]
    three = jnp.stack(rows, axis=1).reshape(FR // 2, 2, 3, COLS, CH)
    for y in range(NY):
        part = three[..., y * ASL : (y + 1) * ASL]
        pair = jnp.concatenate([part[:, 0], part[:, 1]], axis=-1)
        out_ref[y] = pair.reshape(AROWS, 2 * ASL)


def backward_conv(g_ref, hp_ref, hn_ref, k_ref, live_ref, pad_ref, held):
    live = live_ref[...][:, None, :]
    before, after = outside(hp_ref, hn_ref)
    rows = [before, g_ref[:, 0], g_ref[:, 1], after]
    for r in range(4):
        cells = rows[r].astype(F32) * live
        for k in range(3):
            pad_ref[k, :FR, r] = shifted(cells, k).astype(BF16)
    pad_ref[:, FR:] = jnp.zeros((3, 2, 4, COLS, CH), BF16)
    held.wait()
    total = jnp.zeros((FR * CELLS, CH), F32)
    for i in range(3):
        for j in range(3):
            for k in range(3):
                window = pad_ref[2 - k, 2 - i : 2 - i + FR, 2 - j : 4 - j]
                total = total + lax.dot_general(
                    window.reshape(FR * CELLS, CH),
                    k_ref[(i * 3 + j) * 3 + k],
                    (((1,), (1,)), ((), ())),
                    preferred_element_type=F32,
                )
    return total


def backward_terms(
    g_ref, hp_ref, hn_ref, k_ref, live_ref, st_ref, x_ref, gain_ref,
    out_ref, sc_ref, mean_ref, inv_ref, pad_ref, held,
):
    act_grad = backward_conv(g_ref, hp_ref, hn_ref, k_ref, live_ref, pad_ref, held)
    mean, whole = combined(
        st_ref[:, :FR, :GROUPS], st_ref[:, :FR, GROUPS : 2 * GROUPS], NC * CELLS * GC
    )
    spread = spread_matrix()
    mean_all = hdot(mean, spread)
    inv_all = hdot(lax.rsqrt(whole / COUNT + EPSILON), spread)
    mean_ref[...] = mean_all
    inv_ref[...] = inv_all
    gain = gain_ref[...][None]
    xf = x_ref[...].astype(F32).reshape(FR, CELLS, CH)
    normalized = (xf - mean_all[:, None, :]) * inv_all[:, None, :]
    gated = normalized * gain
    sig = jax.nn.sigmoid(gated)
    pre = act_grad.reshape(FR, CELLS, CH) * sig * (1.0 + gated * (1.0 - sig))
    scaled = pre * gain
    sc_ref[...] = scaled
    gather = gather_matrix()
    first = hdot(jnp.sum(scaled, axis=1), gather)
    by_channel = jnp.sum(pre * normalized, axis=1)
    second = hdot(by_channel * gain_ref[...], gather)
    gain_part = jnp.sum(by_channel, axis=0, keepdims=True)
    row = lax.broadcasted_iota(jnp.int32, (FR, CH), 0)
    lane = lax.broadcasted_iota(jnp.int32, (FR, CH), 1)
    folded = jnp.where(lane // GROUPS == row, jnp.broadcast_to(gain_part, (FR, CH)), 0.0)
    fold_lane = lax.broadcasted_iota(jnp.int32, (CH, GROUPS), 0)
    fold_at = lax.broadcasted_iota(jnp.int32, (CH, GROUPS), 1)
    folded = hdot(folded, (fold_lane % GROUPS == fold_at).astype(F32))
    everything = jnp.concatenate([first, second, folded, jnp.zeros((FR, GROUPS), F32)], axis=1)
    out_ref[...] = jnp.broadcast_to(everything[None], (NY * NC, FR, 128))


def kernel_part(*refs):
    blocks, (mean_h, inv_h, gain_h, live_h, out_h) = refs[:8], refs[8:13]
    in_ref, mean_ref, inv_ref, gain_ref, live_ref, out_ref, pad_ref, grad_ref, sum_ref, sem = refs[13:]
    y_at, z_at, c_at = lax.axis_index("y"), lax.axis_index("z"), lax.axis_index("c")
    pairs = [(blocks[n], in_ref.at[n]) for n in range(8)]
    pairs += [(mean_h, mean_ref), (inv_h, inv_ref), (gain_h, gain_ref), (live_h, live_ref)]
    copies = [pltpu.make_async_copy(a, b, sem.at[n]) for n, (a, b) in enumerate(pairs)]
    for copy in copies:
        copy.start()
    for copy in copies[8:]:
        copy.wait()
    width = Q * APART
    lane = lax.broadcasted_iota(jnp.int32, (CH, width), 0)
    slot = lax.broadcasted_iota(jnp.int32, (CH, width), 1)
    channel = GC * ((slot % APART) // 4) + 4 * c_at + slot % 4
    pick = (lane == y_at * ASL + channel).astype(F32)
    mean2 = hdot(mean_ref[...], pick)
    inv2 = hdot(inv_ref[...], pick)
    gain2 = hdot(gain_ref[...], pick)
    live = live_ref[:, :BSL].astype(BF16)[:, None, None, :]
    quarter = lax.broadcasted_iota(jnp.int32, (1, width), 1) // APART
    centers, scales = [], []
    for u in range(2):
        center, scale = mean2[4 * u : 4 * u + 1], inv2[4 * u : 4 * u + 1]
        for q in range(1, Q):
            center = jnp.where(quarter == q, mean2[4 * u + q : 4 * u + q + 1], center)
            scale = jnp.where(quarter == q, inv2[4 * u + q : 4 * u + q + 1], scale)
        centers.append(center)
        scales.append(scale * gain2)
    lane = lax.broadcasted_iota(jnp.int32, (2 * ASL, width), 0)
    slot = lax.broadcasted_iota(jnp.int32, (2 * ASL, width), 1)
    channel = GC * ((slot % APART) // 4) + 4 * c_at + slot % 4
    chosen = [
        (lane == (slot // APART - 2 * half) * ASL + channel).astype(BF16) for half in range(2)
    ]
    shape = (3, COLS, width)
    place = lax.broadcasted_iota(jnp.int32, shape, 2) // APART
    row = lax.broadcasted_iota(jnp.int32, shape, 0)
    block = 3 * COLS
    for copy in copies[:8]:
        copy.wait()
    for n in range(8):
        d = n % 4
        y = lax.rem(y_at + NY - d, NY)
        c = c_at if n < 4 else 1 - c_at
        top = (y == 0) & (z_at == 0) & (c == 0)
        bottom = (y == NY - 1) & (z_at == NZ - 1) & (c == NC - 1)
        edge = jnp.where(top, 0, jnp.where(bottom, 2, 3))
        inside = (row != edge).astype(F32)
        acts = []
        for u in range(2):
            at = 2 * u * block
            raw = jnp.dot(
                in_ref[n, at : at + block], chosen[0], preferred_element_type=F32
            ) + jnp.dot(
                in_ref[n, at + block : at + 2 * block], chosen[1], preferred_element_type=F32
            )
            gated = (raw - centers[u]) * scales[u]
            acts.append((gated * jax.nn.sigmoid(gated)).reshape(shape) * inside)
        a, b = acts
        a1, a2, b1 = pltpu.roll(a, 32, 2), pltpu.roll(a, 64, 2), pltpu.roll(b, 32, 2)
        b2 = pltpu.roll(b, 64, 2)
        frames = [
            jnp.where(place < 2, 0.0, a2),
            jnp.where(place < 1, 0.0, a1),
            a,
            pltpu.roll(a, 96, 2),
            jnp.where(place < 2, a2, b2),
            jnp.where(place < 1, a1, b1),
            b,
            pltpu.roll(b, 96, 2),
        ]
        for f in range(FR):
            for k in range(3):
                pad_ref[k, f, d, pl.ds(3 * c, 3)] = shifted(frames[f], k).astype(BF16)
        for h in range(NC):
            at = AROWS + h * GROWS
            cells = in_ref[n, at : at + GROWS].reshape(FR, ROWS, COLS, BSL) * live
            grad_ref[:, d, pl.ds(2 * c, 2), :, h * BSL : (h + 1) * BSL] = cells
    cells = FR * NY * 4 * COLS
    turned_grad = grad_ref[...].reshape(cells, CH).T
    sum_ref[:, 4 * TAPS :] = jnp.zeros((NZ, PROWS - 4 * TAPS, CH), F32)
    combos = [(j, k) for j in range(3) for k in range(3)]
    for first in range(0, 9, 2):
        group = combos[first : first + 2]
        windows = [pad_ref[k, :, :, j : j + 4].reshape(cells, width) for j, k in group]
        window = windows[0] if len(windows) == 1 else jnp.concatenate(windows, axis=1)
        product = jnp.dot(turned_grad, window, preferred_element_type=F32)
        product = product.astype(BF16).T.astype(F32)
        for n, (j, k) in enumerate(group):
            for i in range(3):
                tap = (i * 3 + j) * 3 + k
                at = n * width + i * APART
                piece = product[at : at + APART].reshape(NZ, 4, CH)
                sum_ref[:, tap * 4 : tap * 4 + 4] = piece
    out_ref[...] = sum_ref[...].astype(BF16)
    copy = pltpu.make_async_copy(out_ref, out_h.at[:, :PROWS], sem.at[0])
    copy.start()
    copy.wait()


def add_sums(part_h, b_h, out_h, b_ref, out_ref, sem):
    copy = pltpu.make_async_copy(b_h, b_ref, sem.at[0])
    copy.start()
    copy.wait()
    terms = as_terms(jnp.sum(b_ref[...], axis=0))
    out_ref[...] = jnp.broadcast_to(terms[None], (NZ, TERMS, CH))
    copy = pltpu.make_async_copy(out_ref, out_h.at[:, PROWS:], sem.at[1])
    copy.start()
    copy.wait()


def scale_of(values):
    most = jnp.max(jnp.max(jnp.abs(values), axis=0, keepdims=True), axis=1, keepdims=True)
    most = jnp.broadcast_to(jnp.maximum(most, 1e-36), (1, CH))
    return jnp.ceil(jnp.log2(most))


def sum_rows(in_ref, out_ref, sums_ref):
    total = jnp.sum(in_ref[...].astype(F32), axis=0)
    sums = from_terms(total[PROWS:])
    sums_ref[...] = sums
    fold_at = lax.broadcasted_iota(jnp.int32, (GROUPS, CH), 0)
    fold_lane = lax.broadcasted_iota(jnp.int32, (GROUPS, CH), 1)
    wide = hdot(sums[:, 2 * GROUPS : 3 * GROUPS], (fold_lane % GROUPS == fold_at).astype(F32))
    row = lax.broadcasted_iota(jnp.int32, (FR, CH), 0)
    lane = lax.broadcasted_iota(jnp.int32, (FR, CH), 1)
    gain = jnp.sum(jnp.where(lane // GROUPS == row, wide, 0.0), axis=0, keepdims=True)
    part = total[: 4 * TAPS]
    exponent, gain_exponent = scale_of(part), scale_of(gain)
    code = jnp.floor(part / jnp.exp2(exponent) * STEPS + 0.5)
    steps = gain / jnp.exp2(gain_exponent) * STEPS
    upper = jnp.floor(steps + 0.5)
    lower = jnp.floor((steps - upper) * STEPS + 0.5)
    rows = jnp.concatenate([code, upper, lower, exponent, gain_exponent], axis=0)
    out_ref[...] = rows.astype(jnp.int32).astype(jnp.int16)


def forward_conv(x_ref, hp_ref, hn_ref, mean_ref, inv_ref, gain_ref, k_ref, live_ref, out_ref, pad_ref, held):
    s_at = (lax.axis_index("y") * NZ + lax.axis_index("z")) * NC + lax.axis_index("c")
    before, after = outside(hp_ref, hn_ref)
    rows = [before, x_ref[:, 0], x_ref[:, 1], after]
    mean = mean_ref[...][:, None, :]
    inv = inv_ref[...][:, None, :]
    gain = gain_ref[...][None]
    for r in range(4):
        gated = (rows[r].astype(F32) - mean) * inv * gain
        act = gated * jax.nn.sigmoid(gated)
        if r == 0:
            act = jnp.where(s_at == 0, 0.0, act)
        if r == 3:
            act = jnp.where(s_at == SPACE - 1, 0.0, act)
        for k in range(3):
            pad_ref[k, 2:, r] = shifted(act, k).astype(BF16)
    pad_ref[:, :2] = jnp.zeros((3, 2, 4, COLS, CH), BF16)
    held.wait()
    total = jnp.zeros((FR * CELLS, CH), F32)
    for i in range(3):
        for j in range(3):
            for k in range(3):
                window = pad_ref[k, i : i + FR, j : j + 2]
                total = total + jnp.dot(
                    window.reshape(FR * CELLS, CH),
                    k_ref[(i * 3 + j) * 3 + k],
                    preferred_element_type=F32,
                )
    cells = total.reshape(FR, CELLS, CH) + x_ref[...].astype(F32).reshape(FR, CELLS, CH)
    cells = cells * live_ref[...][:, None, :]
    out_ref[...] = cells.astype(BF16).reshape(FR, ROWS, COLS, CH)


def finish_input(sums_ref, sc_ref, x_ref, g_ref, mean_ref, inv_ref, live_ref, out_ref):
    sums = sums_ref[...]
    spread = spread_matrix()
    first = hdot(sums[:, :GROUPS] / COUNT, spread)[:, None, :]
    second = hdot(sums[:, GROUPS : 2 * GROUPS] / COUNT, spread)[:, None, :]
    inv = inv_ref[...][:, None, :]
    xf = x_ref[...].astype(F32).reshape(FR, CELLS, CH)
    normalized = (xf - mean_ref[...][:, None, :]) * inv
    norm_grad = inv * (sc_ref[...] - first - normalized * second)
    grad = g_ref[...].astype(F32).reshape(FR, CELLS, CH) * live_ref[...][:, None, :]
    out_ref[...] = (grad + norm_grad).astype(BF16).reshape(FR, ROWS, COLS, CH)


def sum_clips(own_h, one_h, two_h, three_h, kg_h, gain_h, in_ref, kg_ref, gain_ref, sem):
    x_at = lax.axis_index("x")
    copies = []
    for d, src in enumerate((own_h, one_h, two_h, three_h)):
        copies.append(
            pltpu.make_async_copy(src, in_ref.at[lax.rem(x_at + NX - d, NX)], sem.at[d])
        )
    for copy in copies:
        copy.start()
    for copy in copies:
        copy.wait()
    total = jnp.zeros((4 * TAPS, CH), F32)
    gain = jnp.zeros((1, CH), F32)
    at = 4 * TAPS
    for n in range(NX):
        rows = in_ref[n].astype(jnp.int32).astype(F32)
        total = total + rows[:at] / STEPS * jnp.exp2(rows[at + 2 : at + 3])
        steps = rows[at : at + 1] + rows[at + 1 : at + 2] / STEPS
        gain = gain + steps / STEPS * jnp.exp2(rows[at + 3 : at + 4])
    for tap in range(TAPS):
        kg_ref[tap] = total[4 * tap : 4 * tap + 4]
    gain_ref[...] = gain
    out = (
        pltpu.make_async_copy(kg_ref, kg_h, sem.at[4]),
        pltpu.make_async_copy(gain_ref, gain_h, sem.at[5]),
    )
    for copy in out:
        copy.start()
    for copy in out:
        copy.wait()


HBM = pl.BlockSpec(memory_space=pltpu.HBM)
SMEM = pl.BlockSpec(memory_space=pltpu.SMEM)


def stay_out(array):
    return pltpu.with_memory_space_constraint(array, pltpu.HBM)


def shapes(outs):
    return tuple(jax.ShapeDtypeStruct(s, d) for s, d in outs)


def call(body, outs, args, specs, scratch, flops=0, limit=32, aliases={}):
    return pl.pallas_call(
        body,
        out_shape=shapes(outs),
        in_specs=specs,
        out_specs=tuple(HBM for _ in outs),
        scratch_shapes=list(scratch),
        input_output_aliases=aliases,
        compiler_params=pltpu.CompilerParams(vmem_limit_bytes=limit * 2**20),
        cost_estimate=pl.CostEstimate(flops=flops, bytes_accessed=2**20, transcendentals=0),
        name=body.__name__,
    )(*args)


def run(body, outs, args, scratch=(), late=None, smem=(), flops=0, rows={}):
    count, outputs = len(args), len(outs)
    moved = [at for at in range(count) if at not in smem]

    def kernel(*refs):
        ins, targets = list(refs[:count]), refs[count : count + outputs]
        rest = refs[count + outputs :]
        buffers, rest = rest[: len(moved)], rest[len(moved) :]
        results, rest = rest[:outputs], rest[outputs:]
        sem, extra = rest[0], rest[1:]
        copies = [
            pltpu.make_async_copy(
                ins[at].at[rows[at][0] : rows[at][1]] if at in rows else ins[at], buffers[n], sem.at[n]
            )
            for n, at in enumerate(moved)
        ]
        held = copies.pop(moved.index(late)) if late is not None else None
        for copy in copies + ([held] if held is not None else []):
            copy.start()
        for n, at in enumerate(moved):
            ins[at] = buffers[n]
        for copy in copies:
            copy.wait()
        if held is None:
            body(*ins, *results, *extra)
        else:
            body(*ins, *results, *extra, held)
        copies = [
            pltpu.make_async_copy(results[n], targets[n], sem.at[len(moved) + n])
            for n in range(outputs)
        ]
        for copy in copies:
            copy.start()
        for copy in copies:
            copy.wait()

    kernel.__name__ = body.__name__
    specs = [SMEM if at in smem else HBM for at in range(count)]
    buffers = []
    for at in moved:
        shape = args[at].shape
        if at in rows:
            shape = (rows[at][1] - rows[at][0],) + shape[1:]
        buffers.append(pltpu.VMEM(shape, args[at].dtype))
    buffers += [pltpu.VMEM(s, d) for s, d in outs]
    buffers += [pltpu.SemaphoreType.DMA((len(moved) + outputs,))]
    return call(kernel, outs, args, specs, buffers + list(scratch), flops)


def pack_body(x_h, g_h, hp_h, hn_h, *refs):
    outs = refs[:NY]
    x_ref, hp_ref, hn_ref, buf, sem = refs[NY:]
    pairs = ((x_h, x_ref), (hp_h.at[:HALO], hp_ref), (hn_h.at[:HALO], hn_ref))
    copies = [pltpu.make_async_copy(a, b, sem.at[n]) for n, (a, b) in enumerate(pairs)]
    for copy in copies:
        copy.start()
    straight = []
    for d, out in enumerate(outs):
        for c in range(NC):
            at = AROWS + c * GROWS
            straight.append(
                pltpu.make_async_copy(
                    g_h.at[:, c * BSL : (c + 1) * BSL],
                    out.at[at : at + GROWS],
                    sem.at[3 + NC * d + c],
                )
            )
    for copy in straight:
        copy.start()
    for copy in copies:
        copy.wait()
    pack_slices(x_ref, hp_ref, hn_ref, buf)
    y_at = lax.axis_index("y")
    copies = [
        pltpu.make_async_copy(
            buf.at[lax.rem(y_at + d, NY)], out.at[:AROWS], sem.at[3 + NC * NY + d]
        )
        for d, out in enumerate(outs)
    ]
    for copy in copies:
        copy.start()
    for copy in straight + copies:
        copy.wait()


def local(video_latent, frame_counts, conv_kernel, norm_gain, output_grad):
    x = stay_out(video_latent.reshape(FR, ROWS, COLS, CH))
    g = stay_out(output_grad.reshape(FR, ROWS, COLS, CH))
    gain = stay_out(norm_gain.reshape(1, CH))
    conv_kernel = stay_out(conv_kernel)
    space = ("y", "z", "c")
    cells = (FR, ROWS, COLS, CH)
    wide = (FR, CH)
    swap = [(0, 1), (1, 0)]
    dma = pltpu.SemaphoreType.DMA

    inner, outer, stats = run(
        edges_and_sums,
        [
            ((2 * HALO + TERMS, CH), BF16),
            ((2 * HALO, CH), BF16),
            ((FR, 128), F32),
        ],
        (x, g),
    )
    stats, counts = lax.optimization_barrier((stats, frame_counts))
    live = jnp.broadcast_to(jnp.arange(FR)[:, None] < counts[0], wide).astype(F32)
    hp = lax.ppermute(inner, "c", swap)
    hn = lax.ppermute(
        outer,
        space,
        [(i, i - 1 if i % 2 == 0 else i + 1) for i in range(1, SPACE - 1)],
    )
    (stats,) = run(
        pair_sums,
        [((NY * NZ, FR, 128), F32)],
        (stats, hp),
        rows={1: (2 * HALO, 2 * HALO + TERMS)},
    )
    stats = lax.all_to_all(stats, ("y", "z"), 0, 0)
    block = (BLOCK, BSL)
    packed = call(
        pack_body,
        [(block, BF16)] * NY,
        (x, stay_out(output_grad.reshape(GROWS, CH)), hp, hn),
        [HBM] * 4,
        [pltpu.VMEM(cells, BF16)]
        + [pltpu.VMEM((HALO, CH), BF16)] * 2
        + [pltpu.VMEM((NY, AROWS, BSL), BF16), dma((3 + NC * NY + NY,))],
    )
    near = [packed[0]] + [
        lax.ppermute(packed[d], "y", [(i, (i + d) % NY) for i in range(NY)]) for d in range(1, NY)
    ]
    conv_flops = 16 * TAPS * FR * CELLS * CH * CH
    padded = pltpu.VMEM((3, FR + 2, 4, COLS, CH), BF16)
    terms, scaled, mean, inv = run(
        backward_terms,
        [((NY * NC, FR, 128), F32), ((FR, CELLS, CH), F32), (wide, F32), (wide, F32)],
        (g, hp, hn, conv_kernel, live, stats, x, gain),
        rows={1: (HALO, 2 * HALO), 2: (HALO, 2 * HALO)},
        scratch=[padded],
        late=3,
    )
    *near, terms = lax.optimization_barrier((*near, terms))
    terms = lax.all_to_all(terms, ("y", "c"), 0, 0)
    far = [lax.ppermute(a, "c", swap) for a in near]
    part = (NZ, PROWS, CH)
    whole_part = (NZ, PROWS + TERMS, CH)
    (partial,) = call(
        kernel_part,
        [(whole_part, BF16)],
        (*near, *far, mean, inv, gain, live),
        [HBM] * 12,
        [
            pltpu.VMEM((8, BLOCK, BSL), BF16),
            pltpu.VMEM(wide, F32),
            pltpu.VMEM(wide, F32),
            pltpu.VMEM((1, CH), F32),
            pltpu.VMEM(wide, F32),
            pltpu.VMEM(part, BF16),
            pltpu.VMEM((3, FR, NY, 6, COLS, Q * APART), BF16),
            pltpu.VMEM((FR, NY, 4, COLS, CH), BF16),
            pltpu.VMEM(part, F32),
            dma((12,)),
        ],
        flops=conv_flops,
    )
    (merged,) = call(
        add_sums,
        [(whole_part, BF16)],
        (partial, terms),
        [HBM] * 2,
        [pltpu.VMEM((NY * NC, FR, 128), F32), pltpu.VMEM((NZ, TERMS, CH), BF16), dma((2,))],
        aliases={0: 0},
    )
    merged, late_mean = lax.optimization_barrier((merged, mean))
    merged = lax.all_to_all(merged, "z", 0, 0)
    (block_output,) = run(
        forward_conv,
        [(cells, BF16)],
        (x, hp, hn, late_mean, inv, gain, conv_kernel, live),
        rows={1: (0, HALO), 2: (0, HALO)},
        scratch=[padded],
        late=6,
        flops=conv_flops,
    )
    merged, block_output = lax.optimization_barrier((merged, block_output))
    rows, sums = run(sum_rows, [((PROWS, CH), jnp.int16), ((FR, 128), F32)], (merged,))
    others = [rows] + [
        lax.ppermute(rows, "x", [(i, (i + d) % NX) for i in range(NX)]) for d in range(1, NX)
    ]
    (input_grad,) = run(
        finish_input, [(cells, BF16)], (sums, scaled, x, g, mean, inv, live)
    )
    kernel_grad, gain_grad = call(
        sum_clips,
        [((TAPS, 4, CH), F32), ((1, CH), F32)],
        others,
        [HBM] * 4,
        [
            pltpu.VMEM((NX, PROWS, CH), jnp.int16),
            pltpu.VMEM((TAPS, 4, CH), F32),
            pltpu.VMEM((1, CH), F32),
            dma((6,)),
        ],
    )
    whole = (1,) + cells
    return (
        block_output.reshape(whole),
        input_grad.reshape(whole),
        jnp.swapaxes(kernel_grad, 0, 1),
        gain_grad.reshape(CH),
    )


def solution(mesh):
    fine = Mesh(mesh.devices.reshape(NX, NY, NZ, NC), ("x", "y", "z", "c"))
    space = ("y", "z", "c")
    cells = P("x", None, space, None, None)
    return jax.shard_map(
        local,
        mesh=fine,
        in_specs=(cells, P("x"), P(), P(), cells),
        out_specs=(cells, cells, P(space, None, None), P()),
        check_vma=False,
    )
```

```python
import jax
import jax.numpy as jnp
from jax import lax
from jax.experimental import pallas as pl
from jax.experimental.pallas import tpu as pltpu
from jax.sharding import Mesh
from jax.sharding import PartitionSpec as P

F32 = jnp.float32
BF16 = jnp.bfloat16
NX, NY, NZ, NC = 4, 4, 8, 2
SPACE = NY * NZ * NC
FR, ROWS, COLS, CH = 8, 2, 16, 256
CELLS = ROWS * COLS
GROUPS = 32
GC = CH // GROUPS
ASL = CH // NY
BSL = CH // NC
EPSILON = 1e-05
COUNT = CELLS * SPACE * GC
AROWS = FR // 2 * 3 * COLS
GROWS = FR * ROWS * COLS
TAPS = 27
PROWS = 112
Q = 4
APART = ASL // NC
BLOCK = AROWS + NC * GROWS
TERMS = 16
STEPS = 32000.0
HALO = FR
HI = lax.Precision.HIGHEST


def hdot(a, b):
    return jnp.dot(a, b, preferred_element_type=F32, precision=HI)


def gather_matrix():
    lane = lax.broadcasted_iota(jnp.int32, (CH, GROUPS), 0)
    group = lax.broadcasted_iota(jnp.int32, (CH, GROUPS), 1)
    return (lane // GC == group).astype(F32)


def spread_matrix():
    group = lax.broadcasted_iota(jnp.int32, (GROUPS, CH), 0)
    lane = lax.broadcasted_iota(jnp.int32, (GROUPS, CH), 1)
    return (lane // GC == group).astype(F32)


def shifted(cells, k):
    if k == 1:
        return cells
    zero = jnp.zeros(cells.shape[:-2] + (1, cells.shape[-1]), cells.dtype)
    if k == 0:
        return jnp.concatenate([zero, cells[..., :-1, :]], axis=-2)
    return jnp.concatenate([cells[..., 1:, :], zero], axis=-2)


def edges_and_sums(x_h, g_h, in_h, out_h, st_h, x_ref, st_ref, term_ref, sem):
    c_at = lax.axis_index("c")
    load = pltpu.make_async_copy(x_h, x_ref, sem.at[0])
    load.start()
    halo = []
    for n, source in enumerate((x_h, g_h)):
        part = slice(n * FR, (n + 1) * FR)
        halo.append(pltpu.make_async_copy(source.at[:, 1 - c_at], in_h.at[part], sem.at[1 + 2 * n]))
        halo.append(pltpu.make_async_copy(source.at[:, c_at], out_h.at[part], sem.at[2 + 2 * n]))
    for copy in halo:
        copy.start()
    load.wait()
    xf = x_ref[...].astype(F32).reshape(FR, CELLS, CH)
    gather = gather_matrix()
    mean = hdot(jnp.sum(xf, axis=1), gather) / (CELLS * GC)
    centered = xf - hdot(mean, spread_matrix())[:, None, :]
    squares = hdot(jnp.sum(centered * centered, axis=1), gather)
    sums = jnp.concatenate([mean, squares, jnp.zeros((FR, 2 * GROUPS), F32)], axis=1)
    st_ref[...] = sums
    term_ref[0] = as_terms(sums)
    halo.append(pltpu.make_async_copy(term_ref, in_h.at[2 * FR :], sem.at[5]))
    halo.append(pltpu.make_async_copy(st_ref, st_h, sem.at[6]))
    for copy in halo[4:]:
        copy.start()
    for copy in halo:
        copy.wait()


def outside(in_ref, out_ref):
    first = lax.axis_index("c") == 0
    inner = in_ref[...].reshape(FR, COLS, CH)
    outer = out_ref[...].reshape(FR, COLS, CH)
    return jnp.where(first, outer, inner), jnp.where(first, inner, outer)


def combined(parts, squares, each):
    count = parts.shape[0]
    mean = jnp.sum(parts, axis=0) / count
    apart = parts - mean[None]
    return mean, jnp.sum(squares + each * (apart * apart), axis=0)


def pair_sums(own_ref, other_ref, out_ref):
    both = jnp.stack([own_ref[...], from_terms(other_ref[0].astype(F32))])
    mean, squares = combined(both[:, :, :GROUPS], both[:, :, GROUPS : 2 * GROUPS], CELLS * GC)
    row = jnp.concatenate([mean, squares, jnp.zeros((FR, 2 * GROUPS), F32)], axis=1)
    out_ref[...] = jnp.broadcast_to(row[None], (NY * NZ, FR, 128))


def as_terms(values):
    high = values.astype(BF16).astype(F32)
    middle = (values - high).astype(BF16).astype(F32)
    low = values - high - middle
    upper = jnp.concatenate([high, middle], axis=1)
    lower = jnp.concatenate([low, jnp.zeros((FR, 128), F32)], axis=1)
    return jnp.concatenate([upper, lower], axis=0).astype(BF16)


def from_terms(terms):
    return (terms[FR:, :128] + terms[:FR, 128:]) + terms[:FR, :128]


def pack_slices(x_ref, hp_ref, hn_ref, out_ref):
    upper = lax.axis_index("c") == 0
    own = [x_ref[:, 0], x_ref[:, 1]]
    before, after = outside(hp_ref, hn_ref)
    rows = [
        jnp.where(upper, before, own[0]),
        jnp.where(upper, own[0], own[1]),
        jnp.where(upper, own[1], after),
    ]
    three = jnp.stack(rows, axis=1).reshape(FR // 2, 2, 3, COLS, CH)
    for y in range(NY):
        part = three[..., y * ASL : (y + 1) * ASL]
        pair = jnp.concatenate([part[:, 0], part[:, 1]], axis=-1)
        out_ref[y] = pair.reshape(AROWS, 2 * ASL)


def backward_conv(g_ref, hp_ref, hn_ref, k_ref, live_ref, pad_ref, held):
    live = live_ref[...][:, None, :]
    before, after = outside(hp_ref, hn_ref)
    rows = [before, g_ref[:, 0], g_ref[:, 1], after]
    for r in range(4):
        cells = rows[r].astype(F32) * live
        for k in range(3):
            pad_ref[k, :FR, r] = shifted(cells, k).astype(BF16)
    pad_ref[:, FR:] = jnp.zeros((3, 2, 4, COLS, CH), BF16)
    held.wait()
    total = jnp.zeros((FR * CELLS, CH), F32)
    for i in range(3):
        for j in range(3):
            for k in range(3):
                window = pad_ref[2 - k, 2 - i : 2 - i + FR, 2 - j : 4 - j]
                total = total + lax.dot_general(
                    window.reshape(FR * CELLS, CH),
                    k_ref[(i * 3 + j) * 3 + k],
                    (((1,), (1,)), ((), ())),
                    preferred_element_type=F32,
                )
    return total


def backward_terms(
    g_ref, hp_ref, hn_ref, k_ref, live_ref, st_ref, x_ref, gain_ref,
    out_ref, sc_ref, mean_ref, inv_ref, pad_ref, held,
):
    act_grad = backward_conv(g_ref, hp_ref, hn_ref, k_ref, live_ref, pad_ref, held)
    mean, whole = combined(
        st_ref[:, :FR, :GROUPS], st_ref[:, :FR, GROUPS : 2 * GROUPS], NC * CELLS * GC
    )
    spread = spread_matrix()
    mean_all = hdot(mean, spread)
    inv_all = hdot(lax.rsqrt(whole / COUNT + EPSILON), spread)
    mean_ref[...] = mean_all
    inv_ref[...] = inv_all
    gain = gain_ref[...][None]
    xf = x_ref[...].astype(F32).reshape(FR, CELLS, CH)
    normalized = (xf - mean_all[:, None, :]) * inv_all[:, None, :]
    gated = normalized * gain
    sig = jax.nn.sigmoid(gated)
    pre = act_grad.reshape(FR, CELLS, CH) * sig * (1.0 + gated * (1.0 - sig))
    scaled = pre * gain
    sc_ref[...] = scaled
    gather = gather_matrix()
    first = hdot(jnp.sum(scaled, axis=1), gather)
    by_channel = jnp.sum(pre * normalized, axis=1)
    second = hdot(by_channel * gain_ref[...], gather)
    gain_part = jnp.sum(by_channel, axis=0, keepdims=True)
    row = lax.broadcasted_iota(jnp.int32, (FR, CH), 0)
    lane = lax.broadcasted_iota(jnp.int32, (FR, CH), 1)
    folded = jnp.where(lane // GROUPS == row, jnp.broadcast_to(gain_part, (FR, CH)), 0.0)
    fold_lane = lax.broadcasted_iota(jnp.int32, (CH, GROUPS), 0)
    fold_at = lax.broadcasted_iota(jnp.int32, (CH, GROUPS), 1)
    folded = hdot(folded, (fold_lane % GROUPS == fold_at).astype(F32))
    everything = jnp.concatenate([first, second, folded, jnp.zeros((FR, GROUPS), F32)], axis=1)
    out_ref[...] = jnp.broadcast_to(everything[None], (NY * NC, FR, 128))


def kernel_part(*refs):
    blocks, (mean_h, inv_h, gain_h, live_h, out_h) = refs[:8], refs[8:13]
    in_ref, mean_ref, inv_ref, gain_ref, live_ref, out_ref, pad_ref, grad_ref, sum_ref, sem = refs[13:]
    y_at, z_at, c_at = lax.axis_index("y"), lax.axis_index("z"), lax.axis_index("c")
    pairs = [(blocks[n], in_ref.at[n]) for n in range(8)]
    pairs += [(mean_h, mean_ref), (inv_h, inv_ref), (gain_h, gain_ref), (live_h, live_ref)]
    copies = [pltpu.make_async_copy(a, b, sem.at[n]) for n, (a, b) in enumerate(pairs)]
    for copy in copies:
        copy.start()
    for copy in copies[8:]:
        copy.wait()
    width = Q * APART
    lane = lax.broadcasted_iota(jnp.int32, (CH, width), 0)
    slot = lax.broadcasted_iota(jnp.int32, (CH, width), 1)
    channel = GC * ((slot % APART) // 4) + 4 * c_at + slot % 4
    pick = (lane == y_at * ASL + channel).astype(F32)
    mean2 = hdot(mean_ref[...], pick)
    inv2 = hdot(inv_ref[...], pick)
    gain2 = hdot(gain_ref[...], pick)
    live = live_ref[:, :BSL].astype(BF16)[:, None, None, :]
    quarter = lax.broadcasted_iota(jnp.int32, (1, width), 1) // APART
    centers, scales = [], []
    for u in range(2):
        center, scale = mean2[4 * u : 4 * u + 1], inv2[4 * u : 4 * u + 1]
        for q in range(1, Q):
            center = jnp.where(quarter == q, mean2[4 * u + q : 4 * u + q + 1], center)
            scale = jnp.where(quarter == q, inv2[4 * u + q : 4 * u + q + 1], scale)
        centers.append(center)
        scales.append(scale * gain2)
    lane = lax.broadcasted_iota(jnp.int32, (2 * ASL, width), 0)
    slot = lax.broadcasted_iota(jnp.int32, (2 * ASL, width), 1)
    channel = GC * ((slot % APART) // 4) + 4 * c_at + slot % 4
    chosen = [
        (lane == (slot // APART - 2 * half) * ASL + channel).astype(BF16) for half in range(2)
    ]
    shape = (3, COLS, width)
    place = lax.broadcasted_iota(jnp.int32, shape, 2) // APART
    row = lax.broadcasted_iota(jnp.int32, shape, 0)
    block = 3 * COLS
    for copy in copies[:8]:
        copy.wait()
    for n in range(8):
        d = n % 4
        y = lax.rem(y_at + NY - d, NY)
        c = c_at if n < 4 else 1 - c_at
        top = (y == 0) & (z_at == 0) & (c == 0)
        bottom = (y == NY - 1) & (z_at == NZ - 1) & (c == NC - 1)
        edge = jnp.where(top, 0, jnp.where(bottom, 2, 3))
        inside = (row != edge).astype(F32)
        acts = []
        for u in range(2):
            at = 2 * u * block
            raw = jnp.dot(
                in_ref[n, at : at + block], chosen[0], preferred_element_type=F32
            ) + jnp.dot(
                in_ref[n, at + block : at + 2 * block], chosen[1], preferred_element_type=F32
            )
            gated = (raw - centers[u]) * scales[u]
            acts.append((gated * jax.nn.sigmoid(gated)).reshape(shape) * inside)
        a, b = acts
        a1, a2, b1 = pltpu.roll(a, 32, 2), pltpu.roll(a, 64, 2), pltpu.roll(b, 32, 2)
        b2 = pltpu.roll(b, 64, 2)
        frames = [
            jnp.where(place < 2, 0.0, a2),
            jnp.where(place < 1, 0.0, a1),
            a,
            pltpu.roll(a, 96, 2),
            jnp.where(place < 2, a2, b2),
            jnp.where(place < 1, a1, b1),
            b,
            pltpu.roll(b, 96, 2),
        ]
        for f in range(FR):
            for k in range(3):
                pad_ref[k, f, d, pl.ds(3 * c, 3)] = shifted(frames[f], k).astype(BF16)
        for h in range(NC):
            at = AROWS + h * GROWS
            cells = in_ref[n, at : at + GROWS].reshape(FR, ROWS, COLS, BSL) * live
            grad_ref[:, d, pl.ds(2 * c, 2), :, h * BSL : (h + 1) * BSL] = cells
    cells = FR * NY * 4 * COLS
    turned_grad = grad_ref[...].reshape(cells, CH).T
    sum_ref[:, 4 * TAPS :] = jnp.zeros((NZ, PROWS - 4 * TAPS, CH), F32)
    combos = [(j, k) for j in range(3) for k in range(3)]
    for first in range(0, 9, 2):
        group = combos[first : first + 2]
        windows = [pad_ref[k, :, :, j : j + 4].reshape(cells, width) for j, k in group]
        window = windows[0] if len(windows) == 1 else jnp.concatenate(windows, axis=1)
        product = jnp.dot(turned_grad, window, preferred_element_type=F32)
        product = product.astype(BF16).T.astype(F32)
        for n, (j, k) in enumerate(group):
            for i in range(3):
                tap = (i * 3 + j) * 3 + k
                at = n * width + i * APART
                piece = product[at : at + APART].reshape(NZ, 4, CH)
                sum_ref[:, tap * 4 : tap * 4 + 4] = piece
    out_ref[...] = sum_ref[...].astype(BF16)
    copy = pltpu.make_async_copy(out_ref, out_h.at[:, :PROWS], sem.at[0])
    copy.start()
    copy.wait()


def add_sums(part_h, b_h, out_h, b_ref, out_ref, sem):
    copy = pltpu.make_async_copy(b_h, b_ref, sem.at[0])
    copy.start()
    copy.wait()
    terms = as_terms(jnp.sum(b_ref[...], axis=0))
    out_ref[...] = jnp.broadcast_to(terms[None], (NZ, TERMS, CH))
    copy = pltpu.make_async_copy(out_ref, out_h.at[:, PROWS:], sem.at[1])
    copy.start()
    copy.wait()


def scale_of(values):
    most = jnp.max(jnp.max(jnp.abs(values), axis=0, keepdims=True), axis=1, keepdims=True)
    most = jnp.broadcast_to(jnp.maximum(most, 1e-36), (1, CH))
    return jnp.ceil(jnp.log2(most))


def sum_rows(in_ref, out_ref, sums_ref):
    total = jnp.sum(in_ref[...].astype(F32), axis=0)
    sums = from_terms(total[PROWS:])
    sums_ref[...] = sums
    fold_at = lax.broadcasted_iota(jnp.int32, (GROUPS, CH), 0)
    fold_lane = lax.broadcasted_iota(jnp.int32, (GROUPS, CH), 1)
    wide = hdot(sums[:, 2 * GROUPS : 3 * GROUPS], (fold_lane % GROUPS == fold_at).astype(F32))
    row = lax.broadcasted_iota(jnp.int32, (FR, CH), 0)
    lane = lax.broadcasted_iota(jnp.int32, (FR, CH), 1)
    gain = jnp.sum(jnp.where(lane // GROUPS == row, wide, 0.0), axis=0, keepdims=True)
    part = total[: 4 * TAPS]
    exponent, gain_exponent = scale_of(part), scale_of(gain)
    code = jnp.floor(part / jnp.exp2(exponent) * STEPS + 0.5)
    steps = gain / jnp.exp2(gain_exponent) * STEPS
    upper = jnp.floor(steps + 0.5)
    lower = jnp.floor((steps - upper) * STEPS + 0.5)
    rows = jnp.concatenate([code, upper, lower, exponent, gain_exponent], axis=0)
    out_ref[...] = rows.astype(jnp.int32).astype(jnp.int16)


def forward_conv(x_ref, hp_ref, hn_ref, mean_ref, inv_ref, gain_ref, k_ref, live_ref, out_ref, pad_ref, held):
    s_at = (lax.axis_index("y") * NZ + lax.axis_index("z")) * NC + lax.axis_index("c")
    before, after = outside(hp_ref, hn_ref)
    rows = [before, x_ref[:, 0], x_ref[:, 1], after]
    mean = mean_ref[...][:, None, :]
    inv = inv_ref[...][:, None, :]
    gain = gain_ref[...][None]
    for r in range(4):
        gated = (rows[r].astype(F32) - mean) * inv * gain
        act = gated * jax.nn.sigmoid(gated)
        if r == 0:
            act = jnp.where(s_at == 0, 0.0, act)
        if r == 3:
            act = jnp.where(s_at == SPACE - 1, 0.0, act)
        for k in range(3):
            pad_ref[k, 2:, r] = shifted(act, k).astype(BF16)
    pad_ref[:, :2] = jnp.zeros((3, 2, 4, COLS, CH), BF16)
    held.wait()
    total = jnp.zeros((FR * CELLS, CH), F32)
    for i in range(3):
        for j in range(3):
            for k in range(3):
                window = pad_ref[k, i : i + FR, j : j + 2]
                total = total + jnp.dot(
                    window.reshape(FR * CELLS, CH),
                    k_ref[(i * 3 + j) * 3 + k],
                    preferred_element_type=F32,
                )
    cells = total.reshape(FR, CELLS, CH) + x_ref[...].astype(F32).reshape(FR, CELLS, CH)
    cells = cells * live_ref[...][:, None, :]
    out_ref[...] = cells.astype(BF16).reshape(FR, ROWS, COLS, CH)


def finish_input(sums_ref, sc_ref, x_ref, g_ref, mean_ref, inv_ref, live_ref, out_ref):
    sums = sums_ref[...]
    spread = spread_matrix()
    first = hdot(sums[:, :GROUPS] / COUNT, spread)[:, None, :]
    second = hdot(sums[:, GROUPS : 2 * GROUPS] / COUNT, spread)[:, None, :]
    inv = inv_ref[...][:, None, :]
    xf = x_ref[...].astype(F32).reshape(FR, CELLS, CH)
    normalized = (xf - mean_ref[...][:, None, :]) * inv
    norm_grad = inv * (sc_ref[...] - first - normalized * second)
    grad = g_ref[...].astype(F32).reshape(FR, CELLS, CH) * live_ref[...][:, None, :]
    out_ref[...] = (grad + norm_grad).astype(BF16).reshape(FR, ROWS, COLS, CH)


def sum_clips(own_h, one_h, two_h, three_h, kg_h, gain_h, in_ref, kg_ref, gain_ref, sem):
    x_at = lax.axis_index("x")
    copies = []
    for d, src in enumerate((own_h, one_h, two_h, three_h)):
        copies.append(
            pltpu.make_async_copy(src, in_ref.at[lax.rem(x_at + NX - d, NX)], sem.at[d])
        )
    for copy in copies:
        copy.start()
    for copy in copies:
        copy.wait()
    total = jnp.zeros((4 * TAPS, CH), F32)
    gain = jnp.zeros((1, CH), F32)
    at = 4 * TAPS
    for n in range(NX):
        rows = in_ref[n].astype(jnp.int32).astype(F32)
        total = total + rows[:at] / STEPS * jnp.exp2(rows[at + 2 : at + 3])
        steps = rows[at : at + 1] + rows[at + 1 : at + 2] / STEPS
        gain = gain + steps / STEPS * jnp.exp2(rows[at + 3 : at + 4])
    for tap in range(TAPS):
        kg_ref[tap] = total[4 * tap : 4 * tap + 4]
    gain_ref[...] = gain
    out = (
        pltpu.make_async_copy(kg_ref, kg_h, sem.at[4]),
        pltpu.make_async_copy(gain_ref, gain_h, sem.at[5]),
    )
    for copy in out:
        copy.start()
    for copy in out:
        copy.wait()


HBM = pl.BlockSpec(memory_space=pltpu.HBM)
SMEM = pl.BlockSpec(memory_space=pltpu.SMEM)


def stay_out(array):
    return pltpu.with_memory_space_constraint(array, pltpu.HBM)


def shapes(outs):
    return tuple(jax.ShapeDtypeStruct(s, d) for s, d in outs)


def call(body, outs, args, specs, scratch, flops=0, limit=32, aliases={}):
    return pl.pallas_call(
        body,
        out_shape=shapes(outs),
        in_specs=specs,
        out_specs=tuple(HBM for _ in outs),
        scratch_shapes=list(scratch),
        input_output_aliases=aliases,
        compiler_params=pltpu.CompilerParams(vmem_limit_bytes=limit * 2**20),
        cost_estimate=pl.CostEstimate(flops=flops, bytes_accessed=2**20, transcendentals=0),
        name=body.__name__,
    )(*args)


def run(body, outs, args, scratch=(), late=None, smem=(), flops=0, rows={}):
    count, outputs = len(args), len(outs)
    moved = [at for at in range(count) if at not in smem]

    def kernel(*refs):
        ins, targets = list(refs[:count]), refs[count : count + outputs]
        rest = refs[count + outputs :]
        buffers, rest = rest[: len(moved)], rest[len(moved) :]
        results, rest = rest[:outputs], rest[outputs:]
        sem, extra = rest[0], rest[1:]
        copies = [
            pltpu.make_async_copy(
                ins[at].at[rows[at][0] : rows[at][1]] if at in rows else ins[at], buffers[n], sem.at[n]
            )
            for n, at in enumerate(moved)
        ]
        held = copies.pop(moved.index(late)) if late is not None else None
        for copy in copies + ([held] if held is not None else []):
            copy.start()
        for n, at in enumerate(moved):
            ins[at] = buffers[n]
        for copy in copies:
            copy.wait()
        if held is None:
            body(*ins, *results, *extra)
        else:
            body(*ins, *results, *extra, held)
        copies = [
            pltpu.make_async_copy(results[n], targets[n], sem.at[len(moved) + n])
            for n in range(outputs)
        ]
        for copy in copies:
            copy.start()
        for copy in copies:
            copy.wait()

    kernel.__name__ = body.__name__
    specs = [SMEM if at in smem else HBM for at in range(count)]
    buffers = []
    for at in moved:
        shape = args[at].shape
        if at in rows:
            shape = (rows[at][1] - rows[at][0],) + shape[1:]
        buffers.append(pltpu.VMEM(shape, args[at].dtype))
    buffers += [pltpu.VMEM(s, d) for s, d in outs]
    buffers += [pltpu.SemaphoreType.DMA((len(moved) + outputs,))]
    return call(kernel, outs, args, specs, buffers + list(scratch), flops)


def pack_body(x_h, g_h, hp_h, hn_h, *refs):
    outs = refs[:NY]
    x_ref, hp_ref, hn_ref, buf, sem = refs[NY:]
    pairs = ((x_h, x_ref), (hp_h.at[:HALO], hp_ref), (hn_h.at[:HALO], hn_ref))
    copies = [pltpu.make_async_copy(a, b, sem.at[n]) for n, (a, b) in enumerate(pairs)]
    for copy in copies:
        copy.start()
    straight = []
    for d, out in enumerate(outs):
        for c in range(NC):
            at = AROWS + c * GROWS
            straight.append(
                pltpu.make_async_copy(
                    g_h.at[:, c * BSL : (c + 1) * BSL],
                    out.at[at : at + GROWS],
                    sem.at[3 + NC * d + c],
                )
            )
    for copy in straight:
        copy.start()
    for copy in copies:
        copy.wait()
    pack_slices(x_ref, hp_ref, hn_ref, buf)
    y_at = lax.axis_index("y")
    copies = [
        pltpu.make_async_copy(
            buf.at[lax.rem(y_at + d, NY)], out.at[:AROWS], sem.at[3 + NC * NY + d]
        )
        for d, out in enumerate(outs)
    ]
    for copy in copies:
        copy.start()
    for copy in straight + copies:
        copy.wait()


def local(video_latent, frame_counts, conv_kernel, norm_gain, output_grad):
    x = stay_out(video_latent.reshape(FR, ROWS, COLS, CH))
    g = stay_out(output_grad.reshape(FR, ROWS, COLS, CH))
    gain = stay_out(norm_gain.reshape(1, CH))
    conv_kernel = stay_out(conv_kernel)
    space = ("y", "z", "c")
    cells = (FR, ROWS, COLS, CH)
    wide = (FR, CH)
    swap = [(0, 1), (1, 0)]
    dma = pltpu.SemaphoreType.DMA

    inner, outer, stats = call(
        edges_and_sums,
        [
            ((2 * HALO + 1, COLS, CH), BF16),
            ((2 * HALO, COLS, CH), BF16),
            ((FR, 128), F32),
        ],
        (x, g),
        [HBM] * 2,
        [
            pltpu.VMEM(cells, BF16),
            pltpu.VMEM((FR, 128), F32),
            pltpu.VMEM((1, TERMS, CH), BF16),
            dma((7,)),
        ],
    )
    stats, counts = lax.optimization_barrier((stats, frame_counts))
    live = jnp.broadcast_to(jnp.arange(FR)[:, None] < counts[0], wide).astype(F32)
    hp = lax.ppermute(inner, "c", swap)
    hn = lax.ppermute(
        outer,
        space,
        [(i, i - 1 if i % 2 == 0 else i + 1) for i in range(1, SPACE - 1)],
    )
    (stats,) = run(
        pair_sums,
        [((NY * NZ, FR, 128), F32)],
        (stats, hp),
        rows={1: (2 * HALO, 2 * HALO + 1)},
    )
    stats = lax.all_to_all(stats, ("y", "z"), 0, 0)
    block = (BLOCK, BSL)
    packed = call(
        pack_body,
        [(block, BF16)] * NY,
        (x, stay_out(output_grad.reshape(GROWS, CH)), hp, hn),
        [HBM] * 4,
        [pltpu.VMEM(cells, BF16)]
        + [pltpu.VMEM((HALO, COLS, CH), BF16)] * 2
        + [pltpu.VMEM((NY, AROWS, BSL), BF16), dma((3 + NC * NY + NY,))],
    )
    near = [packed[0]] + [
        lax.ppermute(packed[d], "y", [(i, (i + d) % NY) for i in range(NY)]) for d in range(1, NY)
    ]
    conv_flops = 16 * TAPS * FR * CELLS * CH * CH
    padded = pltpu.VMEM((3, FR + 2, 4, COLS, CH), BF16)
    terms, scaled, mean, inv = run(
        backward_terms,
        [((NY * NC, FR, 128), F32), ((FR, CELLS, CH), F32), (wide, F32), (wide, F32)],
        (g, hp, hn, conv_kernel, live, stats, x, gain),
        rows={1: (HALO, 2 * HALO), 2: (HALO, 2 * HALO)},
        scratch=[padded],
        late=3,
    )
    *moved, terms = lax.optimization_barrier((*near[1:], terms))
    near = [near[0], *moved]
    terms = lax.all_to_all(terms, ("y", "c"), 0, 0)
    far = [lax.ppermute(a, "c", swap) for a in near]
    part = (NZ, PROWS, CH)
    whole_part = (NZ, PROWS + TERMS, CH)
    (partial,) = call(
        kernel_part,
        [(whole_part, BF16)],
        (*near, *far, mean, inv, gain, live),
        [HBM] * 12,
        [
            pltpu.VMEM((8, BLOCK, BSL), BF16),
            pltpu.VMEM(wide, F32),
            pltpu.VMEM(wide, F32),
            pltpu.VMEM((1, CH), F32),
            pltpu.VMEM(wide, F32),
            pltpu.VMEM(part, BF16),
            pltpu.VMEM((3, FR, NY, 6, COLS, Q * APART), BF16),
            pltpu.VMEM((FR, NY, 4, COLS, CH), BF16),
            pltpu.VMEM(part, F32),
            dma((12,)),
        ],
        flops=conv_flops,
    )
    (merged,) = call(
        add_sums,
        [(whole_part, BF16)],
        (partial, terms),
        [HBM] * 2,
        [pltpu.VMEM((NY * NC, FR, 128), F32), pltpu.VMEM((NZ, TERMS, CH), BF16), dma((2,))],
        aliases={0: 0},
    )
    merged, late_mean = lax.optimization_barrier((merged, mean))
    merged = lax.all_to_all(merged, "z", 0, 0)
    (block_output,) = run(
        forward_conv,
        [(cells, BF16)],
        (x, hp, hn, late_mean, inv, gain, conv_kernel, live),
        rows={1: (0, HALO), 2: (0, HALO)},
        scratch=[padded],
        late=6,
        flops=conv_flops,
    )
    merged, block_output = lax.optimization_barrier((merged, block_output))
    rows, sums = run(sum_rows, [((PROWS, CH), jnp.int16), ((FR, 128), F32)], (merged,))
    others = [rows] + [
        lax.ppermute(rows, "x", [(i, (i + d) % NX) for i in range(NX)]) for d in range(1, NX)
    ]
    (input_grad,) = run(
        finish_input, [(cells, BF16)], (sums, scaled, x, g, mean, inv, live)
    )
    kernel_grad, gain_grad = call(
        sum_clips,
        [((TAPS, 4, CH), F32), ((1, CH), F32)],
        others,
        [HBM] * 4,
        [
            pltpu.VMEM((NX, PROWS, CH), jnp.int16),
            pltpu.VMEM((TAPS, 4, CH), F32),
            pltpu.VMEM((1, CH), F32),
            dma((6,)),
        ],
    )
    whole = (1,) + cells
    return (
        block_output.reshape(whole),
        input_grad.reshape(whole),
        jnp.swapaxes(kernel_grad, 0, 1),
        gain_grad.reshape(CH),
    )


def solution(mesh):
    fine = Mesh(mesh.devices.reshape(NX, NY, NZ, NC), ("x", "y", "z", "c"))
    space = ("y", "z", "c")
    cells = P("x", None, space, None, None)
    return jax.shard_map(
        local,
        mesh=fine,
        in_specs=(cells, P("x"), P(), P(), cells),
        out_specs=(cells, cells, P(space, None, None), P()),
        check_vma=False,
    )
```

```python
import jax
import jax.numpy as jnp
from jax import lax
from jax.experimental import pallas as pl
from jax.experimental.pallas import tpu as pltpu
from jax.sharding import Mesh
from jax.sharding import PartitionSpec as P

F32 = jnp.float32
BF16 = jnp.bfloat16
NX, NY, NZ, NC = 4, 4, 8, 2
SPACE = NY * NZ * NC
FR, ROWS, COLS, CH = 8, 2, 16, 256
CELLS = ROWS * COLS
GROUPS = 32
GC = CH // GROUPS
ASL = CH // NY
BSL = CH // NC
EPSILON = 1e-05
COUNT = CELLS * SPACE * GC
AROWS = FR // 2 * 3 * COLS
GROWS = FR * ROWS * COLS
TAPS = 27
PROWS = 112
Q = 4
APART = ASL // NC
BLOCK = AROWS + NC * GROWS
TERMS = 16
STEPS = 32000.0
HALO = FR
HI = lax.Precision.HIGHEST


def hdot(a, b):
    return jnp.dot(a, b, preferred_element_type=F32, precision=HI)


def gather_matrix():
    lane = lax.broadcasted_iota(jnp.int32, (CH, GROUPS), 0)
    group = lax.broadcasted_iota(jnp.int32, (CH, GROUPS), 1)
    return (lane // GC == group).astype(F32)


def spread_matrix():
    group = lax.broadcasted_iota(jnp.int32, (GROUPS, CH), 0)
    lane = lax.broadcasted_iota(jnp.int32, (GROUPS, CH), 1)
    return (lane // GC == group).astype(F32)


def shifted(cells, k):
    if k == 1:
        return cells
    zero = jnp.zeros(cells.shape[:-2] + (1, cells.shape[-1]), cells.dtype)
    if k == 0:
        return jnp.concatenate([zero, cells[..., :-1, :]], axis=-2)
    return jnp.concatenate([cells[..., 1:, :], zero], axis=-2)


def edges_and_sums(x_h, g_h, in_h, out_h, st_h, x_ref, st_ref, term_ref, sem):
    c_at = lax.axis_index("c")
    load = pltpu.make_async_copy(x_h, x_ref, sem.at[0])
    load.start()
    halo = []
    for n, source in enumerate((x_h, g_h)):
        part = slice(n * FR, (n + 1) * FR)
        halo.append(pltpu.make_async_copy(source.at[:, 1 - c_at], in_h.at[part], sem.at[1 + 2 * n]))
        halo.append(pltpu.make_async_copy(source.at[:, c_at], out_h.at[part], sem.at[2 + 2 * n]))
    for copy in halo:
        copy.start()
    load.wait()
    xf = x_ref[...].astype(F32).reshape(FR, CELLS, CH)
    gather = gather_matrix()
    mean = hdot(jnp.sum(xf, axis=1), gather) / (CELLS * GC)
    centered = xf - hdot(mean, spread_matrix())[:, None, :]
    squares = hdot(jnp.sum(centered * centered, axis=1), gather)
    sums = jnp.concatenate([mean, squares, jnp.zeros((FR, 2 * GROUPS), F32)], axis=1)
    st_ref[...] = sums
    term_ref[0] = as_terms(sums)
    halo.append(pltpu.make_async_copy(term_ref, in_h.at[2 * FR :], sem.at[5]))
    halo.append(pltpu.make_async_copy(st_ref, st_h, sem.at[6]))
    for copy in halo[4:]:
        copy.start()
    for copy in halo:
        copy.wait()


def outside(in_ref, out_ref):
    first = lax.axis_index("c") == 0
    inner = in_ref[...].reshape(FR, COLS, CH)
    outer = out_ref[...].reshape(FR, COLS, CH)
    return jnp.where(first, outer, inner), jnp.where(first, inner, outer)


def combined(parts, squares, each):
    count = parts.shape[0]
    mean = jnp.sum(parts, axis=0) / count
    apart = parts - mean[None]
    return mean, jnp.sum(squares + each * (apart * apart), axis=0)


def pair_sums(own_ref, other_ref, out_ref):
    both = jnp.stack([own_ref[...], from_terms(other_ref[0].astype(F32))])
    mean, squares = combined(both[:, :, :GROUPS], both[:, :, GROUPS : 2 * GROUPS], CELLS * GC)
    row = jnp.concatenate([mean, squares, jnp.zeros((FR, 2 * GROUPS), F32)], axis=1)
    out_ref[...] = jnp.broadcast_to(row[None], (NY * NZ, FR, 128))


def as_terms(values):
    high = values.astype(BF16).astype(F32)
    middle = (values - high).astype(BF16).astype(F32)
    low = values - high - middle
    upper = jnp.concatenate([high, middle], axis=1)
    lower = jnp.concatenate([low, jnp.zeros((FR, 128), F32)], axis=1)
    return jnp.concatenate([upper, lower], axis=0).astype(BF16)


def from_terms(terms):
    return (terms[FR:, :128] + terms[:FR, 128:]) + terms[:FR, :128]


def pack_slices(x_ref, hp_ref, hn_ref, out_ref):
    upper = lax.axis_index("c") == 0
    own = [x_ref[:, 0], x_ref[:, 1]]
    before, after = outside(hp_ref, hn_ref)
    rows = [
        jnp.where(upper, before, own[0]),
        jnp.where(upper, own[0], own[1]),
        jnp.where(upper, own[1], after),
    ]
    three = jnp.stack(rows, axis=1).reshape(FR // 2, 2, 3, COLS, CH)
    for y in range(NY):
        part = three[..., y * ASL : (y + 1) * ASL]
        pair = jnp.concatenate([part[:, 0], part[:, 1]], axis=-1)
        out_ref[y] = pair.reshape(AROWS, 2 * ASL)


def backward_conv(g_ref, hp_ref, hn_ref, k_ref, live_ref, pad_ref, held):
    live = live_ref[...][:, None, :]
    before, after = outside(hp_ref, hn_ref)
    rows = [before, g_ref[:, 0], g_ref[:, 1], after]
    for r in range(4):
        cells = rows[r].astype(F32) * live
        for k in range(3):
            pad_ref[k, :FR, r] = shifted(cells, k).astype(BF16)
    pad_ref[:, FR:] = jnp.zeros((3, 2, 4, COLS, CH), BF16)
    held.wait()
    total = jnp.zeros((FR * CELLS, CH), F32)
    for i in range(3):
        for j in range(3):
            for k in range(3):
                window = pad_ref[2 - k, 2 - i : 2 - i + FR, 2 - j : 4 - j]
                total = total + lax.dot_general(
                    window.reshape(FR * CELLS, CH),
                    k_ref[(i * 3 + j) * 3 + k],
                    (((1,), (1,)), ((), ())),
                    preferred_element_type=F32,
                )
    return total


def backward_terms(
    g_ref, hp_ref, hn_ref, k_ref, live_ref, st_ref, x_ref, gain_ref,
    out_ref, sc_ref, mean_ref, inv_ref, pad_ref, held,
):
    act_grad = backward_conv(g_ref, hp_ref, hn_ref, k_ref, live_ref, pad_ref, held)
    mean, whole = combined(
        st_ref[:, :FR, :GROUPS], st_ref[:, :FR, GROUPS : 2 * GROUPS], NC * CELLS * GC
    )
    spread = spread_matrix()
    mean_all = hdot(mean, spread)
    inv_all = hdot(lax.rsqrt(whole / COUNT + EPSILON), spread)
    mean_ref[...] = mean_all
    inv_ref[...] = inv_all
    gain = gain_ref[...][None]
    xf = x_ref[...].astype(F32).reshape(FR, CELLS, CH)
    normalized = (xf - mean_all[:, None, :]) * inv_all[:, None, :]
    gated = normalized * gain
    sig = jax.nn.sigmoid(gated)
    pre = act_grad.reshape(FR, CELLS, CH) * sig * (1.0 + gated * (1.0 - sig))
    scaled = pre * gain
    sc_ref[...] = scaled
    gather = gather_matrix()
    first = hdot(jnp.sum(scaled, axis=1), gather)
    by_channel = jnp.sum(pre * normalized, axis=1)
    second = hdot(by_channel * gain_ref[...], gather)
    gain_part = jnp.sum(by_channel, axis=0, keepdims=True)
    row = lax.broadcasted_iota(jnp.int32, (FR, CH), 0)
    lane = lax.broadcasted_iota(jnp.int32, (FR, CH), 1)
    folded = jnp.where(lane // GROUPS == row, jnp.broadcast_to(gain_part, (FR, CH)), 0.0)
    fold_lane = lax.broadcasted_iota(jnp.int32, (CH, GROUPS), 0)
    fold_at = lax.broadcasted_iota(jnp.int32, (CH, GROUPS), 1)
    folded = hdot(folded, (fold_lane % GROUPS == fold_at).astype(F32))
    everything = jnp.concatenate([first, second, folded, jnp.zeros((FR, GROUPS), F32)], axis=1)
    out_ref[...] = jnp.broadcast_to(everything[None], (NY * NC, FR, 128))


def kernel_part(*refs):
    blocks, (mean_h, inv_h, gain_h, live_h, out_h) = refs[:8], refs[8:13]
    in_ref, mean_ref, inv_ref, gain_ref, live_ref, out_ref, pad_ref, grad_ref, sum_ref, sem = refs[13:]
    y_at, z_at, c_at = lax.axis_index("y"), lax.axis_index("z"), lax.axis_index("c")
    pairs = [(blocks[n].at[:AROWS], in_ref.at[n, :AROWS]) for n in range(8)]
    pairs += [(mean_h, mean_ref), (inv_h, inv_ref), (gain_h, gain_ref), (live_h, live_ref)]
    pairs += [(blocks[n].at[AROWS:], in_ref.at[n, AROWS:]) for n in range(8)]
    copies = [pltpu.make_async_copy(a, b, sem.at[n]) for n, (a, b) in enumerate(pairs)]
    for copy in copies:
        copy.start()
    for copy in copies[8:12]:
        copy.wait()
    width = Q * APART
    lane = lax.broadcasted_iota(jnp.int32, (CH, width), 0)
    slot = lax.broadcasted_iota(jnp.int32, (CH, width), 1)
    channel = GC * ((slot % APART) // 4) + 4 * c_at + slot % 4
    pick = (lane == y_at * ASL + channel).astype(F32)
    mean2 = hdot(mean_ref[...], pick)
    inv2 = hdot(inv_ref[...], pick)
    gain2 = hdot(gain_ref[...], pick)
    live = live_ref[:, :BSL].astype(BF16)[:, None, None, :]
    quarter = lax.broadcasted_iota(jnp.int32, (1, width), 1) // APART
    centers, scales = [], []
    for u in range(2):
        center, scale = mean2[4 * u : 4 * u + 1], inv2[4 * u : 4 * u + 1]
        for q in range(1, Q):
            center = jnp.where(quarter == q, mean2[4 * u + q : 4 * u + q + 1], center)
            scale = jnp.where(quarter == q, inv2[4 * u + q : 4 * u + q + 1], scale)
        centers.append(center)
        scales.append(scale * gain2)
    lane = lax.broadcasted_iota(jnp.int32, (2 * ASL, width), 0)
    slot = lax.broadcasted_iota(jnp.int32, (2 * ASL, width), 1)
    channel = GC * ((slot % APART) // 4) + 4 * c_at + slot % 4
    chosen = [
        (lane == (slot // APART - 2 * half) * ASL + channel).astype(BF16) for half in range(2)
    ]
    shape = (3, COLS, width)
    place = lax.broadcasted_iota(jnp.int32, shape, 2) // APART
    row = lax.broadcasted_iota(jnp.int32, shape, 0)
    block = 3 * COLS
    for copy in copies[:8]:
        copy.wait()
    for n in range(8):
        d = n % 4
        y = lax.rem(y_at + NY - d, NY)
        c = c_at if n < 4 else 1 - c_at
        top = (y == 0) & (z_at == 0) & (c == 0)
        bottom = (y == NY - 1) & (z_at == NZ - 1) & (c == NC - 1)
        edge = jnp.where(top, 0, jnp.where(bottom, 2, 3))
        inside = (row != edge).astype(F32)
        acts = []
        for u in range(2):
            at = 2 * u * block
            raw = jnp.dot(
                in_ref[n, at : at + block], chosen[0], preferred_element_type=F32
            ) + jnp.dot(
                in_ref[n, at + block : at + 2 * block], chosen[1], preferred_element_type=F32
            )
            gated = (raw - centers[u]) * scales[u]
            acts.append((gated * jax.nn.sigmoid(gated)).reshape(shape) * inside)
        a, b = acts
        a1, a2, b1 = pltpu.roll(a, 32, 2), pltpu.roll(a, 64, 2), pltpu.roll(b, 32, 2)
        b2 = pltpu.roll(b, 64, 2)
        frames = [
            jnp.where(place < 2, 0.0, a2),
            jnp.where(place < 1, 0.0, a1),
            a,
            pltpu.roll(a, 96, 2),
            jnp.where(place < 2, a2, b2),
            jnp.where(place < 1, a1, b1),
            b,
            pltpu.roll(b, 96, 2),
        ]
        for f in range(FR):
            for k in range(3):
                pad_ref[k, f, d, pl.ds(3 * c, 3)] = shifted(frames[f], k).astype(BF16)
    for copy in copies[12:]:
        copy.wait()
    for n in range(8):
        d = n % 4
        c = c_at if n < 4 else 1 - c_at
        for h in range(NC):
            at = AROWS + h * GROWS
            cells = in_ref[n, at : at + GROWS].reshape(FR, ROWS, COLS, BSL) * live
            grad_ref[:, d, pl.ds(2 * c, 2), :, h * BSL : (h + 1) * BSL] = cells
    cells = FR * NY * 4 * COLS
    turned_grad = grad_ref[...].reshape(cells, CH).T
    sum_ref[:, 4 * TAPS :] = jnp.zeros((NZ, PROWS - 4 * TAPS, CH), F32)
    combos = [(j, k) for j in range(3) for k in range(3)]
    for first in range(0, 9, 2):
        group = combos[first : first + 2]
        windows = [pad_ref[k, :, :, j : j + 4].reshape(cells, width) for j, k in group]
        window = windows[0] if len(windows) == 1 else jnp.concatenate(windows, axis=1)
        product = jnp.dot(turned_grad, window, preferred_element_type=F32)
        product = product.astype(BF16).T.astype(F32)
        for n, (j, k) in enumerate(group):
            for i in range(3):
                tap = (i * 3 + j) * 3 + k
                at = n * width + i * APART
                piece = product[at : at + APART].reshape(NZ, 4, CH)
                sum_ref[:, tap * 4 : tap * 4 + 4] = piece
    out_ref[...] = sum_ref[...].astype(BF16)
    copy = pltpu.make_async_copy(out_ref, out_h.at[:, :PROWS], sem.at[0])
    copy.start()
    copy.wait()


def add_sums(part_h, b_h, out_h, b_ref, out_ref, sem):
    copy = pltpu.make_async_copy(b_h, b_ref, sem.at[0])
    copy.start()
    copy.wait()
    terms = as_terms(jnp.sum(b_ref[...], axis=0))
    out_ref[...] = jnp.broadcast_to(terms[None], (NZ, TERMS, CH))
    copy = pltpu.make_async_copy(out_ref, out_h.at[:, PROWS:], sem.at[1])
    copy.start()
    copy.wait()


def scale_of(values):
    most = jnp.max(jnp.max(jnp.abs(values), axis=0, keepdims=True), axis=1, keepdims=True)
    most = jnp.broadcast_to(jnp.maximum(most, 1e-36), (1, CH))
    return jnp.ceil(jnp.log2(most))


def sum_rows(in_ref, out_ref, sums_ref):
    total = jnp.sum(in_ref[...].astype(F32), axis=0)
    sums = from_terms(total[PROWS:])
    sums_ref[...] = sums
    fold_at = lax.broadcasted_iota(jnp.int32, (GROUPS, CH), 0)
    fold_lane = lax.broadcasted_iota(jnp.int32, (GROUPS, CH), 1)
    wide = hdot(sums[:, 2 * GROUPS : 3 * GROUPS], (fold_lane % GROUPS == fold_at).astype(F32))
    row = lax.broadcasted_iota(jnp.int32, (FR, CH), 0)
    lane = lax.broadcasted_iota(jnp.int32, (FR, CH), 1)
    gain = jnp.sum(jnp.where(lane // GROUPS == row, wide, 0.0), axis=0, keepdims=True)
    part = total[: 4 * TAPS]
    exponent, gain_exponent = scale_of(part), scale_of(gain)
    code = jnp.floor(part / jnp.exp2(exponent) * STEPS + 0.5)
    steps = gain / jnp.exp2(gain_exponent) * STEPS
    upper = jnp.floor(steps + 0.5)
    lower = jnp.floor((steps - upper) * STEPS + 0.5)
    rows = jnp.concatenate([code, upper, lower, exponent, gain_exponent], axis=0)
    out_ref[...] = rows.astype(jnp.int32).astype(jnp.int16)


def forward_conv(x_ref, hp_ref, hn_ref, mean_ref, inv_ref, gain_ref, k_ref, live_ref, out_ref, pad_ref, held):
    s_at = (lax.axis_index("y") * NZ + lax.axis_index("z")) * NC + lax.axis_index("c")
    before, after = outside(hp_ref, hn_ref)
    rows = [before, x_ref[:, 0], x_ref[:, 1], after]
    mean = mean_ref[...][:, None, :]
    inv = inv_ref[...][:, None, :]
    gain = gain_ref[...][None]
    for r in range(4):
        gated = (rows[r].astype(F32) - mean) * inv * gain
        act = gated * jax.nn.sigmoid(gated)
        if r == 0:
            act = jnp.where(s_at == 0, 0.0, act)
        if r == 3:
            act = jnp.where(s_at == SPACE - 1, 0.0, act)
        for k in range(3):
            pad_ref[k, 2:, r] = shifted(act, k).astype(BF16)
    pad_ref[:, :2] = jnp.zeros((3, 2, 4, COLS, CH), BF16)
    held.wait()
    total = jnp.zeros((FR * CELLS, CH), F32)
    for i in range(3):
        for j in range(3):
            for k in range(3):
                window = pad_ref[k, i : i + FR, j : j + 2]
                total = total + jnp.dot(
                    window.reshape(FR * CELLS, CH),
                    k_ref[(i * 3 + j) * 3 + k],
                    preferred_element_type=F32,
                )
    cells = total.reshape(FR, CELLS, CH) + x_ref[...].astype(F32).reshape(FR, CELLS, CH)
    cells = cells * live_ref[...][:, None, :]
    out_ref[...] = cells.astype(BF16).reshape(FR, ROWS, COLS, CH)


def finish_input(sums_ref, sc_ref, x_ref, g_ref, mean_ref, inv_ref, live_ref, out_ref):
    sums = sums_ref[...]
    spread = spread_matrix()
    first = hdot(sums[:, :GROUPS] / COUNT, spread)[:, None, :]
    second = hdot(sums[:, GROUPS : 2 * GROUPS] / COUNT, spread)[:, None, :]
    inv = inv_ref[...][:, None, :]
    xf = x_ref[...].astype(F32).reshape(FR, CELLS, CH)
    normalized = (xf - mean_ref[...][:, None, :]) * inv
    norm_grad = inv * (sc_ref[...] - first - normalized * second)
    grad = g_ref[...].astype(F32).reshape(FR, CELLS, CH) * live_ref[...][:, None, :]
    out_ref[...] = (grad + norm_grad).astype(BF16).reshape(FR, ROWS, COLS, CH)


def sum_clips(own_h, one_h, two_h, three_h, kg_h, gain_h, in_ref, kg_ref, gain_ref, sem):
    x_at = lax.axis_index("x")
    copies = []
    for d, src in enumerate((own_h, one_h, two_h, three_h)):
        copies.append(
            pltpu.make_async_copy(src, in_ref.at[lax.rem(x_at + NX - d, NX)], sem.at[d])
        )
    for copy in copies:
        copy.start()
    for copy in copies:
        copy.wait()
    total = jnp.zeros((4 * TAPS, CH), F32)
    gain = jnp.zeros((1, CH), F32)
    at = 4 * TAPS
    for n in range(NX):
        rows = in_ref[n].astype(jnp.int32).astype(F32)
        total = total + rows[:at] / STEPS * jnp.exp2(rows[at + 2 : at + 3])
        steps = rows[at : at + 1] + rows[at + 1 : at + 2] / STEPS
        gain = gain + steps / STEPS * jnp.exp2(rows[at + 3 : at + 4])
    for tap in range(TAPS):
        kg_ref[tap] = total[4 * tap : 4 * tap + 4]
    gain_ref[...] = gain
    out = (
        pltpu.make_async_copy(kg_ref, kg_h, sem.at[4]),
        pltpu.make_async_copy(gain_ref, gain_h, sem.at[5]),
    )
    for copy in out:
        copy.start()
    for copy in out:
        copy.wait()


HBM = pl.BlockSpec(memory_space=pltpu.HBM)
SMEM = pl.BlockSpec(memory_space=pltpu.SMEM)


def stay_out(array):
    return pltpu.with_memory_space_constraint(array, pltpu.HBM)


def shapes(outs):
    return tuple(jax.ShapeDtypeStruct(s, d) for s, d in outs)


def call(body, outs, args, specs, scratch, flops=0, limit=32, aliases={}):
    return pl.pallas_call(
        body,
        out_shape=shapes(outs),
        in_specs=specs,
        out_specs=tuple(HBM for _ in outs),
        scratch_shapes=list(scratch),
        input_output_aliases=aliases,
        compiler_params=pltpu.CompilerParams(vmem_limit_bytes=limit * 2**20),
        cost_estimate=pl.CostEstimate(flops=flops, bytes_accessed=2**20, transcendentals=0),
        name=body.__name__,
    )(*args)


def run(body, outs, args, scratch=(), late=None, smem=(), flops=0, rows={}):
    count, outputs = len(args), len(outs)
    moved = [at for at in range(count) if at not in smem]

    def kernel(*refs):
        ins, targets = list(refs[:count]), refs[count : count + outputs]
        rest = refs[count + outputs :]
        buffers, rest = rest[: len(moved)], rest[len(moved) :]
        results, rest = rest[:outputs], rest[outputs:]
        sem, extra = rest[0], rest[1:]
        copies = [
            pltpu.make_async_copy(
                ins[at].at[rows[at][0] : rows[at][1]] if at in rows else ins[at], buffers[n], sem.at[n]
            )
            for n, at in enumerate(moved)
        ]
        held = copies.pop(moved.index(late)) if late is not None else None
        for copy in copies + ([held] if held is not None else []):
            copy.start()
        for n, at in enumerate(moved):
            ins[at] = buffers[n]
        for copy in copies:
            copy.wait()
        if held is None:
            body(*ins, *results, *extra)
        else:
            body(*ins, *results, *extra, held)
        copies = [
            pltpu.make_async_copy(results[n], targets[n], sem.at[len(moved) + n])
            for n in range(outputs)
        ]
        for copy in copies:
            copy.start()
        for copy in copies:
            copy.wait()

    kernel.__name__ = body.__name__
    specs = [SMEM if at in smem else HBM for at in range(count)]
    buffers = []
    for at in moved:
        shape = args[at].shape
        if at in rows:
            shape = (rows[at][1] - rows[at][0],) + shape[1:]
        buffers.append(pltpu.VMEM(shape, args[at].dtype))
    buffers += [pltpu.VMEM(s, d) for s, d in outs]
    buffers += [pltpu.SemaphoreType.DMA((len(moved) + outputs,))]
    return call(kernel, outs, args, specs, buffers + list(scratch), flops)


def pack_body(x_h, g_h, hp_h, hn_h, *refs):
    outs = refs[:NY]
    x_ref, hp_ref, hn_ref, buf, sem = refs[NY:]
    pairs = ((x_h, x_ref), (hp_h.at[:HALO], hp_ref), (hn_h.at[:HALO], hn_ref))
    copies = [pltpu.make_async_copy(a, b, sem.at[n]) for n, (a, b) in enumerate(pairs)]
    for copy in copies:
        copy.start()
    straight = []
    for d, out in enumerate(outs):
        for c in range(NC):
            at = AROWS + c * GROWS
            straight.append(
                pltpu.make_async_copy(
                    g_h.at[:, c * BSL : (c + 1) * BSL],
                    out.at[at : at + GROWS],
                    sem.at[3 + NC * d + c],
                )
            )
    for copy in straight:
        copy.start()
    for copy in copies:
        copy.wait()
    pack_slices(x_ref, hp_ref, hn_ref, buf)
    y_at = lax.axis_index("y")
    copies = [
        pltpu.make_async_copy(
            buf.at[lax.rem(y_at + d, NY)], out.at[:AROWS], sem.at[3 + NC * NY + d]
        )
        for d, out in enumerate(outs)
    ]
    for copy in copies:
        copy.start()
    for copy in straight + copies:
        copy.wait()


def local(video_latent, frame_counts, conv_kernel, norm_gain, output_grad):
    x = stay_out(video_latent.reshape(FR, ROWS, COLS, CH))
    g = stay_out(output_grad.reshape(FR, ROWS, COLS, CH))
    gain = stay_out(norm_gain.reshape(1, CH))
    conv_kernel = stay_out(conv_kernel)
    space = ("y", "z", "c")
    cells = (FR, ROWS, COLS, CH)
    wide = (FR, CH)
    swap = [(0, 1), (1, 0)]
    dma = pltpu.SemaphoreType.DMA

    inner, outer, stats = call(
        edges_and_sums,
        [
            ((2 * HALO + 1, COLS, CH), BF16),
            ((2 * HALO, COLS, CH), BF16),
            ((FR, 128), F32),
        ],
        (x, g),
        [HBM] * 2,
        [
            pltpu.VMEM(cells, BF16),
            pltpu.VMEM((FR, 128), F32),
            pltpu.VMEM((1, TERMS, CH), BF16),
            dma((7,)),
        ],
    )
    stats, counts = lax.optimization_barrier((stats, frame_counts))
    live = jnp.broadcast_to(jnp.arange(FR)[:, None] < counts[0], wide).astype(F32)
    hp = lax.ppermute(inner, "c", swap)
    hn = lax.ppermute(
        outer,
        space,
        [(i, i - 1 if i % 2 == 0 else i + 1) for i in range(1, SPACE - 1)],
    )
    (stats,) = run(
        pair_sums,
        [((NY * NZ, FR, 128), F32)],
        (stats, hp),
        rows={1: (2 * HALO, 2 * HALO + 1)},
    )
    stats = lax.all_to_all(stats, ("y", "z"), 0, 0)
    block = (BLOCK, BSL)
    packed = call(
        pack_body,
        [(block, BF16)] * NY,
        (x, stay_out(output_grad.reshape(GROWS, CH)), hp, hn),
        [HBM] * 4,
        [pltpu.VMEM(cells, BF16)]
        + [pltpu.VMEM((HALO, COLS, CH), BF16)] * 2
        + [pltpu.VMEM((NY, AROWS, BSL), BF16), dma((3 + NC * NY + NY,))],
    )
    near = [packed[0]] + [
        lax.ppermute(packed[d], "y", [(i, (i + d) % NY) for i in range(NY)]) for d in range(1, NY)
    ]
    conv_flops = 16 * TAPS * FR * CELLS * CH * CH
    padded = pltpu.VMEM((3, FR + 2, 4, COLS, CH), BF16)
    terms, scaled, mean, inv = run(
        backward_terms,
        [((NY * NC, FR, 128), F32), ((FR, CELLS, CH), F32), (wide, F32), (wide, F32)],
        (g, hp, hn, conv_kernel, live, stats, x, gain),
        rows={1: (HALO, 2 * HALO), 2: (HALO, 2 * HALO)},
        scratch=[padded],
        late=3,
    )
    *moved, terms = lax.optimization_barrier((*near[1:], terms))
    near = [near[0], *moved]
    terms = lax.all_to_all(terms, ("y", "c"), 0, 0)
    far = [lax.ppermute(a, "c", swap) for a in near]
    part = (NZ, PROWS, CH)
    whole_part = (NZ, PROWS + TERMS, CH)
    (partial,) = call(
        kernel_part,
        [(whole_part, BF16)],
        (*near, *far, mean, inv, gain, live),
        [HBM] * 12,
        [
            pltpu.VMEM((8, BLOCK, BSL), BF16),
            pltpu.VMEM(wide, F32),
            pltpu.VMEM(wide, F32),
            pltpu.VMEM((1, CH), F32),
            pltpu.VMEM(wide, F32),
            pltpu.VMEM(part, BF16),
            pltpu.VMEM((3, FR, NY, 6, COLS, Q * APART), BF16),
            pltpu.VMEM((FR, NY, 4, COLS, CH), BF16),
            pltpu.VMEM(part, F32),
            dma((20,)),
        ],
        flops=conv_flops,
    )
    (merged,) = call(
        add_sums,
        [(whole_part, BF16)],
        (partial, terms),
        [HBM] * 2,
        [pltpu.VMEM((NY * NC, FR, 128), F32), pltpu.VMEM((NZ, TERMS, CH), BF16), dma((2,))],
        aliases={0: 0},
    )
    merged, late_mean = lax.optimization_barrier((merged, mean))
    merged = lax.all_to_all(merged, "z", 0, 0)
    (block_output,) = run(
        forward_conv,
        [(cells, BF16)],
        (x, hp, hn, late_mean, inv, gain, conv_kernel, live),
        rows={1: (0, HALO), 2: (0, HALO)},
        scratch=[padded],
        late=6,
        flops=conv_flops,
    )
    merged, block_output = lax.optimization_barrier((merged, block_output))
    rows, sums = run(sum_rows, [((PROWS, CH), jnp.int16), ((FR, 128), F32)], (merged,))
    others = [rows] + [
        lax.ppermute(rows, "x", [(i, (i + d) % NX) for i in range(NX)]) for d in range(1, NX)
    ]
    (input_grad,) = run(
        finish_input, [(cells, BF16)], (sums, scaled, x, g, mean, inv, live)
    )
    kernel_grad, gain_grad = call(
        sum_clips,
        [((TAPS, 4, CH), F32), ((1, CH), F32)],
        others,
        [HBM] * 4,
        [
            pltpu.VMEM((NX, PROWS, CH), jnp.int16),
            pltpu.VMEM((TAPS, 4, CH), F32),
            pltpu.VMEM((1, CH), F32),
            dma((6,)),
        ],
    )
    whole = (1,) + cells
    return (
        block_output.reshape(whole),
        input_grad.reshape(whole),
        jnp.swapaxes(kernel_grad, 0, 1),
        gain_grad.reshape(CH),
    )


def solution(mesh):
    fine = Mesh(mesh.devices.reshape(NX, NY, NZ, NC), ("x", "y", "z", "c"))
    space = ("y", "z", "c")
    cells = P("x", None, space, None, None)
    return jax.shard_map(
        local,
        mesh=fine,
        in_specs=(cells, P("x"), P(), P(), cells),
        out_specs=(cells, cells, P(space, None, None), P()),
        check_vma=False,
    )
```

```python
import jax
import jax.numpy as jnp
from jax import lax
from jax.experimental import pallas as pl
from jax.experimental.pallas import tpu as pltpu
from jax.sharding import Mesh
from jax.sharding import PartitionSpec as P

F32 = jnp.float32
BF16 = jnp.bfloat16
NX, NY, NZ, NC = 4, 4, 8, 2
SPACE = NY * NZ * NC
FR, ROWS, COLS, CH = 8, 2, 16, 256
CELLS = ROWS * COLS
GROUPS = 32
GC = CH // GROUPS
ASL = CH // NY
BSL = CH // NC
EPSILON = 1e-05
COUNT = CELLS * SPACE * GC
AROWS = FR // 2 * 3 * COLS
GROWS = FR * ROWS * COLS
TAPS = 27
PROWS = 112
Q = 4
APART = ASL // NC
BLOCK = AROWS + NC * GROWS
TERMS = 16
STEPS = 32000.0
HALO = FR
HI = lax.Precision.HIGHEST


def hdot(a, b):
    return jnp.dot(a, b, preferred_element_type=F32, precision=HI)


def gather_matrix():
    lane = lax.broadcasted_iota(jnp.int32, (CH, GROUPS), 0)
    group = lax.broadcasted_iota(jnp.int32, (CH, GROUPS), 1)
    return (lane // GC == group).astype(F32)


def spread_matrix():
    group = lax.broadcasted_iota(jnp.int32, (GROUPS, CH), 0)
    lane = lax.broadcasted_iota(jnp.int32, (GROUPS, CH), 1)
    return (lane // GC == group).astype(F32)


def shifted(cells, k):
    if k == 1:
        return cells
    zero = jnp.zeros(cells.shape[:-2] + (1, cells.shape[-1]), cells.dtype)
    if k == 0:
        return jnp.concatenate([zero, cells[..., :-1, :]], axis=-2)
    return jnp.concatenate([cells[..., 1:, :], zero], axis=-2)


def edges_and_sums(x_h, g_h, in_h, out_h, st_h, x_ref, st_ref, term_ref, sem):
    c_at = lax.axis_index("c")
    load = pltpu.make_async_copy(x_h, x_ref, sem.at[0])
    load.start()
    halo = []
    for n, source in enumerate((x_h, g_h)):
        part = slice(n * FR, (n + 1) * FR)
        halo.append(pltpu.make_async_copy(source.at[:, 1 - c_at], in_h.at[part], sem.at[1 + 2 * n]))
        halo.append(pltpu.make_async_copy(source.at[:, c_at], out_h.at[part], sem.at[2 + 2 * n]))
    for copy in halo:
        copy.start()
    load.wait()
    xf = x_ref[...].astype(F32).reshape(FR, CELLS, CH)
    gather = gather_matrix()
    mean = hdot(jnp.sum(xf, axis=1), gather) / (CELLS * GC)
    centered = xf - hdot(mean, spread_matrix())[:, None, :]
    squares = hdot(jnp.sum(centered * centered, axis=1), gather)
    sums = jnp.concatenate([mean, squares, jnp.zeros((FR, 2 * GROUPS), F32)], axis=1)
    st_ref[...] = sums
    term_ref[0] = as_terms(sums)
    halo.append(pltpu.make_async_copy(term_ref, in_h.at[2 * FR :], sem.at[5]))
    halo.append(pltpu.make_async_copy(st_ref, st_h, sem.at[6]))
    for copy in halo[4:]:
        copy.start()
    for copy in halo:
        copy.wait()


def outside(in_ref, out_ref):
    first = lax.axis_index("c") == 0
    inner = in_ref[...].reshape(FR, COLS, CH)
    outer = out_ref[...].reshape(FR, COLS, CH)
    return jnp.where(first, outer, inner), jnp.where(first, inner, outer)


def combined(parts, squares, each):
    count = parts.shape[0]
    mean = jnp.sum(parts, axis=0) / count
    apart = parts - mean[None]
    return mean, jnp.sum(squares + each * (apart * apart), axis=0)


def pair_sums(own_ref, other_ref, out_ref):
    both = jnp.stack([own_ref[...], from_terms(other_ref[0].astype(F32))])
    mean, squares = combined(both[:, :, :GROUPS], both[:, :, GROUPS : 2 * GROUPS], CELLS * GC)
    row = jnp.concatenate([mean, squares, jnp.zeros((FR, 2 * GROUPS), F32)], axis=1)
    out_ref[...] = jnp.broadcast_to(row[None], (NY * NZ, FR, 128))


def as_terms(values):
    high = values.astype(BF16).astype(F32)
    middle = (values - high).astype(BF16).astype(F32)
    low = values - high - middle
    upper = jnp.concatenate([high, middle], axis=1)
    lower = jnp.concatenate([low, jnp.zeros((FR, 128), F32)], axis=1)
    return jnp.concatenate([upper, lower], axis=0).astype(BF16)


def from_terms(terms):
    return (terms[FR:, :128] + terms[:FR, 128:]) + terms[:FR, :128]


def pack_slices(x_ref, hp_ref, hn_ref, out_ref):
    upper = lax.axis_index("c") == 0
    own = [x_ref[:, 0], x_ref[:, 1]]
    before, after = outside(hp_ref, hn_ref)
    rows = [
        jnp.where(upper, before, own[0]),
        jnp.where(upper, own[0], own[1]),
        jnp.where(upper, own[1], after),
    ]
    three = jnp.stack(rows, axis=1).reshape(FR // 2, 2, 3, COLS, CH)
    for y in range(NY):
        part = three[..., y * ASL : (y + 1) * ASL]
        pair = jnp.concatenate([part[:, 0], part[:, 1]], axis=-1)
        out_ref[y] = pair.reshape(AROWS, 2 * ASL)


def backward_conv(g_ref, hp_ref, hn_ref, k_ref, live_ref, pad_ref, held):
    live = live_ref[...][:, None, :]
    before, after = outside(hp_ref, hn_ref)
    rows = [before, g_ref[:, 0], g_ref[:, 1], after]
    for r in range(4):
        cells = rows[r].astype(F32) * live
        for k in range(3):
            pad_ref[k, :FR, r] = shifted(cells, k).astype(BF16)
    pad_ref[:, FR:] = jnp.zeros((3, 2, 4, COLS, CH), BF16)
    held.wait()
    total = jnp.zeros((FR * CELLS, CH), F32)
    for i in range(3):
        for j in range(3):
            for k in range(3):
                window = pad_ref[2 - k, 2 - i : 2 - i + FR, 2 - j : 4 - j]
                total = total + lax.dot_general(
                    window.reshape(FR * CELLS, CH),
                    k_ref[(i * 3 + j) * 3 + k],
                    (((1,), (1,)), ((), ())),
                    preferred_element_type=F32,
                )
    return total


def backward_terms(
    g_ref, hp_ref, hn_ref, k_ref, live_ref, st_ref, x_ref, gain_ref,
    out_ref, sc_ref, mean_ref, inv_ref, pad_ref, held,
):
    act_grad = backward_conv(g_ref, hp_ref, hn_ref, k_ref, live_ref, pad_ref, held)
    mean, whole = combined(
        st_ref[:, :FR, :GROUPS], st_ref[:, :FR, GROUPS : 2 * GROUPS], NC * CELLS * GC
    )
    spread = spread_matrix()
    mean_all = hdot(mean, spread)
    inv_all = hdot(lax.rsqrt(whole / COUNT + EPSILON), spread)
    mean_ref[...] = mean_all
    inv_ref[...] = inv_all
    gain = gain_ref[...][None]
    xf = x_ref[...].astype(F32).reshape(FR, CELLS, CH)
    normalized = (xf - mean_all[:, None, :]) * inv_all[:, None, :]
    gated = normalized * gain
    sig = jax.nn.sigmoid(gated)
    pre = act_grad.reshape(FR, CELLS, CH) * sig * (1.0 + gated * (1.0 - sig))
    scaled = pre * gain
    sc_ref[...] = scaled
    gather = gather_matrix()
    first = hdot(jnp.sum(scaled, axis=1), gather)
    by_channel = jnp.sum(pre * normalized, axis=1)
    second = hdot(by_channel * gain_ref[...], gather)
    gain_part = jnp.sum(by_channel, axis=0, keepdims=True)
    row = lax.broadcasted_iota(jnp.int32, (FR, CH), 0)
    lane = lax.broadcasted_iota(jnp.int32, (FR, CH), 1)
    folded = jnp.where(lane // GROUPS == row, jnp.broadcast_to(gain_part, (FR, CH)), 0.0)
    fold_lane = lax.broadcasted_iota(jnp.int32, (CH, GROUPS), 0)
    fold_at = lax.broadcasted_iota(jnp.int32, (CH, GROUPS), 1)
    folded = hdot(folded, (fold_lane % GROUPS == fold_at).astype(F32))
    everything = jnp.concatenate([first, second, folded, jnp.zeros((FR, GROUPS), F32)], axis=1)
    out_ref[...] = jnp.broadcast_to(everything[None], (NY * NC, FR, 128))


def kernel_part(*refs):
    blocks, (mean_h, inv_h, gain_h, live_h, out_h) = refs[:8], refs[8:13]
    in_ref, mean_ref, inv_ref, gain_ref, live_ref, out_ref, pad_ref, grad_ref, sum_ref, sem = refs[13:]
    y_at, z_at, c_at = lax.axis_index("y"), lax.axis_index("z"), lax.axis_index("c")
    pairs = [(blocks[n].at[:AROWS], in_ref.at[n, :AROWS]) for n in range(8)]
    pairs += [(mean_h, mean_ref), (inv_h, inv_ref), (gain_h, gain_ref), (live_h, live_ref)]
    pairs += [(blocks[n].at[AROWS:], in_ref.at[n, AROWS:]) for n in range(8)]
    copies = [pltpu.make_async_copy(a, b, sem.at[n]) for n, (a, b) in enumerate(pairs)]
    for copy in copies:
        copy.start()
    for copy in copies[8:12]:
        copy.wait()
    width = Q * APART
    lane = lax.broadcasted_iota(jnp.int32, (CH, width), 0)
    slot = lax.broadcasted_iota(jnp.int32, (CH, width), 1)
    channel = GC * ((slot % APART) // 4) + 4 * c_at + slot % 4
    pick = (lane == y_at * ASL + channel).astype(F32)
    mean2 = hdot(mean_ref[...], pick)
    inv2 = hdot(inv_ref[...], pick)
    gain2 = hdot(gain_ref[...], pick)
    live = live_ref[:, :BSL].astype(BF16)[:, None, None, :]
    quarter = lax.broadcasted_iota(jnp.int32, (1, width), 1) // APART
    centers, scales = [], []
    for u in range(2):
        center, scale = mean2[4 * u : 4 * u + 1], inv2[4 * u : 4 * u + 1]
        for q in range(1, Q):
            center = jnp.where(quarter == q, mean2[4 * u + q : 4 * u + q + 1], center)
            scale = jnp.where(quarter == q, inv2[4 * u + q : 4 * u + q + 1], scale)
        centers.append(center)
        scales.append(scale * gain2)
    lane = lax.broadcasted_iota(jnp.int32, (2 * ASL, width), 0)
    slot = lax.broadcasted_iota(jnp.int32, (2 * ASL, width), 1)
    channel = GC * ((slot % APART) // 4) + 4 * c_at + slot % 4
    chosen = [
        (lane == (slot // APART - 2 * half) * ASL + channel).astype(BF16) for half in range(2)
    ]
    shape = (3, COLS, width)
    place = lax.broadcasted_iota(jnp.int32, shape, 2) // APART
    row = lax.broadcasted_iota(jnp.int32, shape, 0)
    block = 3 * COLS
    for copy in copies[:8]:
        copy.wait()
    for n in range(8):
        d = n % 4
        y = lax.rem(y_at + NY - d, NY)
        c = c_at if n < 4 else 1 - c_at
        top = (y == 0) & (z_at == 0) & (c == 0)
        bottom = (y == NY - 1) & (z_at == NZ - 1) & (c == NC - 1)
        edge = jnp.where(top, 0, jnp.where(bottom, 2, 3))
        inside = (row != edge).astype(F32)
        acts = []
        for u in range(2):
            at = 2 * u * block
            raw = jnp.dot(
                in_ref[n, at : at + block], chosen[0], preferred_element_type=F32
            ) + jnp.dot(
                in_ref[n, at + block : at + 2 * block], chosen[1], preferred_element_type=F32
            )
            gated = (raw - centers[u]) * scales[u]
            acts.append((gated * jax.nn.sigmoid(gated)).reshape(shape) * inside)
        a, b = acts
        a1, a2, b1 = pltpu.roll(a, 32, 2), pltpu.roll(a, 64, 2), pltpu.roll(b, 32, 2)
        b2 = pltpu.roll(b, 64, 2)
        frames = [
            jnp.where(place < 2, 0.0, a2),
            jnp.where(place < 1, 0.0, a1),
            a,
            pltpu.roll(a, 96, 2),
            jnp.where(place < 2, a2, b2),
            jnp.where(place < 1, a1, b1),
            b,
            pltpu.roll(b, 96, 2),
        ]
        for f in range(FR):
            for k in range(3):
                pad_ref[k, f, d, pl.ds(3 * c, 3)] = shifted(frames[f], k).astype(BF16)
    for copy in copies[12:]:
        copy.wait()
    for n in range(8):
        d = n % 4
        c = c_at if n < 4 else 1 - c_at
        for h in range(NC):
            at = AROWS + h * GROWS
            cells = in_ref[n, at : at + GROWS].reshape(FR, ROWS, COLS, BSL) * live
            grad_ref[:, d, pl.ds(2 * c, 2), :, h * BSL : (h + 1) * BSL] = cells
    cells = FR * NY * 4 * COLS
    turned_grad = grad_ref[...].reshape(cells, CH).T
    sum_ref[:, 4 * TAPS :] = jnp.zeros((NZ, PROWS - 4 * TAPS, CH), F32)
    combos = [(j, k) for j in range(3) for k in range(3)]
    for first in range(0, 9, 2):
        group = combos[first : first + 2]
        windows = [pad_ref[k, :, :, j : j + 4].reshape(cells, width) for j, k in group]
        window = windows[0] if len(windows) == 1 else jnp.concatenate(windows, axis=1)
        product = jnp.dot(turned_grad, window, preferred_element_type=F32)
        product = product.astype(BF16).T.astype(F32)
        for n, (j, k) in enumerate(group):
            for i in range(3):
                tap = (i * 3 + j) * 3 + k
                at = n * width + i * APART
                piece = product[at : at + APART].reshape(NZ, 4, CH)
                sum_ref[:, tap * 4 : tap * 4 + 4] = piece
    copies = []
    for n in range(0, NZ, 2):
        out_ref[n : n + 2] = sum_ref[n : n + 2].astype(BF16)
        copies.append(
            pltpu.make_async_copy(
                out_ref.at[n : n + 2], out_h.at[n : n + 2, :PROWS], sem.at[n // 2]
            )
        )
        copies[-1].start()
    for copy in copies:
        copy.wait()


def add_sums(part_h, b_h, out_h, b_ref, out_ref, sem):
    copy = pltpu.make_async_copy(b_h, b_ref, sem.at[0])
    copy.start()
    copy.wait()
    terms = as_terms(jnp.sum(b_ref[...], axis=0))
    out_ref[...] = jnp.broadcast_to(terms[None], (NZ, TERMS, CH))
    copy = pltpu.make_async_copy(out_ref, out_h.at[:, PROWS:], sem.at[1])
    copy.start()
    copy.wait()


def scale_of(values):
    most = jnp.max(jnp.max(jnp.abs(values), axis=0, keepdims=True), axis=1, keepdims=True)
    most = jnp.broadcast_to(jnp.maximum(most, 1e-36), (1, CH))
    return jnp.ceil(jnp.log2(most))


def sum_rows(in_ref, out_ref, sums_ref):
    total = jnp.sum(in_ref[...].astype(F32), axis=0)
    sums = from_terms(total[PROWS:])
    sums_ref[...] = sums
    fold_at = lax.broadcasted_iota(jnp.int32, (GROUPS, CH), 0)
    fold_lane = lax.broadcasted_iota(jnp.int32, (GROUPS, CH), 1)
    wide = hdot(sums[:, 2 * GROUPS : 3 * GROUPS], (fold_lane % GROUPS == fold_at).astype(F32))
    row = lax.broadcasted_iota(jnp.int32, (FR, CH), 0)
    lane = lax.broadcasted_iota(jnp.int32, (FR, CH), 1)
    gain = jnp.sum(jnp.where(lane // GROUPS == row, wide, 0.0), axis=0, keepdims=True)
    part = total[: 4 * TAPS]
    exponent, gain_exponent = scale_of(part), scale_of(gain)
    code = jnp.floor(part / jnp.exp2(exponent) * STEPS + 0.5)
    steps = gain / jnp.exp2(gain_exponent) * STEPS
    upper = jnp.floor(steps + 0.5)
    lower = jnp.floor((steps - upper) * STEPS + 0.5)
    rows = jnp.concatenate([code, upper, lower, exponent, gain_exponent], axis=0)
    out_ref[...] = rows.astype(jnp.int32).astype(jnp.int16)


def forward_conv(x_ref, hp_ref, hn_ref, mean_ref, inv_ref, gain_ref, k_ref, live_ref, out_ref, pad_ref, held):
    s_at = (lax.axis_index("y") * NZ + lax.axis_index("z")) * NC + lax.axis_index("c")
    before, after = outside(hp_ref, hn_ref)
    rows = [before, x_ref[:, 0], x_ref[:, 1], after]
    mean = mean_ref[...][:, None, :]
    inv = inv_ref[...][:, None, :]
    gain = gain_ref[...][None]
    for r in range(4):
        gated = (rows[r].astype(F32) - mean) * inv * gain
        act = gated * jax.nn.sigmoid(gated)
        if r == 0:
            act = jnp.where(s_at == 0, 0.0, act)
        if r == 3:
            act = jnp.where(s_at == SPACE - 1, 0.0, act)
        for k in range(3):
            pad_ref[k, 2:, r] = shifted(act, k).astype(BF16)
    pad_ref[:, :2] = jnp.zeros((3, 2, 4, COLS, CH), BF16)
    held.wait()
    total = jnp.zeros((FR * CELLS, CH), F32)
    for i in range(3):
        for j in range(3):
            for k in range(3):
                window = pad_ref[k, i : i + FR, j : j + 2]
                total = total + jnp.dot(
                    window.reshape(FR * CELLS, CH),
                    k_ref[(i * 3 + j) * 3 + k],
                    preferred_element_type=F32,
                )
    cells = total.reshape(FR, CELLS, CH) + x_ref[...].astype(F32).reshape(FR, CELLS, CH)
    cells = cells * live_ref[...][:, None, :]
    out_ref[...] = cells.astype(BF16).reshape(FR, ROWS, COLS, CH)


def finish_input(sums_ref, sc_ref, x_ref, g_ref, mean_ref, inv_ref, live_ref, out_ref):
    sums = sums_ref[...]
    spread = spread_matrix()
    first = hdot(sums[:, :GROUPS] / COUNT, spread)[:, None, :]
    second = hdot(sums[:, GROUPS : 2 * GROUPS] / COUNT, spread)[:, None, :]
    inv = inv_ref[...][:, None, :]
    xf = x_ref[...].astype(F32).reshape(FR, CELLS, CH)
    normalized = (xf - mean_ref[...][:, None, :]) * inv
    norm_grad = inv * (sc_ref[...] - first - normalized * second)
    grad = g_ref[...].astype(F32).reshape(FR, CELLS, CH) * live_ref[...][:, None, :]
    out_ref[...] = (grad + norm_grad).astype(BF16).reshape(FR, ROWS, COLS, CH)


def sum_clips(own_h, one_h, two_h, three_h, kg_h, gain_h, in_ref, kg_ref, gain_ref, sem):
    x_at = lax.axis_index("x")
    copies = []
    for d, src in enumerate((own_h, one_h, two_h, three_h)):
        copies.append(
            pltpu.make_async_copy(src, in_ref.at[lax.rem(x_at + NX - d, NX)], sem.at[d])
        )
    for copy in copies:
        copy.start()
    for copy in copies:
        copy.wait()
    total = jnp.zeros((4 * TAPS, CH), F32)
    gain = jnp.zeros((1, CH), F32)
    at = 4 * TAPS
    for n in range(NX):
        rows = in_ref[n].astype(jnp.int32).astype(F32)
        total = total + rows[:at] / STEPS * jnp.exp2(rows[at + 2 : at + 3])
        steps = rows[at : at + 1] + rows[at + 1 : at + 2] / STEPS
        gain = gain + steps / STEPS * jnp.exp2(rows[at + 3 : at + 4])
    for tap in range(TAPS):
        kg_ref[tap] = total[4 * tap : 4 * tap + 4]
    gain_ref[...] = gain
    out = (
        pltpu.make_async_copy(kg_ref, kg_h, sem.at[4]),
        pltpu.make_async_copy(gain_ref, gain_h, sem.at[5]),
    )
    for copy in out:
        copy.start()
    for copy in out:
        copy.wait()


HBM = pl.BlockSpec(memory_space=pltpu.HBM)
SMEM = pl.BlockSpec(memory_space=pltpu.SMEM)


def stay_out(array):
    return pltpu.with_memory_space_constraint(array, pltpu.HBM)


def shapes(outs):
    return tuple(jax.ShapeDtypeStruct(s, d) for s, d in outs)


def call(body, outs, args, specs, scratch, flops=0, limit=32, aliases={}):
    return pl.pallas_call(
        body,
        out_shape=shapes(outs),
        in_specs=specs,
        out_specs=tuple(HBM for _ in outs),
        scratch_shapes=list(scratch),
        input_output_aliases=aliases,
        compiler_params=pltpu.CompilerParams(vmem_limit_bytes=limit * 2**20),
        cost_estimate=pl.CostEstimate(flops=flops, bytes_accessed=2**20, transcendentals=0),
        name=body.__name__,
    )(*args)


def run(body, outs, args, scratch=(), late=None, smem=(), flops=0, rows={}):
    count, outputs = len(args), len(outs)
    moved = [at for at in range(count) if at not in smem]

    def kernel(*refs):
        ins, targets = list(refs[:count]), refs[count : count + outputs]
        rest = refs[count + outputs :]
        buffers, rest = rest[: len(moved)], rest[len(moved) :]
        results, rest = rest[:outputs], rest[outputs:]
        sem, extra = rest[0], rest[1:]
        copies = [
            pltpu.make_async_copy(
                ins[at].at[rows[at][0] : rows[at][1]] if at in rows else ins[at], buffers[n], sem.at[n]
            )
            for n, at in enumerate(moved)
        ]
        held = copies.pop(moved.index(late)) if late is not None else None
        for copy in copies + ([held] if held is not None else []):
            copy.start()
        for n, at in enumerate(moved):
            ins[at] = buffers[n]
        for copy in copies:
            copy.wait()
        if held is None:
            body(*ins, *results, *extra)
        else:
            body(*ins, *results, *extra, held)
        copies = [
            pltpu.make_async_copy(results[n], targets[n], sem.at[len(moved) + n])
            for n in range(outputs)
        ]
        for copy in copies:
            copy.start()
        for copy in copies:
            copy.wait()

    kernel.__name__ = body.__name__
    specs = [SMEM if at in smem else HBM for at in range(count)]
    buffers = []
    for at in moved:
        shape = args[at].shape
        if at in rows:
            shape = (rows[at][1] - rows[at][0],) + shape[1:]
        buffers.append(pltpu.VMEM(shape, args[at].dtype))
    buffers += [pltpu.VMEM(s, d) for s, d in outs]
    buffers += [pltpu.SemaphoreType.DMA((len(moved) + outputs,))]
    return call(kernel, outs, args, specs, buffers + list(scratch), flops)


def pack_body(x_h, g_h, hp_h, hn_h, *refs):
    outs = refs[:NY]
    x_ref, hp_ref, hn_ref, buf, sem = refs[NY:]
    pairs = ((x_h, x_ref), (hp_h.at[:HALO], hp_ref), (hn_h.at[:HALO], hn_ref))
    copies = [pltpu.make_async_copy(a, b, sem.at[n]) for n, (a, b) in enumerate(pairs)]
    for copy in copies:
        copy.start()
    straight = []
    for d, out in enumerate(outs):
        for c in range(NC):
            at = AROWS + c * GROWS
            straight.append(
                pltpu.make_async_copy(
                    g_h.at[:, c * BSL : (c + 1) * BSL],
                    out.at[at : at + GROWS],
                    sem.at[3 + NC * d + c],
                )
            )
    for copy in straight:
        copy.start()
    for copy in copies:
        copy.wait()
    pack_slices(x_ref, hp_ref, hn_ref, buf)
    y_at = lax.axis_index("y")
    copies = [
        pltpu.make_async_copy(
            buf.at[lax.rem(y_at + d, NY)], out.at[:AROWS], sem.at[3 + NC * NY + d]
        )
        for d, out in enumerate(outs)
    ]
    for copy in copies:
        copy.start()
    for copy in straight + copies:
        copy.wait()


def local(video_latent, frame_counts, conv_kernel, norm_gain, output_grad):
    x = stay_out(video_latent.reshape(FR, ROWS, COLS, CH))
    g = stay_out(output_grad.reshape(FR, ROWS, COLS, CH))
    gain = stay_out(norm_gain.reshape(1, CH))
    conv_kernel = stay_out(conv_kernel)
    space = ("y", "z", "c")
    cells = (FR, ROWS, COLS, CH)
    wide = (FR, CH)
    swap = [(0, 1), (1, 0)]
    dma = pltpu.SemaphoreType.DMA

    inner, outer, stats = call(
        edges_and_sums,
        [
            ((2 * HALO + 1, COLS, CH), BF16),
            ((2 * HALO, COLS, CH), BF16),
            ((FR, 128), F32),
        ],
        (x, g),
        [HBM] * 2,
        [
            pltpu.VMEM(cells, BF16),
            pltpu.VMEM((FR, 128), F32),
            pltpu.VMEM((1, TERMS, CH), BF16),
            dma((7,)),
        ],
    )
    stats, counts = lax.optimization_barrier((stats, frame_counts))
    live = jnp.broadcast_to(jnp.arange(FR)[:, None] < counts[0], wide).astype(F32)
    hp = lax.ppermute(inner, "c", swap)
    hn = lax.ppermute(
        outer,
        space,
        [(i, i - 1 if i % 2 == 0 else i + 1) for i in range(1, SPACE - 1)],
    )
    (stats,) = run(
        pair_sums,
        [((NY * NZ, FR, 128), F32)],
        (stats, hp),
        rows={1: (2 * HALO, 2 * HALO + 1)},
    )
    stats = lax.all_to_all(stats, ("y", "z"), 0, 0)
    block = (BLOCK, BSL)
    packed = call(
        pack_body,
        [(block, BF16)] * NY,
        (x, stay_out(output_grad.reshape(GROWS, CH)), hp, hn),
        [HBM] * 4,
        [pltpu.VMEM(cells, BF16)]
        + [pltpu.VMEM((HALO, COLS, CH), BF16)] * 2
        + [pltpu.VMEM((NY, AROWS, BSL), BF16), dma((3 + NC * NY + NY,))],
    )
    near = [packed[0]] + [
        lax.ppermute(packed[d], "y", [(i, (i + d) % NY) for i in range(NY)]) for d in range(1, NY)
    ]
    conv_flops = 16 * TAPS * FR * CELLS * CH * CH
    padded = pltpu.VMEM((3, FR + 2, 4, COLS, CH), BF16)
    terms, scaled, mean, inv = run(
        backward_terms,
        [((NY * NC, FR, 128), F32), ((FR, CELLS, CH), F32), (wide, F32), (wide, F32)],
        (g, hp, hn, conv_kernel, live, stats, x, gain),
        rows={1: (HALO, 2 * HALO), 2: (HALO, 2 * HALO)},
        scratch=[padded],
        late=3,
    )
    *moved, terms = lax.optimization_barrier((*near[1:], terms))
    near = [near[0], *moved]
    terms = lax.all_to_all(terms, ("y", "c"), 0, 0)
    far = [lax.ppermute(a, "c", swap) for a in near]
    part = (NZ, PROWS, CH)
    whole_part = (NZ, PROWS + TERMS, CH)
    (partial,) = call(
        kernel_part,
        [(whole_part, BF16)],
        (*near, *far, mean, inv, gain, live),
        [HBM] * 12,
        [
            pltpu.VMEM((8, BLOCK, BSL), BF16),
            pltpu.VMEM(wide, F32),
            pltpu.VMEM(wide, F32),
            pltpu.VMEM((1, CH), F32),
            pltpu.VMEM(wide, F32),
            pltpu.VMEM(part, BF16),
            pltpu.VMEM((3, FR, NY, 6, COLS, Q * APART), BF16),
            pltpu.VMEM((FR, NY, 4, COLS, CH), BF16),
            pltpu.VMEM(part, F32),
            dma((20,)),
        ],
        flops=conv_flops,
    )
    (merged,) = call(
        add_sums,
        [(whole_part, BF16)],
        (partial, terms),
        [HBM] * 2,
        [pltpu.VMEM((NY * NC, FR, 128), F32), pltpu.VMEM((NZ, TERMS, CH), BF16), dma((2,))],
        aliases={0: 0},
    )
    merged, late_mean = lax.optimization_barrier((merged, mean))
    merged = lax.all_to_all(merged, "z", 0, 0)
    (block_output,) = run(
        forward_conv,
        [(cells, BF16)],
        (x, hp, hn, late_mean, inv, gain, conv_kernel, live),
        rows={1: (0, HALO), 2: (0, HALO)},
        scratch=[padded],
        late=6,
        flops=conv_flops,
    )
    merged, block_output = lax.optimization_barrier((merged, block_output))
    rows, sums = run(sum_rows, [((PROWS, CH), jnp.int16), ((FR, 128), F32)], (merged,))
    others = [rows] + [
        lax.ppermute(rows, "x", [(i, (i + d) % NX) for i in range(NX)]) for d in range(1, NX)
    ]
    (input_grad,) = run(
        finish_input, [(cells, BF16)], (sums, scaled, x, g, mean, inv, live)
    )
    kernel_grad, gain_grad = call(
        sum_clips,
        [((TAPS, 4, CH), F32), ((1, CH), F32)],
        others,
        [HBM] * 4,
        [
            pltpu.VMEM((NX, PROWS, CH), jnp.int16),
            pltpu.VMEM((TAPS, 4, CH), F32),
            pltpu.VMEM((1, CH), F32),
            dma((6,)),
        ],
    )
    whole = (1,) + cells
    return (
        block_output.reshape(whole),
        input_grad.reshape(whole),
        jnp.swapaxes(kernel_grad, 0, 1),
        gain_grad.reshape(CH),
    )


def solution(mesh):
    fine = Mesh(mesh.devices.reshape(NX, NY, NZ, NC), ("x", "y", "z", "c"))
    space = ("y", "z", "c")
    cells = P("x", None, space, None, None)
    return jax.shard_map(
        local,
        mesh=fine,
        in_specs=(cells, P("x"), P(), P(), cells),
        out_specs=(cells, cells, P(space, None, None), P()),
        check_vma=False,
    )
```
